32 devices in a mesh: parts: 2 (over y), walk: 4 (over z), slab: 2 (over x), row: 2 (over core).
Axes of the slice: x: 2, y: 2, z: 4, core: 2. Of those that a mesh axis runs over, the one named last changes fastest.
Arguments:
- walkers: bfloat16 [64, 1024, 256], P(('parts', 'walk'), ('slab', 'row')), parts along dimension 0
- trial_orbitals: bfloat16 [2048, 256], P(('parts', 'slab', 'row')), parts along dimension 0
- cholesky: bfloat16 [16, 256, 1024], P(('parts', 'slab', 'row')), parts along dimension 0, may hold values from -0.359375 to 0.359375
- branches: int32 [64], P('parts'), parts along dimension 0, may hold values from 0 to 31, as said below
- counts: int32 [8], P(('parts', 'walk')), parts along dimension 0, may hold values from 4 to 8, as said below
- field: float32 [64, 1024], P(('parts', 'walk'), ('slab', 'row')), parts along dimension 0, may hold values from 0.7 to 1.3
Outputs:
- force_bias: float32 [64, 8], P(('parts', 'walk'), ('slab', 'row')), parts along dimension 0
- exchange_energy: float32 [64, 8], P(('parts', 'walk'), ('slab', 'row')), parts along dimension 0
The draws below stay inside these ranges and needn't reach their ends.
There are 2 independent parts, one for each index of `parts`. The reference program is written for one: setup_inputs(seed, part) draws one part's arguments, and reference() takes and returns one part's arrays. A program takes and returns all parts, laid end to end along the dimension named above; each array names one. Nothing has to cross between parts.
Inputs may be any that keep to these rules, and one draw needn't show every extreme that they name: `branches`: the new walkers of one walk index copy at most 2 walkers from any one walk index, and some walk index gives exactly 2 to some walk index. `counts`: at least one walk index has all 8 alive; the alive ones are the first of its walkers.
All inputs are finite; a program needn't handle non-finite values. Where the reference program divides by a largest or mean magnitude, that divisor is 1e-20 or more.
Results may differ from the reference program's by a relative error of at most 0.0068.
Values may be sent and summed in bfloat16 or wider, within the bound.
No kernel may reach another device: no remote copies, remote signals or barrier semaphores. Data moves between devices by JAX's collectives and lax.ppermute only.
A program may use at most 64 MiB of HBM per device.

```python
import math
import jax
import jax.numpy as jnp
from jax import lax

ORB = 1024
ELEC = 256
WALK_DEV = 8
ITERS = 10
WALKERS = 32
NCHOL = 8
SLOTS = 2


def joint_draw(key):
    folded = jax.random.fold_in(key, 101)
    key_orbitals = jax.random.fold_in(folded, 0)
    key_mixing = jax.random.fold_in(folded, 1)
    key_residue = jax.random.fold_in(folded, 3)
    orbitals = jax.random.normal(key_orbitals, (ORB, ELEC), jnp.float32) / math.sqrt(ORB)
    mixing = jnp.eye(ELEC, dtype=jnp.float32)[None] + 0.3 / math.sqrt(ELEC) * jax.random.normal(key_mixing, (WALKERS, ELEC, ELEC), jnp.float32)
    residue = 0.5 / math.sqrt(ORB) * jax.random.normal(key_residue, (WALKERS, ORB, ELEC), jnp.float32)
    walkers = jnp.einsum('mn,wnk->wmk', orbitals, mixing) + residue
    return (orbitals, walkers)


def draw_walkers(key, part):
    orbitals, walkers = joint_draw(key)
    return walkers.astype(jnp.bfloat16)


def draw_trial_orbitals(key, part):
    orbitals, walkers = joint_draw(key)
    return orbitals.astype(jnp.bfloat16)


def draw_branches(key, part):
    folded = jax.random.fold_in(key, 202)
    key_scores, key_favour, key_local = jax.random.split(folded, 3)
    walk_count = WALKERS // WALK_DEV
    capacity = SLOTS
    candidates = walk_count * capacity
    favour = jax.random.randint(key_favour, (walk_count,), 0, 4) * 1536
    scores = jax.random.randint(key_scores, (walk_count, candidates), 0, 4096) + jnp.repeat(favour, capacity)[None, :]
    scores = scores * candidates + jnp.arange(candidates, dtype=jnp.int32)[None, :]
    top_values, chosen = lax.top_k(scores, WALK_DEV)
    sender = chosen // capacity
    local_index = jax.random.randint(key_local, (walk_count, WALK_DEV), 0, WALK_DEV)
    return (sender * WALK_DEV + local_index).reshape(WALKERS).astype(jnp.int32)


def draw_counts(key, part):
    folded = jax.random.fold_in(key, 303)
    key_counts, key_fullest = jax.random.split(folded)
    walk_count = WALKERS // WALK_DEV
    living = jax.random.randint(key_counts, (walk_count,), WALK_DEV // 2, WALK_DEV + 1)
    fullest = jax.random.randint(key_fullest, (), 0, walk_count)
    return living.at[fullest].set(WALK_DEV).astype(jnp.int32)


def shard_levels(rng, shape, cuts, low, top_value):
    level, own = 1.0, jax.random.fold_in(rng, 6)
    for dim, shards_of in cuts:
        draws = jnp.exp(jax.random.uniform(jax.random.fold_in(own, dim), (shards_of,), jnp.float32, low / len(cuts), top_value / len(cuts)))
        level = level * jnp.repeat(draws, shape[dim] // shards_of).reshape([-1 if axis == dim else 1 for axis in range(len(shape))])
    return level


def noise(own_key, extent, spread, limit, shards=(), kind=jnp.bfloat16):
    level = shard_levels(own_key, extent, shards, -0.22, 0.18) if shards else 1.0
    result = jax.random.normal(own_key, extent, jnp.float32) * spread * level
    return jnp.minimum(jnp.maximum(result, -limit), limit).astype(kind)


def setup_inputs(seed: int = 0, part: int = 0) -> dict:
    splits = jax.random.split(jax.random.key(seed), 7)
    part_splits = jax.random.split(jax.random.fold_in(splits[6], part), 7)
    return {
        "walkers": draw_walkers(jax.random.fold_in(jax.random.fold_in(splits[6], part), 71), part),
        "trial_orbitals": draw_trial_orbitals(jax.random.fold_in(jax.random.fold_in(splits[6], part), 71), part),
        "cholesky": noise(part_splits[2], (NCHOL, ELEC, ORB), 0.06, 0.359375, ((0, 4),)),
        "branches": draw_branches(jax.random.fold_in(jax.random.fold_in(splits[6], part), 71), part),
        "counts": draw_counts(jax.random.fold_in(jax.random.fold_in(splits[6], part), 71), part),
        "field": jnp.clip(0.7 + 0.59999996 * jax.random.uniform(part_splits[5], (WALKERS, ORB), jnp.float32) ** shard_levels(part_splits[5], (WALKERS, ORB), ((0, 4), (1, 4)), -0.2, 0.2), 0.7, 1.3),
    }


HIGHEST = lax.Precision.HIGHEST


def newton_schulz(intersection):
    column_max = jnp.max(jnp.sum(jnp.abs(intersection), axis=0))
    row_max = jnp.max(jnp.sum(jnp.abs(intersection), axis=1))
    inverse = intersection.T / (column_max * row_max)
    twice_identity = 2.0 * jnp.eye(intersection.shape[0], dtype=intersection.dtype)
    for iteration in range(ITERS):
        inverse = jnp.dot(inverse, twice_identity - jnp.dot(intersection, inverse, precision=HIGHEST), precision=HIGHEST)
    return inverse


def reference(walkers, trial_orbitals, cholesky, branches, counts, field):
    vectors = cholesky.astype(jnp.float32)

    def per_walker(walker_index):
        source = walkers[branches[walker_index]]
        walker = (source.astype(jnp.float32) * field[walker_index][:, None]).astype(jnp.bfloat16)
        intersection = jnp.dot(trial_orbitals.T, walker, preferred_element_type=jnp.float32)
        inverse = newton_schulz(intersection).astype(jnp.bfloat16)
        green_half = jnp.dot(walker, inverse, preferred_element_type=jnp.float32).astype(jnp.bfloat16)
        contracted = jnp.einsum('gnm,mk->gnk', vectors, green_half.astype(jnp.float32), precision=HIGHEST)
        living = (walker_index % WALK_DEV < counts[walker_index // WALK_DEV]).astype(jnp.float32)
        force_bias = jnp.trace(contracted, axis1=1, axis2=2) * living
        exchange_energy = -0.5 * jnp.einsum('gnk,gkn->g', contracted, contracted, precision=HIGHEST) * living
        return force_bias, exchange_energy

    force_bias, exchange_energy = lax.map(per_walker, jnp.arange(WALKERS, dtype=jnp.int32))
    return force_bias, exchange_energy
```

```python
import functools

import jax
import jax.numpy as jnp
from jax import lax
from jax.experimental import pallas as pl
from jax.experimental.pallas import tpu as pltpu
from jax.sharding import PartitionSpec as P

ITERS = 10
SR = ("slab", "row")
ALL = ("walk", "slab", "row")
F32 = jnp.float32
BF16 = jnp.bfloat16
VMEM_LIMIT = 24 * 2**20
SMALL_LIMIT = 2**20
HIGHEST = lax.Precision.HIGHEST


def dot(a, b, dims=((1,), (0,))):
    return lax.dot_general(a, b, (dims, ((), ())), preferred_element_type=F32)


def split(x):
    high = x.astype(BF16)
    return high, (x - high.astype(F32)).astype(BF16)


def place():
    return lax.axis_index("walk"), lax.axis_index("slab") * lax.axis_size("row") + lax.axis_index("row")


def whole(memory=pltpu.VMEM):
    return pl.BlockSpec(memory_space=memory)


def select_kernel(n, per, share, branches, walkers, field, *refs):
    sends, fields, sems = refs[:n], refs[n : 2 * n], refs[2 * n]
    walk, q = place()
    for k in range(n):
        other = q ^ k
        rank = jnp.int32(0)
        for i in range(per):
            branch = branches[other * per + i]
            hit = lax.div(branch, per) == walk

            @pl.when(hit)
            def _(branch=branch, rank=rank):
                pltpu.make_async_copy(
                    walkers.at[lax.rem(branch, per)], sends[k].at[rank], sems.at[k, rank]
                ).start()

            rank = rank + hit.astype(jnp.int32)
    for k in range(n):
        other = q ^ k
        rank = jnp.int32(0)
        for i in range(per):
            hit = lax.div(branches[walk * per + i], per) == other

            @pl.when(hit)
            def _(i=i, rank=rank):
                fields[k][pl.ds(rank, 1), :] = field[i : i + 1, :]

            rank = rank + hit.astype(jnp.int32)
    for k in range(n):
        for rank in range(share):
            pltpu.make_async_copy(walkers.at[0], sends[k].at[rank], sems.at[k, rank]).wait()


def select(n, per, share, branches, walkers, field):
    rows, electrons = walkers.shape[1:]
    return pl.pallas_call(
        functools.partial(select_kernel, n, per, share),
        out_shape=[jax.ShapeDtypeStruct((share, rows, electrons), walkers.dtype)] * n
        + [jax.ShapeDtypeStruct((share, rows), field.dtype)] * n,
        in_specs=[whole(pltpu.SMEM), whole(pl.ANY), whole()],
        out_specs=[whole(pl.ANY)] * n + [whole()] * n,
        scratch_shapes=[pltpu.SemaphoreType.DMA((n, share))],
        compiler_params=pltpu.CompilerParams(vmem_limit_bytes=VMEM_LIMIT),
        cost_estimate=pl.CostEstimate(flops=0, bytes_accessed=4 * walkers.size, transcendentals=0),
        name="select",
    )(branches, walkers, field)


def green_kernel(n, share, *refs):
    blocks, fields, trials = refs[:n], refs[n : 2 * n], refs[2 * n : 3 * n]
    green, by_block, moved, state = refs[3 * n :]
    walk, q = place()
    rows, electrons = blocks[0].shape[1:]
    for k in range(n):
        by_block[pl.ds(walk ^ k, 1), :share, :] = fields[k][...][None]
    columns = [by_block[pl.ds(q ^ k, 1), :, :].reshape(by_block.shape[1:]).T for k in range(n)]
    for i in range(share):
        transposed = jnp.zeros((electrons, electrons), F32)
        for k in range(n):
            part = (blocks[k][i].astype(F32) * columns[k][:, i : i + 1]).astype(BF16)
            moved[i, k * rows : (k + 1) * rows, :] = part
            transposed = transposed + dot(part, trials[k][...], ((0,), (0,)))
        size = jnp.abs(transposed)
        scale = jnp.max(jnp.sum(size, axis=0)) * jnp.max(jnp.sum(size, axis=1))
        start = transposed / scale
        high, low = split(transposed)
        start_high, start_low = split(start)
        across = ((0,), (0,))
        state[i, :electrons, :] = start
        state[i, electrons:, :] = dot(high, start_high, across) + (
            dot(high, start_low, across) + dot(low, start_high, across)
        )

    def advance(step, carry):
        for i in range(share):
            now = state[i]
            high, low = split(now)
            right_high, right_low = high[electrons:], low[electrons:]
            product = dot(high, right_high) + (dot(high, right_low) + dot(low, right_high))
            state[i] = 2.0 * now - product
        return carry

    lax.fori_loop(0, ITERS - 1, advance, 0)
    for i in range(share):
        now = state[i]
        high, low = split(now)
        left_high, left_low = high[:electrons], low[:electrons]
        right_high, right_low = high[electrons:], low[electrons:]
        product = dot(left_high, right_high) + (dot(left_high, right_low) + dot(left_low, right_high))
        inverse = (2.0 * now[:electrons] - product).astype(BF16)
        for k in range(n):
            at = pl.multiple_of((q ^ k) * rows, rows)
            green[pl.ds(at, rows), i * electrons : (i + 1) * electrons] = dot(
                moved[i, k * rows : (k + 1) * rows, :], inverse
            ).astype(BF16)


def make_green(n, share, blocks, fields, trials):
    rows, electrons = blocks[0].shape[1:]
    padded = -(-share // 8) * 8
    flops = share * (8 * rows * n * electrons**2 + 2 * 6 * ITERS * electrons**3)
    return pl.pallas_call(
        functools.partial(green_kernel, n, share),
        out_shape=jax.ShapeDtypeStruct((n * rows, share * electrons), BF16),
        in_specs=[whole()] * (3 * n),
        out_specs=whole(),
        scratch_shapes=[
            pltpu.VMEM((n, padded, rows), F32),
            pltpu.VMEM((share, n * rows, electrons), BF16),
            pltpu.VMEM((share, 2 * electrons, electrons), F32),
        ],
        compiler_params=pltpu.CompilerParams(vmem_limit_bytes=VMEM_LIMIT),
        cost_estimate=pl.CostEstimate(flops=flops, bytes_accessed=3 * 2**20, transcendentals=0),
        name="green",
    )(*blocks, *fields, *trials)


def contract_kernel(share, count, *refs):
    vectors, green, outs = refs[:count], refs[count], refs[count + 1 :]
    electrons = vectors[0].shape[1]
    half = electrons // 2
    row = lax.broadcasted_iota(jnp.int32, (electrons, electrons), 0)
    column = lax.broadcasted_iota(jnp.int32, (electrons, electrons), 1)
    out_row = lax.broadcasted_iota(jnp.int32, (8, 128), 0)
    lane = lax.broadcasted_iota(jnp.int32, (8, 128), 1)
    for v in range(count):
        held = jnp.zeros((8, 128), F32)
        for g in range(vectors[v].shape[0]):
            both = dot(vectors[v][g], green[...])
            for i in range(share):
                one = both[:, i * electrons : (i + 1) * electrons]
                trace = jnp.sum(jnp.where(row == column, one, 0.0))
                a, b = one[:half, :half], one[:half, half:]
                c, d = one[half:, :half], one[half:, half:]
                exchange = -0.5 * jnp.sum(a * a.T + d * d.T + 2.0 * (b * c.T))
                here = out_row == g * share + i
                held = jnp.where(here & (lane == 0), trace, held)
                held = jnp.where(here & (lane == 1), exchange, held)
        outs[v][...] = held


def contract(share, vectors, green):
    flops = sum(2 * v.size * green.shape[1] for v in vectors)
    return pl.pallas_call(
        functools.partial(contract_kernel, share, len(vectors)),
        out_shape=[jax.ShapeDtypeStruct((8, 128), F32)] * len(vectors),
        in_specs=[whole()] * (len(vectors) + 1),
        out_specs=[whole()] * len(vectors),
        compiler_params=pltpu.CompilerParams(vmem_limit_bytes=VMEM_LIMIT),
        cost_estimate=pl.CostEstimate(
            flops=flops, bytes_accessed=sum(2 * v.size for v in vectors) + 2 * green.size, transcendentals=0
        ),
        name="contract",
    )(*vectors, green)


def unpack_kernel(n, per, share, branches, counts, *refs):
    arrived, force, exchange = refs[:n], refs[n], refs[n + 1]
    walk, q = place()
    vectors = force.shape[0]
    row = lax.broadcasted_iota(jnp.int32, force.shape, 1)
    column = lax.broadcasted_iota(jnp.int32, force.shape, 0)
    force_all = jnp.zeros(force.shape, F32)
    exchange_all = jnp.zeros(force.shape, F32)
    senders = [lax.div(branches[walk * per + i], per) for i in range(per)]
    for i in range(per):
        rank = jnp.int32(0)
        for j in range(i):
            rank = rank + (senders[j] == senders[i]).astype(jnp.int32)
        living = (i < counts[0]).astype(F32)
        for g in range(vectors):
            at = g * share + rank
            values = [jnp.float32(0.0), jnp.float32(0.0)]
            for k in range(n):
                mine = (senders[i] ^ q) == k
                values = [jnp.where(mine, arrived[k][at, c], values[c]) for c in range(2)]
            here = (row == i) & (column == g)
            force_all = jnp.where(here, values[0] * living, force_all)
            exchange_all = jnp.where(here, values[1] * living, exchange_all)
    force[...] = force_all
    exchange[...] = exchange_all


def unpack(n, per, share, vectors, branches, counts, arrived):
    return pl.pallas_call(
        functools.partial(unpack_kernel, n, per, share),
        out_shape=[jax.ShapeDtypeStruct((vectors, per), F32)] * 2,
        in_specs=[whole(pltpu.SMEM)] * (2 + n),
        out_specs=[whole()] * 2,
        compiler_params=pltpu.CompilerParams(vmem_limit_bytes=SMALL_LIMIT),
        name="unpack",
    )(branches, counts, *arrived)


def at_the_source(walkers, trial_orbitals, cholesky, branches, counts, field):
    n = lax.axis_size("walk")
    per = walkers.shape[0]
    share = per // n
    row_size = lax.axis_size("row")
    partner = lambda k: [(i, i ^ k) for i in range(n)]
    move = lambda x, k: lax.ppermute(x, SR, partner(k)) if k else x
    pairs = [(w, q) for w in range(n) for q in range(n)]
    ask = lambda x, k: lax.ppermute(x, ALL, [(w * n + q, (q ^ k) * n + w) for w, q in pairs])
    answer = lambda x, k: lax.ppermute(x, ALL, [(w * n + q, q * n + (w ^ k)) for w, q in pairs])

    def gathered(x):
        blocks = [x]
        for k in range(1, n):
            low = k & (row_size - 1)
            blocks.append(move(x, k) if low == 0 or low == k else move(blocks[k ^ low], low))
        return blocks

    trials = gathered(trial_orbitals)
    chosen = select(n, per, share, branches, walkers, field)
    blocks = [move(x, k) for k, x in enumerate(chosen[:n])]
    fields = [ask(x, k) for k, x in enumerate(chosen[n:])]
    chunks = cholesky.shape[0]
    parts = [cholesky[c : c + 1] for c in range(chunks)]
    near = [k for k in range(n) if k < row_size]
    far = [k for k in range(n) if k >= row_size]
    whole_near = [cholesky] + [move(cholesky, k) for k in near[1:]]
    far_parts = [gathered_far(parts[c], move, far, row_size) for c in range(chunks)]
    green = make_green(n, share, blocks, fields, trials)
    results = dict()
    for k, held in zip(near, contract(share, whole_near, green)):
        results[k] = held
    late = [contract(share, [far_parts[c][k] for k in far], green) for c in range(chunks)]
    merged = merge(n, near, far, chunks, share, results, late)
    arrived = [answer(x, k) for k, x in enumerate(merged)]
    return tuple(x.T for x in unpack(n, per, share, cholesky.shape[0], branches, counts, arrived))


def gathered_far(x, move, far, row_size):
    held = {}
    for k in far:
        low = k & (row_size - 1)
        held[k] = move(x, k) if low == 0 else move(held[k ^ low], low)
    return held


def merge_kernel(n, near, far, chunks, share, *refs):
    close, late, outs = refs[: len(near)], refs[len(near) : -n], refs[-n:]
    walk, q = place()
    rows = lax.broadcasted_iota(jnp.int32, (8, 128), 0)
    groups = {}
    for at, k in enumerate(near):
        groups[k] = close[at][...]
    for at, k in enumerate(far):
        held = late[at][...]
        for c in range(1, chunks):
            moved = pltpu.roll(late[c * len(far) + at][...], c * share, 0)
            held = jnp.where(rows >= c * share, moved, held)
        groups[k] = held
    for k in range(n):
        group = q ^ walk ^ k
        value = groups[0]
        for j in range(1, n):
            value = jnp.where(group == j, groups[j], value)
        outs[k][...] = value


def merge(n, near, far, chunks, share, results, late):
    operands = [results[k] for k in near] + [x for held in late for x in held]
    return pl.pallas_call(
        functools.partial(merge_kernel, n, near, far, chunks, share),
        out_shape=[jax.ShapeDtypeStruct((8, 128), F32)] * n,
        in_specs=[whole()] * len(operands),
        out_specs=[whole()] * n,
        compiler_params=pltpu.CompilerParams(vmem_limit_bytes=SMALL_LIMIT),
        name="merge",
    )(*operands)


def newton_schulz(intersection):
    column_max = jnp.max(jnp.sum(jnp.abs(intersection), axis=0))
    row_max = jnp.max(jnp.sum(jnp.abs(intersection), axis=1))
    inverse = intersection.T / (column_max * row_max)
    twice_identity = 2.0 * jnp.eye(intersection.shape[0], dtype=intersection.dtype)
    for iteration in range(ITERS):
        inverse = jnp.dot(
            inverse,
            twice_identity - jnp.dot(intersection, inverse, precision=HIGHEST),
            precision=HIGHEST,
        )
    return inverse


def pick(array, indices):
    return jnp.concatenate(
        [lax.dynamic_slice_in_dim(array, indices[i], 1, 0) for i in range(indices.shape[0])], axis=0
    )


def at_the_target(walkers, trial_orbitals, cholesky, branches, counts, field):
    walk_size = lax.axis_size("walk")
    position = lax.axis_index("walk")
    per_device, row_count, electrons = walkers.shape
    capacity = (per_device + walk_size - 1) // walk_size
    sender = branches.reshape(walk_size, per_device) // per_device
    local_index = branches.reshape(walk_size, per_device) % per_device
    same_sender = sender[:, :, None] == sender[:, None, :]
    earlier = jnp.arange(per_device)[None, :] < jnp.arange(per_device)[:, None]
    arrival_rank = jnp.sum(same_sender & earlier[None], axis=2)
    wanted = (sender[:, None, :] == position) & (
        arrival_rank[:, None, :] == jnp.arange(capacity, dtype=jnp.int32)[None, :, None]
    )
    chosen = jnp.sum(jnp.where(wanted, local_index[:, None, :], 0), axis=2).reshape(-1)
    outgoing = pick(walkers, chosen).reshape(walk_size, capacity, row_count, electrons)
    arrived = lax.all_to_all(outgoing, "walk", split_axis=0, concat_axis=0, tiled=True)
    my_sender = lax.dynamic_index_in_dim(sender, position, 0, keepdims=False)
    my_rank = lax.dynamic_index_in_dim(arrival_rank, position, 0, keepdims=False)
    arrived_flat = arrived.reshape(walk_size * capacity, row_count, electrons)
    migrated = pick(arrived_flat, my_sender * capacity + my_rank)
    propagated = (migrated.astype(F32) * field[:, :, None]).astype(BF16)
    everything = lax.all_gather(propagated, SR, axis=1, tiled=True)
    shard_count = lax.axis_size(SR)
    share = per_device // shard_count
    trial_whole = lax.all_gather(trial_orbitals, SR, axis=0, tiled=True)
    own_walkers = lax.dynamic_slice_in_dim(everything, lax.axis_index(SR) * share, share, 0)
    intersection = jnp.einsum("mn,wmk->wnk", trial_whole, own_walkers, preferred_element_type=F32)
    inverse = jax.vmap(newton_schulz)(intersection).astype(BF16)
    inverses = lax.all_gather(inverse, SR, axis=0, tiled=True)
    green = jnp.einsum("wmn,wnk->wmk", everything, inverses, preferred_element_type=F32).astype(BF16)
    contracted = jnp.einsum("gnm,wmk->wgnk", cholesky, green, preferred_element_type=F32)
    living = (jnp.arange(per_device, dtype=jnp.int32) < counts[0]).astype(F32)[:, None]
    force_bias = jnp.trace(contracted, axis1=2, axis2=3) * living
    exchange_energy = -0.5 * jnp.einsum("wgnk,wgkn->wg", contracted, contracted) * living
    return (force_bias, exchange_energy)


def on_device(walkers, trial_orbitals, cholesky, branches, counts, field):
    walk_size, shard_count = lax.axis_size("walk"), lax.axis_size(SR)
    per = walkers.shape[0]
    if walk_size == shard_count and per % walk_size == 0 and not walk_size & (walk_size - 1):
        if cholesky.shape[0] * (per // walk_size) <= 8:
            return at_the_source(walkers, trial_orbitals, cholesky, branches, counts, field)
    return at_the_target(walkers, trial_orbitals, cholesky, branches, counts, field)


def solution(mesh):
    return jax.shard_map(
        on_device,
        mesh=mesh,
        in_specs=(
            P(("parts", "walk"), SR, None),
            P(("parts",) + SR, None),
            P(("parts",) + SR, None, None),
            P("parts"),
            P(("parts", "walk")),
            P(("parts", "walk"), SR),
        ),
        out_specs=(P(("parts", "walk"), SR), P(("parts", "walk"), SR)),
        check_vma=False,
    )
```

```python
import functools

import jax
import jax.numpy as jnp
from jax import lax
from jax.experimental import pallas as pl
from jax.experimental.pallas import tpu as pltpu
from jax.sharding import PartitionSpec as P

ITERS = 10
SR = ("slab", "row")
ALL = ("walk", "slab", "row")
F32 = jnp.float32
BF16 = jnp.bfloat16
VMEM_LIMIT = 24 * 2**20
SMALL_LIMIT = 2**20
HIGHEST = lax.Precision.HIGHEST


def dot(a, b, dims=((1,), (0,))):
    return lax.dot_general(a, b, (dims, ((), ())), preferred_element_type=F32)


def split(x):
    high = x.astype(BF16)
    return high, (x - high.astype(F32)).astype(BF16)


def place():
    return lax.axis_index("walk"), lax.axis_index("slab") * lax.axis_size("row") + lax.axis_index("row")


def whole(memory=pltpu.VMEM):
    return pl.BlockSpec(memory_space=memory)


def picks(branches, start, per, sender, share):
    places, olds = [jnp.int32(0)] * share, [jnp.int32(0)] * share
    rank = jnp.int32(0)
    for i in range(per):
        branch = branches[start + i]
        hit = lax.div(branch, per) == sender
        old = lax.rem(branch, per)
        for r in range(share):
            here = hit & (rank == r)
            places[r] = jnp.where(here, i, places[r])
            olds[r] = jnp.where(here, old, olds[r])
        rank = rank + hit.astype(jnp.int32)
    return places, olds


def select_kernel(n, per, share, branches, walkers, cholesky, *refs):
    sends, direct, shared, sems, more = refs[:n], refs[n], refs[n + 1], refs[n + 2], refs[n + 3]
    walk, q = place()
    split_at, half = direct.shape[0], shared.shape[1]
    rows = pl.ds(pl.multiple_of((walk & 1) * half, half), half)
    copies = []
    for k in range(1, n):
        olds = picks(branches, (q ^ k ^ walk) * per, per, walk, share)[1]
        for r in range(share):
            copies.append(pltpu.make_async_copy(walkers.at[olds[r]], sends[k].at[r], sems.at[k, r]))
            copies[-1].start()
    copies.append(pltpu.make_async_copy(cholesky.at[pl.ds(split_at, shared.shape[0]), rows, :], shared, more.at[0]))
    copies[-1].start()
    copies.append(pltpu.make_async_copy(cholesky.at[pl.ds(0, split_at)], direct, more.at[1]))
    copies[-1].start()
    olds = picks(branches, (q ^ walk) * per, per, walk, share)[1]
    for r in range(share):
        copies.append(pltpu.make_async_copy(walkers.at[olds[r]], sends[0].at[r], sems.at[0, r]))
        copies[-1].start()
    for copy in copies:
        copy.wait()


def select(n, per, share, branches, walkers, cholesky):
    rows, electrons = walkers.shape[1:]
    vectors, height, width = cholesky.shape
    later = vectors // 2
    return pl.pallas_call(
        functools.partial(select_kernel, n, per, share),
        out_shape=[jax.ShapeDtypeStruct((share, rows, electrons), walkers.dtype)] * n
        + [
            jax.ShapeDtypeStruct((vectors - later, height, width), cholesky.dtype),
            jax.ShapeDtypeStruct((later, height // 2, width), cholesky.dtype),
        ],
        in_specs=[whole(pltpu.SMEM), whole(pl.ANY), whole(pl.ANY)],
        out_specs=[whole(pl.ANY)] * (n + 2),
        scratch_shapes=[pltpu.SemaphoreType.DMA((n, share)), pltpu.SemaphoreType.DMA((2,))],
        compiler_params=pltpu.CompilerParams(vmem_limit_bytes=SMALL_LIMIT),
        cost_estimate=pl.CostEstimate(flops=0, bytes_accessed=4 * walkers.size, transcendentals=0),
        name="select",
    )(branches, walkers, cholesky)


def message_kernel(trial, field, out):
    rows = trial.shape[0]
    out[:rows, :] = trial[...]
    rest, terms = field[...], []
    for _ in range(3):
        terms.append(rest.astype(BF16).astype(F32))
        rest = rest - terms[-1]
    spare = out.shape[0] - rows - 3 * field.shape[0]
    if spare:
        terms.append(jnp.zeros((spare, field.shape[1]), F32))
    out[rows:, :] = jnp.concatenate(terms, axis=0).astype(BF16)


def message(trial, field):
    height = trial.shape[0] + -(-3 * field.shape[0] // 16) * 16
    return pl.pallas_call(
        message_kernel,
        out_shape=jax.ShapeDtypeStruct((height, trial.shape[1]), trial.dtype),
        in_specs=[whole()] * 2,
        out_specs=whole(),
        compiler_params=pltpu.CompilerParams(vmem_limit_bytes=SMALL_LIMIT),
        name="message",
    )(trial, field)


def fields_kernel(n, per, share, branches, *refs):
    messages, fields = refs[:n], refs[n]
    walk, q = place()
    rows = fields.shape[2]
    places = picks(branches, walk * per, per, q, share)[0]
    walker = lax.broadcasted_iota(jnp.int32, (per, rows), 0)
    for k in range(n):
        terms = messages[k][rows:, :].astype(F32)
        value = terms[:per] + terms[per : 2 * per] + terms[2 * per : 3 * per]
        chosen = [jnp.sum(jnp.where(walker == p, value, 0.0), axis=0, keepdims=True) for p in places]
        fields[pl.ds(q ^ k, 1), :, :] = jnp.concatenate(chosen, axis=0)[None]


def pick_fields(n, per, share, branches, messages):
    return pl.pallas_call(
        functools.partial(fields_kernel, n, per, share),
        out_shape=jax.ShapeDtypeStruct((n, share, messages[0].shape[1]), F32),
        in_specs=[whole(pltpu.SMEM)] + [whole()] * n,
        out_specs=whole(),
        compiler_params=pltpu.CompilerParams(vmem_limit_bytes=SMALL_LIMIT),
        name="fields",
    )(branches, *messages)


def green_kernel(n, share, *refs):
    blocks, messages, fields = refs[:n], refs[n : 2 * n], refs[2 * n]
    green, moved, state = refs[2 * n + 1 :]
    walk, q = place()
    rows, electrons = blocks[0].shape[1:]
    spare = jnp.zeros((-share % 8, rows), F32)
    columns = []
    for k in range(n):
        lines = fields[pl.ds(q ^ k, 1), :, :].reshape(share, rows)
        columns.append((jnp.concatenate([lines, spare], axis=0) if share % 8 else lines).T)
    for i in range(share):
        transposed = jnp.zeros((electrons, electrons), F32)
        for k in range(n):
            part = (blocks[k][i].astype(F32) * columns[k][:, i : i + 1]).astype(BF16)
            moved[i, k * rows : (k + 1) * rows, :] = part
            transposed = transposed + dot(part, messages[k][:rows, :], ((0,), (0,)))
        size = jnp.abs(transposed)
        scale = jnp.max(jnp.sum(size, axis=0)) * jnp.max(jnp.sum(size, axis=1))
        start = transposed / scale
        high, low = split(transposed)
        start_high, start_low = split(start)
        across = ((0,), (0,))
        state[i, :electrons, :] = start
        state[i, electrons:, :] = dot(high, start_high, across) + (
            dot(high, start_low, across) + dot(low, start_high, across)
        )

    def advance(step, carry):
        for i in range(share):
            now = state[i]
            high, low = split(now)
            right_high, right_low = high[electrons:], low[electrons:]
            product = dot(high, right_high) + (dot(high, right_low) + dot(low, right_high))
            state[i] = 2.0 * now - product
        return carry

    lax.fori_loop(0, ITERS - 1, advance, 0)
    for i in range(share):
        now = state[i]
        high, low = split(now)
        left_high, left_low = high[:electrons], low[:electrons]
        right_high, right_low = high[electrons:], low[electrons:]
        product = dot(left_high, right_high) + (dot(left_high, right_low) + dot(left_low, right_high))
        inverse = (2.0 * now[:electrons] - product).astype(BF16)
        for k in range(n):
            at = pl.multiple_of((q ^ k) * rows, rows)
            green[pl.ds(at, rows), i * electrons : (i + 1) * electrons] = dot(
                moved[i, k * rows : (k + 1) * rows, :], inverse
            ).astype(BF16)


def make_green(n, share, blocks, messages, fields):
    rows, electrons = blocks[0].shape[1:]
    flops = share * (8 * rows * n * electrons**2 + 2 * 6 * ITERS * electrons**3)
    return pl.pallas_call(
        functools.partial(green_kernel, n, share),
        out_shape=jax.ShapeDtypeStruct((n * rows, share * electrons), BF16),
        in_specs=[whole()] * (2 * n + 1),
        out_specs=whole(),
        scratch_shapes=[
            pltpu.VMEM((share, n * rows, electrons), BF16),
            pltpu.VMEM((share, 2 * electrons, electrons), F32),
        ],
        compiler_params=pltpu.CompilerParams(vmem_limit_bytes=VMEM_LIMIT),
        cost_estimate=pl.CostEstimate(flops=flops, bytes_accessed=3 * 2**20, transcendentals=0),
        name="green",
    )(*blocks, *messages, fields)


def contract_kernel(share, first, pieces, count, going_on, *refs):
    vectors, green = refs[: pieces * count], refs[pieces * count]
    before = refs[pieces * count + 1 :][: count if going_on else 0]
    outs, both = refs[-1 - count : -1], refs[-1]
    electrons = both.shape[0]
    half = electrons // 2
    parity = lax.axis_index("walk") & 1
    row = lax.broadcasted_iota(jnp.int32, (half, half), 0)
    column = lax.broadcasted_iota(jnp.int32, (half, half), 1)
    out_row = lax.broadcasted_iota(jnp.int32, (8, 128), 0)
    lane = lax.broadcasted_iota(jnp.int32, (8, 128), 1)
    for v in range(count):
        held = before[v][...] if going_on else jnp.zeros((8, 128), F32)
        mine = vectors[v * pieces : (v + 1) * pieces]
        for g in range(mine[0].shape[0]):
            if pieces == 1:
                full = dot(mine[0][g], green[...])
                upper, lower = full[:half], full[half:]
            else:
                for at, piece in zip((parity, 1 - parity), mine):
                    both[pl.ds(pl.multiple_of(at * half, half), half), :] = dot(piece[g], green[...])
                upper, lower = both[:half], both[half:]
            for i in range(share):
                left, middle, right = i * electrons, i * electrons + half, (i + 1) * electrons
                a, b = upper[:, left:middle], upper[:, middle:right]
                c, d = lower[:, left:middle], lower[:, middle:right]
                trace = jnp.sum(jnp.where(row == column, a + d, 0.0))
                exchange = -0.5 * jnp.sum(a * a.T + d * d.T + 2.0 * (b * c.T))
                here = out_row == (first + g) * share + i
                held = jnp.where(here & (lane == 0), trace, held)
                held = jnp.where(here & (lane == 1), exchange, held)
        outs[v][...] = held


def contract(share, first, groups, green, before=(), after=()):
    vectors = [v for group in groups for v in group]
    electrons = green.shape[1] // share
    return pl.pallas_call(
        functools.partial(contract_kernel, share, first, len(groups[0]), len(groups), bool(before)),
        out_shape=[jax.ShapeDtypeStruct((8, 128), F32)] * len(groups),
        in_specs=[whole()] * (len(vectors) + 1 + len(before)) + [whole(pl.ANY)] * len(after),
        out_specs=[whole()] * len(groups),
        scratch_shapes=[pltpu.VMEM((electrons, green.shape[1]), F32)],
        compiler_params=pltpu.CompilerParams(vmem_limit_bytes=VMEM_LIMIT),
        cost_estimate=pl.CostEstimate(
            flops=sum(2 * v.size * green.shape[1] for v in vectors),
            bytes_accessed=sum(2 * v.size for v in vectors) + 2 * green.size,
            transcendentals=0,
        ),
        name="contract",
    )(*vectors, green, *before, *after)


def unpack_kernel(n, per, share, branches, counts, *refs):
    arrived, force, exchange = refs[:n], refs[n], refs[n + 1]
    walk, q = place()
    vectors = force.shape[0]
    walker = lax.broadcasted_iota(jnp.int32, force.shape, 1)
    vector = lax.broadcasted_iota(jnp.int32, force.shape, 0)
    force_all = jnp.zeros(force.shape, F32)
    exchange_all = jnp.zeros(force.shape, F32)
    for k in range(n):
        places = picks(branches, walk * per, per, walk ^ q ^ k, share)[0]
        for r in range(share):
            for g in range(vectors):
                here = (walker == places[r]) & (vector == g)
                force_all = jnp.where(here, arrived[k][g * share + r, 0], force_all)
                exchange_all = jnp.where(here, arrived[k][g * share + r, 1], exchange_all)
    living = (walker < counts[0]).astype(F32)
    force[...] = force_all * living
    exchange[...] = exchange_all * living


def unpack(n, per, share, vectors, branches, counts, arrived):
    return pl.pallas_call(
        functools.partial(unpack_kernel, n, per, share),
        out_shape=[jax.ShapeDtypeStruct((vectors, per), F32)] * 2,
        in_specs=[whole(pltpu.SMEM)] * (2 + n),
        out_specs=[whole()] * 2,
        compiler_params=pltpu.CompilerParams(vmem_limit_bytes=SMALL_LIMIT),
        name="unpack",
    )(branches, counts, *arrived)


def at_the_source(walkers, trial_orbitals, cholesky, branches, counts, field):
    n = lax.axis_size("walk")
    per = walkers.shape[0]
    share = per // n
    row_size = lax.axis_size("row")
    vectors = cholesky.shape[0]
    pairs = [(w, q) for w in range(n) for q in range(n)]
    move = lambda x, k: lax.ppermute(x, SR, [(i, i ^ k) for i in range(n)])
    swap = lambda x: lax.ppermute(x, "walk", [(w, w ^ 1) for w in range(n)])
    ask = lambda x: lax.ppermute(x, ALL, [(w * n + q, q * n + (w ^ q)) for w, q in pairs])
    answer = lambda x, k: lax.ppermute(x, ALL, [(w * n + q, (w ^ q) * n + (q ^ k)) for w, q in pairs])
    near = [k for k in range(n) if k < row_size]
    far = [k for k in range(n) if k >= row_size]

    def spread(x):
        held = {}
        for k in far:
            low = k & (row_size - 1)
            held[k] = move(held[k ^ low], low) if low else move(x, k)
        return held

    def along(held):
        return {k: move(held[k & ~(row_size - 1)], k & (row_size - 1)) if k & (row_size - 1) else held[k] for k in far}

    ordered = lambda x, *first: lax.optimization_barrier((x,) + first)[0]
    heads = [k for k in far if not k & (row_size - 1)]
    own = message(trial_orbitals, field)
    messages = {0: own, **spread(own)}
    messages.update({k: move(own, k) for k in near[1:]})
    messages = [messages[k] for k in range(n)]
    *sends, direct, shared = select(n, per, share, ordered(branches, own), walkers, cholesky)
    blocks = [sends[0]] + [move(sends[k], k) for k in range(1, n)]
    asked = ask(pick_fields(n, per, share, branches, messages))
    shared = ordered(shared, *messages[1 : far[0] + 1])
    crossed = {k: move(shared, k) for k in heads}
    direct = ordered(direct, *messages)
    direct = {k: move(direct, k) for k in heads}
    other = along({k: swap(x) for k, x in crossed.items()})
    crossed = along(crossed)
    close = [cholesky] + [move(ordered(cholesky, asked, *blocks), k) for k in near[1:]]
    green = make_green(n, share, blocks, messages, asked)
    direct = along({k: ordered(x, green) for k, x in direct.items()})
    results = contract(share, 0, [[x] for x in close], green)
    late = contract(share, vectors - vectors // 2, [[crossed[k], other[k]] for k in far], green, after=results[:1])
    late = contract(share, 0, [[direct[k]] for k in far], green, late)
    arrived = [answer(x, k) for k, x in enumerate(list(results) + list(late))]
    return tuple(x.T for x in unpack(n, per, share, vectors, branches, counts, arrived))


def newton_schulz(intersection):
    column_max = jnp.max(jnp.sum(jnp.abs(intersection), axis=0))
    row_max = jnp.max(jnp.sum(jnp.abs(intersection), axis=1))
    inverse = intersection.T / (column_max * row_max)
    twice_identity = 2.0 * jnp.eye(intersection.shape[0], dtype=intersection.dtype)
    for iteration in range(ITERS):
        inverse = jnp.dot(
            inverse,
            twice_identity - jnp.dot(intersection, inverse, precision=HIGHEST),
            precision=HIGHEST,
        )
    return inverse


def pick(array, indices):
    return jnp.concatenate(
        [lax.dynamic_slice_in_dim(array, indices[i], 1, 0) for i in range(indices.shape[0])], axis=0
    )


def at_the_target(walkers, trial_orbitals, cholesky, branches, counts, field):
    walk_size = lax.axis_size("walk")
    position = lax.axis_index("walk")
    per_device, row_count, electrons = walkers.shape
    capacity = (per_device + walk_size - 1) // walk_size
    sender = branches.reshape(walk_size, per_device) // per_device
    local_index = branches.reshape(walk_size, per_device) % per_device
    same_sender = sender[:, :, None] == sender[:, None, :]
    earlier = jnp.arange(per_device)[None, :] < jnp.arange(per_device)[:, None]
    arrival_rank = jnp.sum(same_sender & earlier[None], axis=2)
    wanted = (sender[:, None, :] == position) & (
        arrival_rank[:, None, :] == jnp.arange(capacity, dtype=jnp.int32)[None, :, None]
    )
    chosen = jnp.sum(jnp.where(wanted, local_index[:, None, :], 0), axis=2).reshape(-1)
    outgoing = pick(walkers, chosen).reshape(walk_size, capacity, row_count, electrons)
    arrived = lax.all_to_all(outgoing, "walk", split_axis=0, concat_axis=0, tiled=True)
    my_sender = lax.dynamic_index_in_dim(sender, position, 0, keepdims=False)
    my_rank = lax.dynamic_index_in_dim(arrival_rank, position, 0, keepdims=False)
    arrived_flat = arrived.reshape(walk_size * capacity, row_count, electrons)
    migrated = pick(arrived_flat, my_sender * capacity + my_rank)
    propagated = (migrated.astype(F32) * field[:, :, None]).astype(BF16)
    everything = lax.all_gather(propagated, SR, axis=1, tiled=True)
    shard_count = lax.axis_size(SR)
    share = per_device // shard_count
    trial_whole = lax.all_gather(trial_orbitals, SR, axis=0, tiled=True)
    own_walkers = lax.dynamic_slice_in_dim(everything, lax.axis_index(SR) * share, share, 0)
    intersection = jnp.einsum("mn,wmk->wnk", trial_whole, own_walkers, preferred_element_type=F32)
    inverse = jax.vmap(newton_schulz)(intersection).astype(BF16)
    inverses = lax.all_gather(inverse, SR, axis=0, tiled=True)
    green = jnp.einsum("wmn,wnk->wmk", everything, inverses, preferred_element_type=F32).astype(BF16)
    contracted = jnp.einsum("gnm,wmk->wgnk", cholesky, green, preferred_element_type=F32)
    living = (jnp.arange(per_device, dtype=jnp.int32) < counts[0]).astype(F32)[:, None]
    force_bias = jnp.trace(contracted, axis1=2, axis2=3) * living
    exchange_energy = -0.5 * jnp.einsum("wgnk,wgkn->wg", contracted, contracted) * living
    return (force_bias, exchange_energy)


def on_device(walkers, trial_orbitals, cholesky, branches, counts, field):
    walk_size, shard_count = lax.axis_size("walk"), lax.axis_size(SR)
    per = walkers.shape[0]
    if walk_size == shard_count and per % walk_size == 0 and not walk_size & (walk_size - 1):
        if 2 <= cholesky.shape[0] <= 8 // (per // walk_size):
            return at_the_source(walkers, trial_orbitals, cholesky, branches, counts, field)
    return at_the_target(walkers, trial_orbitals, cholesky, branches, counts, field)


def solution(mesh):
    return jax.shard_map(
        on_device,
        mesh=mesh,
        in_specs=(
            P(("parts", "walk"), SR, None),
            P(("parts",) + SR, None),
            P(("parts",) + SR, None, None),
            P("parts"),
            P(("parts", "walk")),
            P(("parts", "walk"), SR),
        ),
        out_specs=(P(("parts", "walk"), SR), P(("parts", "walk"), SR)),
        check_vma=False,
    )
```

```python
import functools

import jax
import jax.numpy as jnp
from jax import lax
from jax.experimental import pallas as pl
from jax.experimental.pallas import tpu as pltpu
from jax.sharding import PartitionSpec as P

ITERS = 10
SR = ("slab", "row")
ALL = ("walk", "slab", "row")
F32 = jnp.float32
BF16 = jnp.bfloat16
VMEM_LIMIT = 24 * 2**20
SMALL_LIMIT = 2**20
HIGHEST = lax.Precision.HIGHEST


def dot(a, b, dims=((1,), (0,))):
    return lax.dot_general(a, b, (dims, ((), ())), preferred_element_type=F32)


def split(x):
    high = x.astype(BF16)
    return high, (x - high.astype(F32)).astype(BF16)


def place():
    return lax.axis_index("walk"), lax.axis_index("slab") * lax.axis_size("row") + lax.axis_index("row")


def whole(memory=pltpu.VMEM):
    return pl.BlockSpec(memory_space=memory)


def picks(branches, start, per, sender, share):
    places, olds = [jnp.int32(0)] * share, [jnp.int32(0)] * share
    rank = jnp.int32(0)
    for i in range(per):
        branch = branches[start + i]
        hit = lax.div(branch, per) == sender
        old = lax.rem(branch, per)
        for r in range(share):
            here = hit & (rank == r)
            places[r] = jnp.where(here, i, places[r])
            olds[r] = jnp.where(here, old, olds[r])
        rank = rank + hit.astype(jnp.int32)
    return places, olds


def select_kernel(n, per, share, branches, walkers, *refs):
    sends, sems = refs[:n], refs[n]
    walk, q = place()
    copies = []
    for k in list(range(1, n)) + [0]:
        olds = picks(branches, (q ^ k ^ walk) * per, per, walk, share)[1]
        for r in range(share):
            copies.append(pltpu.make_async_copy(walkers.at[olds[r]], sends[k].at[r], sems.at[k, r]))
            copies[-1].start()
    for copy in copies:
        copy.wait()


def select(n, per, share, branches, walkers):
    rows, electrons = walkers.shape[1:]
    return pl.pallas_call(
        functools.partial(select_kernel, n, per, share),
        out_shape=[jax.ShapeDtypeStruct((share, rows, electrons), walkers.dtype)] * n,
        in_specs=[whole(pltpu.SMEM), whole(pl.ANY)],
        out_specs=[whole(pl.ANY)] * n,
        scratch_shapes=[pltpu.SemaphoreType.DMA((n, share))],
        compiler_params=pltpu.CompilerParams(vmem_limit_bytes=SMALL_LIMIT),
        name="select",
    )(branches, walkers)


def message_kernel(trial, field, cholesky, out, shared, terms, sems):
    walk, _ = place()
    rows, height, count = trial.shape[0], cholesky.shape[0], shared.shape[0]
    start = height - 2 * count + (walk & 1) * count
    copies = [
        pltpu.make_async_copy(cholesky.at[pl.ds(pl.multiple_of(start, 16), count)], shared, sems.at[0]),
        pltpu.make_async_copy(trial, out.at[pl.ds(0, rows)], sems.at[1]),
        pltpu.make_async_copy(terms, out.at[pl.ds(rows, terms.shape[0])], sems.at[2]),
    ]
    copies[0].start()
    copies[1].start()
    rest, parts = field[...], []
    for _ in range(3):
        parts.append(rest.astype(BF16).astype(F32))
        rest = rest - parts[-1]
    spare = terms.shape[0] - 3 * field.shape[0]
    if spare:
        parts.append(jnp.zeros((spare, field.shape[1]), F32))
    terms[...] = jnp.concatenate(parts, axis=0).astype(BF16)
    copies[2].start()
    for copy in copies:
        copy.wait()


def message(trial, field, cholesky, shared_rows):
    extra = -(-3 * field.shape[0] // 16) * 16
    return pl.pallas_call(
        message_kernel,
        out_shape=[
            jax.ShapeDtypeStruct((trial.shape[0] + extra, trial.shape[1]), trial.dtype),
            jax.ShapeDtypeStruct((shared_rows, cholesky.shape[1]), cholesky.dtype),
        ],
        in_specs=[whole(pl.ANY), whole(), whole(pl.ANY)],
        out_specs=[whole(pl.ANY)] * 2,
        scratch_shapes=[pltpu.VMEM((extra, trial.shape[1]), BF16), pltpu.SemaphoreType.DMA((3,))],
        compiler_params=pltpu.CompilerParams(vmem_limit_bytes=SMALL_LIMIT),
        name="message",
    )(trial, field, cholesky)


def fields_kernel(n, per, share, branches, *refs):
    messages, fields = refs[:n], refs[n]
    walk, q = place()
    rows = fields.shape[2]
    places = picks(branches, walk * per, per, walk ^ q, share)[0]
    walker = lax.broadcasted_iota(jnp.int32, (per, rows), 0)
    for k in range(n):
        terms = messages[k][rows:, :].astype(F32)
        value = terms[:per] + terms[per : 2 * per] + terms[2 * per : 3 * per]
        chosen = [jnp.sum(jnp.where(walker == p, value, 0.0), axis=0, keepdims=True) for p in places]
        fields[pl.ds(q ^ k, 1), :, :] = jnp.concatenate(chosen, axis=0)[None]


def pick_fields(n, per, share, branches, messages):
    return pl.pallas_call(
        functools.partial(fields_kernel, n, per, share),
        out_shape=jax.ShapeDtypeStruct((n, share, messages[0].shape[1]), F32),
        in_specs=[whole(pltpu.SMEM)] + [whole()] * n,
        out_specs=whole(),
        compiler_params=pltpu.CompilerParams(vmem_limit_bytes=SMALL_LIMIT),
        name="fields",
    )(branches, *messages)


def green_kernel(n, share, *refs):
    blocks, messages, fields = refs[:n], refs[n : 2 * n], refs[2 * n]
    green, moved, state = refs[2 * n + 1 :]
    walk, q = place()
    rows, electrons = blocks[0].shape[1:]
    spare = jnp.zeros((-share % 8, rows), F32)
    columns = []
    for k in range(n):
        lines = fields[pl.ds(q ^ k, 1), :, :].reshape(share, rows)
        columns.append((jnp.concatenate([lines, spare], axis=0) if share % 8 else lines).T)
    for i in range(share):
        transposed = jnp.zeros((electrons, electrons), F32)
        for k in range(n):
            part = (blocks[k][i].astype(F32) * columns[k][:, i : i + 1]).astype(BF16)
            moved[i, k * rows : (k + 1) * rows, :] = part
            transposed = transposed + dot(part, messages[k][:rows, :], ((0,), (0,)))
        size = jnp.abs(transposed)
        scale = jnp.max(jnp.sum(size, axis=0)) * jnp.max(jnp.sum(size, axis=1))
        start = transposed / scale
        high, low = split(transposed)
        start_high, start_low = split(start)
        across = ((0,), (0,))
        state[i, :electrons, :] = start
        state[i, electrons:, :] = dot(high, start_high, across) + (
            dot(high, start_low, across) + dot(low, start_high, across)
        )

    def advance(step, carry):
        for i in range(share):
            now = state[i]
            high, low = split(now)
            right_high, right_low = high[electrons:], low[electrons:]
            product = dot(high, right_high) + (dot(high, right_low) + dot(low, right_high))
            state[i] = 2.0 * now - product
        return carry

    lax.fori_loop(0, ITERS - 1, advance, 0)
    for i in range(share):
        now = state[i]
        high, low = split(now)
        left_high, left_low = high[:electrons], low[:electrons]
        right_high, right_low = high[electrons:], low[electrons:]
        product = dot(left_high, right_high) + (dot(left_high, right_low) + dot(left_low, right_high))
        inverse = (2.0 * now[:electrons] - product).astype(BF16)
        for k in range(n):
            at = pl.multiple_of((q ^ k) * rows, rows)
            green[pl.ds(at, rows), i * electrons : (i + 1) * electrons] = dot(
                moved[i, k * rows : (k + 1) * rows, :], inverse
            ).astype(BF16)


def make_green(n, share, blocks, messages, fields):
    rows, electrons = blocks[0].shape[1:]
    flops = share * (8 * rows * n * electrons**2 + 2 * 6 * ITERS * electrons**3)
    return pl.pallas_call(
        functools.partial(green_kernel, n, share),
        out_shape=jax.ShapeDtypeStruct((n * rows, share * electrons), BF16),
        in_specs=[whole()] * (2 * n + 1),
        out_specs=whole(),
        scratch_shapes=[
            pltpu.VMEM((share, n * rows, electrons), BF16),
            pltpu.VMEM((share, 2 * electrons, electrons), F32),
        ],
        compiler_params=pltpu.CompilerParams(vmem_limit_bytes=VMEM_LIMIT),
        cost_estimate=pl.CostEstimate(flops=flops, bytes_accessed=3 * 2**20, transcendentals=0),
        name="green",
    )(*blocks, *messages, fields)


def report(share, held, index, upper, lower):
    half = upper.shape[0]
    row = lax.broadcasted_iota(jnp.int32, (half, half), 0)
    column = lax.broadcasted_iota(jnp.int32, (half, half), 1)
    out_row = lax.broadcasted_iota(jnp.int32, held.shape, 0)
    lane = lax.broadcasted_iota(jnp.int32, held.shape, 1)
    for i in range(share):
        left, middle, right = 2 * i * half, (2 * i + 1) * half, 2 * (i + 1) * half
        a, b = upper[:, left:middle], upper[:, middle:right]
        c, d = lower[:, left:middle], lower[:, middle:right]
        trace = jnp.sum(jnp.where(row == column, a + d, 0.0))
        exchange = -0.5 * jnp.sum(a * a.T + d * d.T + 2.0 * (b * c.T))
        here = out_row == index * share + i
        held = jnp.where(here & (lane == 0), trace, held)
        held = jnp.where(here & (lane == 1), exchange, held)
    return held


def near_kernel(share, count, height, *refs):
    vectors, green, outs = refs[:count], refs[count], refs[-count:]
    for v in range(count):
        held = jnp.zeros(outs[v].shape, F32)
        for g in range(vectors[v].shape[0] // height):
            full = dot(vectors[v][g * height : (g + 1) * height, :], green[...])
            held = report(share, held, g, full[: height // 2], full[height // 2 :])
        outs[v][...] = held


def shared_kernel(share, count, height, *refs):
    firsts, seconds, green = refs[:count], refs[count : 2 * count], refs[2 * count]
    outs, kept, both = refs[-2 * count - 1 : -count - 1], refs[-count - 1 : -1], refs[-1]
    parity = lax.axis_index("walk") & 1
    half = height // 2
    for v in range(count):
        rows = firsts[v].shape[0]
        for at, piece in ((parity, firsts[v]), (1 - parity, seconds[v])):
            both[pl.ds(pl.multiple_of(at * rows, 16), rows), :] = dot(piece[...], green[...])
        kept[v][...] = both[:half, :]
        held = jnp.zeros(outs[v].shape, F32)
        for g in range(1, (2 * rows + half) // height):
            start = g * height - half
            held = report(share, held, g, both[start : start + half, :], both[start + half : start + height, :])
        outs[v][...] = held


def direct_kernel(share, count, *refs):
    uppers, green, kept, before = refs[:count], refs[count], refs[count + 1 : 2 * count + 1], refs[2 * count + 1 : -count]
    outs = refs[-count:]
    for v in range(count):
        outs[v][...] = report(share, before[v][...], 0, dot(uppers[v][...], green[...]), kept[v][...])


def contract(kernel, count, vectors, green, *more, kept_rows=0, scratch_rows=0):
    wide = green.shape[1]
    kept = [jax.ShapeDtypeStruct((kept_rows, wide), F32)] * count if kept_rows else []
    return pl.pallas_call(
        kernel,
        out_shape=[jax.ShapeDtypeStruct((8, 128), F32)] * count + kept,
        in_specs=[whole()] * (len(vectors) + 1 + len(more)),
        out_specs=[whole()] * (count + len(kept)),
        scratch_shapes=[pltpu.VMEM((scratch_rows, wide), F32)] if scratch_rows else [],
        compiler_params=pltpu.CompilerParams(vmem_limit_bytes=VMEM_LIMIT),
        cost_estimate=pl.CostEstimate(
            flops=sum(2 * v.size * wide for v in vectors),
            bytes_accessed=sum(2 * v.size for v in vectors) + 2 * green.size,
            transcendentals=0,
        ),
        name="contract",
    )(*vectors, green, *more)


def unpack_kernel(n, per, share, branches, counts, *refs):
    arrived, force, exchange = refs[:n], refs[n], refs[n + 1]
    walk, q = place()
    vectors = force.shape[0]
    walker = lax.broadcasted_iota(jnp.int32, force.shape, 1)
    vector = lax.broadcasted_iota(jnp.int32, force.shape, 0)
    force_all = jnp.zeros(force.shape, F32)
    exchange_all = jnp.zeros(force.shape, F32)
    for k in range(n):
        places = picks(branches, walk * per, per, walk ^ q ^ k, share)[0]
        for r in range(share):
            for g in range(vectors):
                here = (walker == places[r]) & (vector == g)
                force_all = jnp.where(here, arrived[k][g * share + r, 0], force_all)
                exchange_all = jnp.where(here, arrived[k][g * share + r, 1], exchange_all)
    living = (walker < counts[0]).astype(F32)
    force[...] = force_all * living
    exchange[...] = exchange_all * living


def unpack(n, per, share, vectors, branches, counts, arrived):
    return pl.pallas_call(
        functools.partial(unpack_kernel, n, per, share),
        out_shape=[jax.ShapeDtypeStruct((vectors, per), F32)] * 2,
        in_specs=[whole(pltpu.SMEM)] * (2 + n),
        out_specs=[whole()] * 2,
        compiler_params=pltpu.CompilerParams(vmem_limit_bytes=SMALL_LIMIT),
        name="unpack",
    )(branches, counts, *arrived)


def at_the_source(walkers, trial_orbitals, cholesky, branches, counts, field):
    n = lax.axis_size("walk")
    per = walkers.shape[0]
    share = per // n
    row_size = lax.axis_size("row")
    vectors = cholesky.shape[0]
    pairs = [(w, q) for w in range(n) for q in range(n)]
    move = lambda x, k: lax.ppermute(x, SR, [(i, i ^ k) for i in range(n)])
    swap = lambda x: lax.ppermute(x, "walk", [(w, w ^ 1) for w in range(n)])
    ask = lambda x: lax.ppermute(x, ALL, [(w * n + q, (w ^ q) * n + q) for w, q in pairs])
    answer = lambda x, k: lax.ppermute(x, ALL, [(w * n + q, (w ^ q) * n + (q ^ k)) for w, q in pairs])
    near = [k for k in range(n) if k < row_size]
    far = [k for k in range(n) if k >= row_size]

    def spread(x):
        held = {}
        for k in far:
            low = k & (row_size - 1)
            held[k] = move(held[k ^ low], low) if low else move(x, k)
        return held

    def along(held):
        return {k: move(held[k & ~(row_size - 1)], k & (row_size - 1)) if k & (row_size - 1) else held[k] for k in far}

    ordered = lambda x, *first: lax.optimization_barrier((x,) + first)[0]
    heads = [k for k in far if not k & (row_size - 1)]
    height = cholesky.shape[1]
    rows = cholesky.reshape(vectors * height, cholesky.shape[2])
    direct_rows = height // 2
    shared_rows = (rows.shape[0] - direct_rows) // 2
    own, shared = message(trial_orbitals, field, rows, shared_rows)
    messages = {0: own, **spread(own)}
    messages.update({k: move(own, k) for k in near[1:]})
    messages = [messages[k] for k in range(n)]
    sends = select(n, per, share, ordered(branches, own), walkers)
    crossed = {k: move(shared, k) for k in heads}
    close = [rows] + [move(rows, k) for k in near[1:]]
    early = [messages[far[0]], *close[1:]]
    blocks = [sends[0]] + [
        move(ordered(sends[k], *(crossed.values() if k == n - 1 else early)), k) for k in range(1, n)
    ]
    asked = ask(pick_fields(n, per, share, branches, messages))
    direct = {k: move(ordered(rows[:direct_rows], asked), k) for k in heads}
    other = {k: swap(x) for k, x in crossed.items()}
    green = make_green(n, share, blocks, messages, asked)
    crossed, other, direct = (along({k: ordered(x, green) for k, x in held.items()}) for held in (crossed, other, direct))
    results = contract(functools.partial(near_kernel, share, len(near), height), len(near), close, green)
    late = contract(
        functools.partial(shared_kernel, share, len(far), height),
        len(far),
        [crossed[k] for k in far] + [other[k] for k in far],
        ordered(green, results[0]),
        kept_rows=direct_rows,
        scratch_rows=2 * shared_rows,
    )
    late = contract(
        functools.partial(direct_kernel, share, len(far)), len(far), [direct[k] for k in far], green,
        *late[len(far) :], *late[: len(far)],
    )
    arrived = [answer(x, k) for k, x in enumerate(list(results) + list(late))]
    return tuple(x.T for x in unpack(n, per, share, vectors, branches, counts, arrived))


def newton_schulz(intersection):
    column_max = jnp.max(jnp.sum(jnp.abs(intersection), axis=0))
    row_max = jnp.max(jnp.sum(jnp.abs(intersection), axis=1))
    inverse = intersection.T / (column_max * row_max)
    twice_identity = 2.0 * jnp.eye(intersection.shape[0], dtype=intersection.dtype)
    for iteration in range(ITERS):
        inverse = jnp.dot(
            inverse,
            twice_identity - jnp.dot(intersection, inverse, precision=HIGHEST),
            precision=HIGHEST,
        )
    return inverse


def pick(array, indices):
    return jnp.concatenate(
        [lax.dynamic_slice_in_dim(array, indices[i], 1, 0) for i in range(indices.shape[0])], axis=0
    )


def at_the_target(walkers, trial_orbitals, cholesky, branches, counts, field):
    walk_size = lax.axis_size("walk")
    position = lax.axis_index("walk")
    per_device, row_count, electrons = walkers.shape
    capacity = (per_device + walk_size - 1) // walk_size
    sender = branches.reshape(walk_size, per_device) // per_device
    local_index = branches.reshape(walk_size, per_device) % per_device
    same_sender = sender[:, :, None] == sender[:, None, :]
    earlier = jnp.arange(per_device)[None, :] < jnp.arange(per_device)[:, None]
    arrival_rank = jnp.sum(same_sender & earlier[None], axis=2)
    wanted = (sender[:, None, :] == position) & (
        arrival_rank[:, None, :] == jnp.arange(capacity, dtype=jnp.int32)[None, :, None]
    )
    chosen = jnp.sum(jnp.where(wanted, local_index[:, None, :], 0), axis=2).reshape(-1)
    outgoing = pick(walkers, chosen).reshape(walk_size, capacity, row_count, electrons)
    arrived = lax.all_to_all(outgoing, "walk", split_axis=0, concat_axis=0, tiled=True)
    my_sender = lax.dynamic_index_in_dim(sender, position, 0, keepdims=False)
    my_rank = lax.dynamic_index_in_dim(arrival_rank, position, 0, keepdims=False)
    arrived_flat = arrived.reshape(walk_size * capacity, row_count, electrons)
    migrated = pick(arrived_flat, my_sender * capacity + my_rank)
    propagated = (migrated.astype(F32) * field[:, :, None]).astype(BF16)
    everything = lax.all_gather(propagated, SR, axis=1, tiled=True)
    shard_count = lax.axis_size(SR)
    share = per_device // shard_count
    trial_whole = lax.all_gather(trial_orbitals, SR, axis=0, tiled=True)
    own_walkers = lax.dynamic_slice_in_dim(everything, lax.axis_index(SR) * share, share, 0)
    intersection = jnp.einsum("mn,wmk->wnk", trial_whole, own_walkers, preferred_element_type=F32)
    inverse = jax.vmap(newton_schulz)(intersection).astype(BF16)
    inverses = lax.all_gather(inverse, SR, axis=0, tiled=True)
    green = jnp.einsum("wmn,wnk->wmk", everything, inverses, preferred_element_type=F32).astype(BF16)
    contracted = jnp.einsum("gnm,wmk->wgnk", cholesky, green, preferred_element_type=F32)
    living = (jnp.arange(per_device, dtype=jnp.int32) < counts[0]).astype(F32)[:, None]
    force_bias = jnp.trace(contracted, axis1=2, axis2=3) * living
    exchange_energy = -0.5 * jnp.einsum("wgnk,wgkn->wg", contracted, contracted) * living
    return (force_bias, exchange_energy)


def on_device(walkers, trial_orbitals, cholesky, branches, counts, field):
    walk_size, shard_count = lax.axis_size("walk"), lax.axis_size(SR)
    per = walkers.shape[0]
    if walk_size == shard_count and per % walk_size == 0 and not walk_size & (walk_size - 1):
        if cholesky.shape[0] * (per // walk_size) <= 8 and cholesky.shape[1] % 64 == 0:
            return at_the_source(walkers, trial_orbitals, cholesky, branches, counts, field)
    return at_the_target(walkers, trial_orbitals, cholesky, branches, counts, field)


def solution(mesh):
    return jax.shard_map(
        on_device,
        mesh=mesh,
        in_specs=(
            P(("parts", "walk"), SR, None),
            P(("parts",) + SR, None),
            P(("parts",) + SR, None, None),
            P("parts"),
            P(("parts", "walk")),
            P(("parts", "walk"), SR),
        ),
        out_specs=(P(("parts", "walk"), SR), P(("parts", "walk"), SR)),
        check_vma=False,
    )
```

```python
import functools

import jax
import jax.numpy as jnp
from jax import lax
from jax.experimental import pallas as pl
from jax.experimental.pallas import tpu as pltpu
from jax.sharding import PartitionSpec as P

ITERS = 10
EARLY = 3
SR = ("slab", "row")
ALL = ("walk", "slab", "row")
F32 = jnp.float32
BF16 = jnp.bfloat16
VMEM_LIMIT = 24 * 2**20
SMALL_LIMIT = 2**20
HIGHEST = lax.Precision.HIGHEST


def dot(a, b, dims=((1,), (0,))):
    return lax.dot_general(a, b, (dims, ((), ())), preferred_element_type=F32)


def split(x):
    high = x.astype(BF16)
    return high, (x - high.astype(F32)).astype(BF16)


def place():
    return lax.axis_index("walk"), lax.axis_index("slab") * lax.axis_size("row") + lax.axis_index("row")


def whole(memory=pltpu.VMEM):
    return pl.BlockSpec(memory_space=memory)


def picks(branches, start, per, sender, share):
    places, olds = [jnp.int32(0)] * share, [jnp.int32(0)] * share
    rank = jnp.int32(0)
    for i in range(per):
        branch = branches[start + i]
        hit = lax.div(branch, per) == sender
        old = lax.rem(branch, per)
        for r in range(share):
            here = hit & (rank == r)
            places[r] = jnp.where(here, i, places[r])
            olds[r] = jnp.where(here, old, olds[r])
        rank = rank + hit.astype(jnp.int32)
    return places, olds


def select_kernel(n, per, share, branches, walkers, *refs):
    sends, sems = refs[:n], refs[n]
    walk, q = place()
    copies = []
    for k in list(range(1, n)) + [0]:
        olds = picks(branches, (q ^ k ^ walk) * per, per, walk, share)[1]
        for r in range(share):
            copies.append(pltpu.make_async_copy(walkers.at[olds[r]], sends[k].at[r], sems.at[k, r]))
            copies[-1].start()
    for copy in copies:
        copy.wait()


def select(n, per, share, branches, walkers):
    rows, electrons = walkers.shape[1:]
    return pl.pallas_call(
        functools.partial(select_kernel, n, per, share),
        out_shape=[jax.ShapeDtypeStruct((share, rows, electrons), walkers.dtype)] * n,
        in_specs=[whole(pltpu.SMEM), whole(pl.ANY)],
        out_specs=[whole(pl.ANY)] * n,
        scratch_shapes=[pltpu.SemaphoreType.DMA((n, share))],
        compiler_params=pltpu.CompilerParams(vmem_limit_bytes=SMALL_LIMIT),
        name="select",
    )(branches, walkers)


def message_kernel(trial, field, out):
    rows = trial.shape[0]
    out[:rows, :] = trial[...]
    rest, parts = field[...], []
    for _ in range(3):
        parts.append(rest.astype(BF16).astype(F32))
        rest = rest - parts[-1]
    spare = out.shape[0] - rows - 3 * field.shape[0]
    if spare:
        parts.append(jnp.zeros((spare, field.shape[1]), F32))
    out[rows:, :] = jnp.concatenate(parts, axis=0).astype(BF16)


def message(trial, field):
    height = trial.shape[0] + -(-3 * field.shape[0] // 16) * 16
    return pl.pallas_call(
        message_kernel,
        out_shape=jax.ShapeDtypeStruct((height, trial.shape[1]), trial.dtype),
        in_specs=[whole()] * 2,
        out_specs=whole(),
        compiler_params=pltpu.CompilerParams(vmem_limit_bytes=SMALL_LIMIT),
        name="message",
    )(trial, field)


def fields_kernel(n, per, share, branches, *refs):
    messages, fields = refs[:n], refs[n]
    walk, q = place()
    rows = fields.shape[2]
    places = picks(branches, walk * per, per, walk ^ q, share)[0]
    walker = lax.broadcasted_iota(jnp.int32, (per, rows), 0)
    for k in range(n):
        terms = messages[k][rows:, :].astype(F32)
        value = terms[:per] + terms[per : 2 * per] + terms[2 * per : 3 * per]
        chosen = [jnp.sum(jnp.where(walker == p, value, 0.0), axis=0, keepdims=True) for p in places]
        fields[pl.ds(q ^ k, 1), :, :] = jnp.concatenate(chosen, axis=0)[None]


def pick_fields(n, per, share, branches, messages):
    return pl.pallas_call(
        functools.partial(fields_kernel, n, per, share),
        out_shape=jax.ShapeDtypeStruct((n, share, messages[0].shape[1]), F32),
        in_specs=[whole(pltpu.SMEM)] + [whole()] * n,
        out_specs=whole(),
        compiler_params=pltpu.CompilerParams(vmem_limit_bytes=SMALL_LIMIT),
        name="fields",
    )(branches, *messages)


def turn_kernel(n, per, share, branches, counts, *refs):
    messages, turned, masks = refs[:n], refs[n], refs[n + 1]
    walk, q = place()
    rows = turned.shape[1] // n
    for k in range(n):
        turned[:, k * rows : (k + 1) * rows] = messages[k][:rows, :].T
    lane = lax.broadcasted_iota(jnp.int32, (1, 128), 1)
    for k in range(n):
        places = picks(branches, walk * per, per, walk ^ q ^ k, share)[0]
        for r in range(share):
            here = (lane == places[r]) & (places[r] < counts[0])
            masks[k * share + r : k * share + r + 1, :] = here.astype(F32)


def turn(n, per, share, branches, counts, messages):
    electrons = messages[0].shape[1]
    rows = n * (messages[0].shape[0] - -(-3 * per // 16) * 16)
    return pl.pallas_call(
        functools.partial(turn_kernel, n, per, share),
        out_shape=[
            jax.ShapeDtypeStruct((electrons, rows), messages[0].dtype),
            jax.ShapeDtypeStruct((n * share, 128), F32),
        ],
        in_specs=[whole(pltpu.SMEM)] * 2 + [whole()] * n,
        out_specs=[whole()] * 2,
        compiler_params=pltpu.CompilerParams(vmem_limit_bytes=SMALL_LIMIT),
        name="turn",
    )(branches, counts, *messages)


def squared(high, low):
    mixed = dot(high, low)
    return dot(high, high) + (mixed + mixed.T)


def green_kernel(n, share, *refs):
    blocks, turned, fields = refs[:n], refs[n], refs[n + 1]
    green, moved, left, right = refs[n + 2 :]
    q = place()[1]
    rows, electrons = blocks[0].shape[1:]
    spare = jnp.zeros((-share % 8, rows), F32)
    for k in range(n):
        lines = fields[pl.ds(q ^ k, 1), :, :].reshape(share, rows)
        columns = (jnp.concatenate([lines, spare], axis=0) if share % 8 else lines).T
        for i in range(share):
            moved[k * rows : (k + 1) * rows, i * electrons : (i + 1) * electrons] = (
                blocks[k][i].astype(F32) * columns[:, i : i + 1]
            ).astype(BF16)
    overlaps = dot(turned[...], moved[...])
    for i in range(share):
        overlap = overlaps[:, i * electrons : (i + 1) * electrons]
        size = jnp.abs(overlap)
        scale = jnp.max(jnp.sum(size, axis=0)) * jnp.max(jnp.sum(size, axis=1))
        left[i] = overlap.T / scale
        high, low = split(overlap)
        mixed = dot(high, low, ((1,), (1,)))
        right[i] = (dot(high, high, ((1,), (1,))) + (mixed + mixed.T)) / scale

    def advance(exact, step, carry):
        for i in range(share):
            now, matrix = left[i], right[i]
            high, low = split(matrix)
            left_high, left_low = split(now)
            product = dot(left_high, high)
            if exact:
                product = product + (dot(left_high, low) + dot(left_low, high))
            left[i] = 2.0 * now - product
            right[i] = 2.0 * matrix - squared(high, low)
        return carry

    lax.fori_loop(0, EARLY, functools.partial(advance, False), 0)
    lax.fori_loop(EARLY, ITERS - 1, functools.partial(advance, True), 0)
    for i in range(share):
        high, low = split(right[i])
        left_high, left_low = split(left[i])
        product = dot(left_high, high) + (dot(left_high, low) + dot(left_low, high))
        inverse = (2.0 * left[i] - product).astype(BF16)
        for k in range(n):
            at = pl.multiple_of((q ^ k) * rows, rows)
            green[pl.ds(at, rows), i * electrons : (i + 1) * electrons] = dot(
                moved[k * rows : (k + 1) * rows, i * electrons : (i + 1) * electrons], inverse
            ).astype(BF16)


def make_green(n, share, blocks, turned, fields):
    rows, electrons = blocks[0].shape[1:]
    return pl.pallas_call(
        functools.partial(green_kernel, n, share),
        out_shape=jax.ShapeDtypeStruct((n * rows, share * electrons), BF16),
        in_specs=[whole()] * (n + 2),
        out_specs=whole(),
        scratch_shapes=[
            pltpu.VMEM((n * rows, share * electrons), BF16),
            pltpu.VMEM((share, electrons, electrons), F32),
            pltpu.VMEM((share, electrons, electrons), F32),
        ],
        compiler_params=pltpu.CompilerParams(vmem_limit_bytes=VMEM_LIMIT),
        name="green",
    )(*blocks, turned, fields)


def report(share, held, index, upper, lower):
    half = upper.shape[0]
    row = lax.broadcasted_iota(jnp.int32, (half, half), 0)
    column = lax.broadcasted_iota(jnp.int32, (half, half), 1)
    out_row = lax.broadcasted_iota(jnp.int32, held.shape, 0)
    for i in range(share):
        left, middle, right = 2 * i * half, (2 * i + 1) * half, 2 * (i + 1) * half
        a, b = upper[:, left:middle], upper[:, middle:right]
        c, d = lower[:, left:middle], lower[:, middle:right]
        trace = jnp.sum(jnp.where(row == column, a + d, 0.0))
        exchange = -0.5 * jnp.sum(a * a.T + d * d.T + 2.0 * (b * c.T))
        held = jnp.where(out_row == index * share + i, trace, held)
        held = jnp.where(out_row == held.shape[0] // 2 + index * share + i, exchange, held)
    return held


def near_kernel(share, count, height, *refs):
    vectors, green, outs = refs[:count], refs[count], refs[-count:]
    for v in range(count):
        held = jnp.zeros(outs[v].shape, F32)
        for g in range(vectors[v].shape[0] // height):
            full = dot(vectors[v][g * height : (g + 1) * height, :], green[...])
            held = report(share, held, g, full[: height // 2], full[height // 2 :])
        outs[v][...] = held


def shared_kernel(share, count, height, *refs):
    firsts, seconds, green = refs[:count], refs[count : 2 * count], refs[2 * count]
    outs, kept, both = refs[-2 * count - 1 : -count - 1], refs[-count - 1 : -1], refs[-1]
    parity = lax.axis_index("walk") & 1
    half = height // 2
    for v in range(count):
        rows = firsts[v].shape[0]
        for at, piece in ((parity, firsts[v]), (1 - parity, seconds[v])):
            both[pl.ds(pl.multiple_of(at * rows, 16), rows), :] = dot(piece[...], green[...])
        kept[v][...] = both[:half, :]
        held = jnp.zeros(outs[v].shape, F32)
        for g in range(1, (2 * rows + half) // height):
            start = g * height - half
            held = report(share, held, g, both[start : start + half, :], both[start + half : start + height, :])
        outs[v][...] = held


def direct_kernel(share, count, *refs):
    uppers, green, kept, before = refs[:count], refs[count], refs[count + 1 : 2 * count + 1], refs[2 * count + 1 : -count]
    outs = refs[-count:]
    for v in range(count):
        outs[v][...] = report(share, before[v][...], 0, dot(uppers[v][...], green[...]), kept[v][...])


def contract(kernel, count, vectors, green, *more, kept_rows=0, scratch_rows=0):
    wide = green.shape[1]
    kept = [jax.ShapeDtypeStruct((kept_rows, wide), F32)] * count if kept_rows else []
    return pl.pallas_call(
        kernel,
        out_shape=[jax.ShapeDtypeStruct((8, 128), F32)] * count + kept,
        in_specs=[whole()] * (len(vectors) + 1 + len(more)),
        out_specs=[whole()] * (count + len(kept)),
        scratch_shapes=[pltpu.VMEM((scratch_rows, wide), F32)] if scratch_rows else [],
        compiler_params=pltpu.CompilerParams(vmem_limit_bytes=VMEM_LIMIT),
        cost_estimate=pl.CostEstimate(
            flops=sum(2 * v.size * wide for v in vectors),
            bytes_accessed=sum(2 * v.size for v in vectors) + 2 * green.size,
            transcendentals=0,
        ),
        name="contract",
    )(*vectors, green, *more)


def unpack_kernel(n, share, masks, *refs):
    arrived, outs = refs[:n], refs[n:]
    vectors, per = outs[0].shape
    for which, out in enumerate(outs):
        for g in range(vectors):
            line = jnp.zeros((1, 128), F32)
            for k in range(n):
                for r in range(share):
                    at = which * (arrived[k].shape[0] // 2) + g * share + r
                    line = jnp.where(masks[k * share + r : k * share + r + 1, :] > 0.0, arrived[k][at : at + 1, :], line)
            out[g : g + 1, :] = line[:, :per]


def unpack(n, per, share, vectors, masks, arrived):
    return pl.pallas_call(
        functools.partial(unpack_kernel, n, share),
        out_shape=[jax.ShapeDtypeStruct((vectors, per), F32)] * 2,
        in_specs=[whole()] * (1 + n),
        out_specs=[whole()] * 2,
        compiler_params=pltpu.CompilerParams(vmem_limit_bytes=SMALL_LIMIT),
        name="unpack",
    )(masks, *arrived)


def at_the_source(walkers, trial_orbitals, cholesky, branches, counts, field):
    n = lax.axis_size("walk")
    per = walkers.shape[0]
    share = per // n
    row_size = lax.axis_size("row")
    vectors = cholesky.shape[0]
    pairs = [(w, q) for w in range(n) for q in range(n)]
    move = lambda x, k: lax.ppermute(x, SR, [(i, i ^ k) for i in range(n)])
    swap = lambda x: lax.ppermute(x, "walk", [(w, w ^ 1) for w in range(n)])
    ask = lambda x: lax.ppermute(x, ALL, [(w * n + q, (w ^ q) * n + q) for w, q in pairs])
    answer = lambda x, k: lax.ppermute(x, ALL, [(w * n + q, (w ^ q) * n + (q ^ k)) for w, q in pairs])
    near = [k for k in range(n) if k < row_size]
    far = [k for k in range(n) if k >= row_size]

    def spread(x):
        held = {}
        for k in far:
            low = k & (row_size - 1)
            held[k] = move(held[k ^ low], low) if low else move(x, k)
        return held

    def along(held):
        return {k: move(held[k & ~(row_size - 1)], k & (row_size - 1)) if k & (row_size - 1) else held[k] for k in far}

    ordered = lambda x, *first: lax.optimization_barrier((x,) + first)[0]
    heads = [k for k in far if not k & (row_size - 1)]
    height = cholesky.shape[1]
    rows = cholesky.reshape(vectors * height, cholesky.shape[2])
    direct_rows = height // 2
    shared_rows = (rows.shape[0] - direct_rows) // 2
    at = direct_rows + (lax.axis_index("walk") & 1) * shared_rows
    shared = lax.dynamic_slice_in_dim(rows, at, shared_rows, 0)
    sends = select(n, per, share, branches, walkers)
    own = message(ordered(trial_orbitals, sends[0]), field)
    messages = {0: own, **spread(own)}
    messages.update({k: move(own, k) for k in near[1:]})
    messages = [messages[k] for k in range(n)]
    crossed = {k: move(shared, k) for k in heads}
    close = [rows] + [move(rows, k) for k in near[1:]]
    early = [messages[far[0]], *close[1:]]
    blocks = [sends[0]] + [
        move(ordered(sends[k], *(crossed.values() if k == n - 1 else early)), k) for k in range(1, n)
    ]
    asked = ask(pick_fields(n, per, share, branches, messages))
    turned, masks = turn(n, per, share, branches, counts, messages)
    direct = {k: move(ordered(rows[:direct_rows], asked, turned), k) for k in heads}
    other = {k: swap(x) for k, x in crossed.items()}
    green = make_green(n, share, blocks, turned, asked)
    crossed, other, direct = (along({k: ordered(x, green) for k, x in held.items()}) for held in (crossed, other, direct))
    results = contract(functools.partial(near_kernel, share, len(near), height), len(near), close, green)
    late = contract(
        functools.partial(shared_kernel, share, len(far), height),
        len(far),
        [crossed[k] for k in far] + [other[k] for k in far],
        ordered(green, results[0]),
        kept_rows=direct_rows,
        scratch_rows=2 * shared_rows,
    )
    late = contract(
        functools.partial(direct_kernel, share, len(far)), len(far), [direct[k] for k in far], green,
        *late[len(far) :], *late[: len(far)],
    )
    arrived = [answer(x, k) for k, x in enumerate(list(results) + list(late))]
    return tuple(x.T for x in unpack(n, per, share, vectors, masks, arrived))


def newton_schulz(intersection):
    column_max = jnp.max(jnp.sum(jnp.abs(intersection), axis=0))
    row_max = jnp.max(jnp.sum(jnp.abs(intersection), axis=1))
    inverse = intersection.T / (column_max * row_max)
    twice_identity = 2.0 * jnp.eye(intersection.shape[0], dtype=intersection.dtype)
    for iteration in range(ITERS):
        inverse = jnp.dot(
            inverse,
            twice_identity - jnp.dot(intersection, inverse, precision=HIGHEST),
            precision=HIGHEST,
        )
    return inverse


def pick(array, indices):
    return jnp.concatenate(
        [lax.dynamic_slice_in_dim(array, indices[i], 1, 0) for i in range(indices.shape[0])], axis=0
    )


def at_the_target(walkers, trial_orbitals, cholesky, branches, counts, field):
    walk_size = lax.axis_size("walk")
    position = lax.axis_index("walk")
    per_device, row_count, electrons = walkers.shape
    capacity = (per_device + walk_size - 1) // walk_size
    sender = branches.reshape(walk_size, per_device) // per_device
    local_index = branches.reshape(walk_size, per_device) % per_device
    same_sender = sender[:, :, None] == sender[:, None, :]
    earlier = jnp.arange(per_device)[None, :] < jnp.arange(per_device)[:, None]
    arrival_rank = jnp.sum(same_sender & earlier[None], axis=2)
    wanted = (sender[:, None, :] == position) & (
        arrival_rank[:, None, :] == jnp.arange(capacity, dtype=jnp.int32)[None, :, None]
    )
    chosen = jnp.sum(jnp.where(wanted, local_index[:, None, :], 0), axis=2).reshape(-1)
    outgoing = pick(walkers, chosen).reshape(walk_size, capacity, row_count, electrons)
    arrived = lax.all_to_all(outgoing, "walk", split_axis=0, concat_axis=0, tiled=True)
    my_sender = lax.dynamic_index_in_dim(sender, position, 0, keepdims=False)
    my_rank = lax.dynamic_index_in_dim(arrival_rank, position, 0, keepdims=False)
    arrived_flat = arrived.reshape(walk_size * capacity, row_count, electrons)
    migrated = pick(arrived_flat, my_sender * capacity + my_rank)
    propagated = (migrated.astype(F32) * field[:, :, None]).astype(BF16)
    everything = lax.all_gather(propagated, SR, axis=1, tiled=True)
    shard_count = lax.axis_size(SR)
    share = per_device // shard_count
    trial_whole = lax.all_gather(trial_orbitals, SR, axis=0, tiled=True)
    own_walkers = lax.dynamic_slice_in_dim(everything, lax.axis_index(SR) * share, share, 0)
    intersection = jnp.einsum("mn,wmk->wnk", trial_whole, own_walkers, preferred_element_type=F32)
    inverse = jax.vmap(newton_schulz)(intersection).astype(BF16)
    inverses = lax.all_gather(inverse, SR, axis=0, tiled=True)
    green = jnp.einsum("wmn,wnk->wmk", everything, inverses, preferred_element_type=F32).astype(BF16)
    contracted = jnp.einsum("gnm,wmk->wgnk", cholesky, green, preferred_element_type=F32)
    living = (jnp.arange(per_device, dtype=jnp.int32) < counts[0]).astype(F32)[:, None]
    force_bias = jnp.trace(contracted, axis1=2, axis2=3) * living
    exchange_energy = -0.5 * jnp.einsum("wgnk,wgkn->wg", contracted, contracted) * living
    return (force_bias, exchange_energy)


def on_device(walkers, trial_orbitals, cholesky, branches, counts, field):
    walk_size, shard_count = lax.axis_size("walk"), lax.axis_size(SR)
    per = walkers.shape[0]
    if walk_size == shard_count and per % walk_size == 0 and not walk_size & (walk_size - 1):
        if cholesky.shape[0] * (per // walk_size) <= 4 and cholesky.shape[1] % 64 == 0 and per <= 128:
            return at_the_source(walkers, trial_orbitals, cholesky, branches, counts, field)
    return at_the_target(walkers, trial_orbitals, cholesky, branches, counts, field)


def solution(mesh):
    return jax.shard_map(
        on_device,
        mesh=mesh,
        in_specs=(
            P(("parts", "walk"), SR, None),
            P(("parts",) + SR, None),
            P(("parts",) + SR, None, None),
            P("parts"),
            P(("parts", "walk")),
            P(("parts", "walk"), SR),
        ),
        out_specs=(P(("parts", "walk"), SR), P(("parts", "walk"), SR)),
        check_vma=False,
    )
```

```python
import functools

import jax
import jax.numpy as jnp
from jax import lax
from jax.experimental import pallas as pl
from jax.experimental.pallas import tpu as pltpu
from jax.sharding import PartitionSpec as P

ITERS = 10
EARLY = 3
SR = ("slab", "row")
ALL = ("walk", "slab", "row")
F32 = jnp.float32
BF16 = jnp.bfloat16
VMEM_LIMIT = 24 * 2**20
SMALL_LIMIT = 2**20
HIGHEST = lax.Precision.HIGHEST


def dot(a, b, dims=((1,), (0,))):
    return lax.dot_general(a, b, (dims, ((), ())), preferred_element_type=F32)


def split(x):
    high = x.astype(BF16)
    return high, (x - high.astype(F32)).astype(BF16)


def place():
    return lax.axis_index("walk"), lax.axis_index("slab") * lax.axis_size("row") + lax.axis_index("row")


def whole(memory=pltpu.VMEM):
    return pl.BlockSpec(memory_space=memory)


def picks(branches, start, per, sender, share):
    places, olds = [jnp.int32(0)] * share, [jnp.int32(0)] * share
    rank = jnp.int32(0)
    for i in range(per):
        branch = branches[start + i]
        hit = lax.div(branch, per) == sender
        old = lax.rem(branch, per)
        for r in range(share):
            here = hit & (rank == r)
            places[r] = jnp.where(here, i, places[r])
            olds[r] = jnp.where(here, old, olds[r])
        rank = rank + hit.astype(jnp.int32)
    return places, olds


def select_kernel(n, per, share, branches, walkers, *refs):
    sends, sems = refs[:n], refs[n]
    walk, q = place()
    copies = []
    for k in list(range(1, n)) + [0]:
        olds = picks(branches, (q ^ k ^ walk) * per, per, walk, share)[1]
        for r in range(share):
            copies.append(pltpu.make_async_copy(walkers.at[olds[r]], sends[k].at[r], sems.at[k, r]))
            copies[-1].start()
    for copy in copies:
        copy.wait()


def select(n, per, share, branches, walkers):
    rows, electrons = walkers.shape[1:]
    return pl.pallas_call(
        functools.partial(select_kernel, n, per, share),
        out_shape=[jax.ShapeDtypeStruct((share, rows, electrons), walkers.dtype)] * n,
        in_specs=[whole(pltpu.SMEM), whole(pl.ANY)],
        out_specs=[whole(pl.ANY)] * n,
        scratch_shapes=[pltpu.SemaphoreType.DMA((n, share))],
        compiler_params=pltpu.CompilerParams(vmem_limit_bytes=SMALL_LIMIT),
        name="select",
    )(branches, walkers)


def message_kernel(trial, field, out):
    rows = trial.shape[0]
    out[:rows, :] = trial[...]
    rest, parts = field[...], []
    for _ in range(3):
        parts.append(rest.astype(BF16).astype(F32))
        rest = rest - parts[-1]
    spare = out.shape[0] - rows - 3 * field.shape[0]
    if spare:
        parts.append(jnp.zeros((spare, field.shape[1]), F32))
    out[rows:, :] = jnp.concatenate(parts, axis=0).astype(BF16)


def message(trial, field):
    height = trial.shape[0] + -(-3 * field.shape[0] // 16) * 16
    return pl.pallas_call(
        message_kernel,
        out_shape=jax.ShapeDtypeStruct((height, trial.shape[1]), trial.dtype),
        in_specs=[whole()] * 2,
        out_specs=whole(),
        compiler_params=pltpu.CompilerParams(vmem_limit_bytes=SMALL_LIMIT),
        name="message",
    )(trial, field)


def fields_kernel(n, per, share, branches, *refs):
    messages, fields = refs[:n], refs[n]
    walk, q = place()
    rows = fields.shape[2]
    places = picks(branches, walk * per, per, walk ^ q, share)[0]
    walker = lax.broadcasted_iota(jnp.int32, (per, rows), 0)
    for k in range(n):
        terms = messages[k][rows:, :].astype(F32)
        value = terms[:per] + terms[per : 2 * per] + terms[2 * per : 3 * per]
        chosen = [jnp.sum(jnp.where(walker == p, value, 0.0), axis=0, keepdims=True) for p in places]
        fields[pl.ds(q ^ k, 1), :, :] = jnp.concatenate(chosen, axis=0)[None]


def pick_fields(n, per, share, branches, messages):
    return pl.pallas_call(
        functools.partial(fields_kernel, n, per, share),
        out_shape=jax.ShapeDtypeStruct((n, share, messages[0].shape[1]), F32),
        in_specs=[whole(pltpu.SMEM)] + [whole()] * n,
        out_specs=whole(),
        compiler_params=pltpu.CompilerParams(vmem_limit_bytes=SMALL_LIMIT),
        name="fields",
    )(branches, *messages)


def turn_kernel(n, per, share, branches, counts, *refs):
    messages, turned, masks = refs[:n], refs[n], refs[n + 1]
    walk, q = place()
    rows = turned.shape[1] // n
    for k in range(n):
        turned[:, k * rows : (k + 1) * rows] = messages[k][:rows, :].T
    lane = lax.broadcasted_iota(jnp.int32, (1, 128), 1)
    for k in range(n):
        places = picks(branches, walk * per, per, walk ^ q ^ k, share)[0]
        for r in range(share):
            here = (lane == places[r]) & (places[r] < counts[0])
            masks[k * share + r : k * share + r + 1, :] = here.astype(F32)


def turn(n, per, share, branches, counts, messages):
    electrons = messages[0].shape[1]
    rows = n * (messages[0].shape[0] - -(-3 * per // 16) * 16)
    return pl.pallas_call(
        functools.partial(turn_kernel, n, per, share),
        out_shape=[
            jax.ShapeDtypeStruct((electrons, rows), messages[0].dtype),
            jax.ShapeDtypeStruct((n * share, 128), F32),
        ],
        in_specs=[whole(pltpu.SMEM)] * 2 + [whole()] * n,
        out_specs=[whole()] * 2,
        compiler_params=pltpu.CompilerParams(vmem_limit_bytes=SMALL_LIMIT),
        name="turn",
    )(branches, counts, *messages)


def squared(high, low):
    mixed = dot(high, low)
    return dot(high, high) + (mixed + mixed.T)


def green_kernel(n, share, *refs):
    blocks, turned, fields = refs[:n], refs[n], refs[n + 1]
    green, moved, left, right = refs[n + 2 :]
    q = place()[1]
    rows, electrons = blocks[0].shape[1:]
    spare = jnp.zeros((-share % 8, rows), F32)
    for k in range(n):
        lines = fields[pl.ds(q ^ k, 1), :, :].reshape(share, rows)
        columns = (jnp.concatenate([lines, spare], axis=0) if share % 8 else lines).T
        for i in range(share):
            moved[k * rows : (k + 1) * rows, i * electrons : (i + 1) * electrons] = (
                blocks[k][i].astype(F32) * columns[:, i : i + 1]
            ).astype(BF16)
    overlaps = dot(turned[...], moved[...])
    for i in range(share):
        overlap = overlaps[:, i * electrons : (i + 1) * electrons]
        size = jnp.abs(overlap)
        scale = jnp.max(jnp.sum(size, axis=0)) * jnp.max(jnp.sum(size, axis=1))
        left[i] = overlap.T / scale
        high, low = split(overlap)
        mixed = dot(high, low, ((1,), (1,)))
        right[i] = (dot(high, high, ((1,), (1,))) + (mixed + mixed.T)) / scale

    def advance(exact, step, carry):
        for i in range(share):
            now, matrix = left[i], right[i]
            high, low = split(matrix)
            left_high, left_low = split(now)
            product = dot(left_high, high)
            if exact:
                product = product + (dot(left_high, low) + dot(left_low, high))
            left[i] = 2.0 * now - product
            right[i] = 2.0 * matrix - squared(high, low)
        return carry

    lax.fori_loop(0, EARLY, functools.partial(advance, False), 0)
    lax.fori_loop(EARLY, ITERS - 1, functools.partial(advance, True), 0)
    for i in range(share):
        high, low = split(right[i])
        left_high, left_low = split(left[i])
        product = dot(left_high, high) + (dot(left_high, low) + dot(left_low, high))
        inverse = (2.0 * left[i] - product).astype(BF16)
        for k in range(n):
            at = pl.multiple_of((q ^ k) * rows, rows)
            green[pl.ds(at, rows), i * electrons : (i + 1) * electrons] = dot(
                moved[k * rows : (k + 1) * rows, i * electrons : (i + 1) * electrons], inverse
            ).astype(BF16)


def make_green(n, share, blocks, turned, fields):
    rows, electrons = blocks[0].shape[1:]
    return pl.pallas_call(
        functools.partial(green_kernel, n, share),
        out_shape=jax.ShapeDtypeStruct((n * rows, share * electrons), BF16),
        in_specs=[whole()] * (n + 2),
        out_specs=whole(),
        scratch_shapes=[
            pltpu.VMEM((n * rows, share * electrons), BF16),
            pltpu.VMEM((share, electrons, electrons), F32),
            pltpu.VMEM((share, electrons, electrons), F32),
        ],
        compiler_params=pltpu.CompilerParams(vmem_limit_bytes=VMEM_LIMIT),
        name="green",
    )(*blocks, turned, fields)


def report(share, held, index, upper, lower):
    half = upper.shape[0]
    row = lax.broadcasted_iota(jnp.int32, (half, half), 0)
    column = lax.broadcasted_iota(jnp.int32, (half, half), 1)
    out_row = lax.broadcasted_iota(jnp.int32, held.shape, 0)
    for i in range(share):
        left, middle, right = 2 * i * half, (2 * i + 1) * half, 2 * (i + 1) * half
        a, b = upper[:, left:middle], upper[:, middle:right]
        c, d = lower[:, left:middle], lower[:, middle:right]
        trace = jnp.sum(jnp.where(row == column, a + d, 0.0))
        exchange = -0.5 * jnp.sum(a * a.T + d * d.T + 2.0 * (b * c.T))
        held = jnp.where(out_row == index * share + i, trace, held)
        held = jnp.where(out_row == held.shape[0] // 2 + index * share + i, exchange, held)
    return held


def near_kernel(share, count, height, *refs):
    vectors, green, outs = refs[:count], refs[count], refs[-count:]
    for v in range(count):
        held = jnp.zeros(outs[v].shape, F32)
        for g in range(vectors[v].shape[0] // height):
            full = dot(vectors[v][g * height : (g + 1) * height, :], green[...])
            held = report(share, held, g, full[: height // 2], full[height // 2 :])
        outs[v][...] = held


def shared_kernel(share, count, height, *refs):
    firsts, seconds, green = refs[:count], refs[count : 2 * count], refs[2 * count]
    outs, kept, both = refs[-2 * count - 1 : -count - 1], refs[-count - 1 : -1], refs[-1]
    parity = lax.axis_index("walk") & 1
    half = height // 2
    for v in range(count):
        rows = firsts[v].shape[0]
        for at, piece in ((parity, firsts[v]), (1 - parity, seconds[v])):
            both[pl.ds(pl.multiple_of(at * rows, 16), rows), :] = dot(piece[...], green[...])
        kept[v][...] = both[:half, :]
        held = jnp.zeros(outs[v].shape, F32)
        for g in range(1, (2 * rows + half) // height):
            start = g * height - half
            held = report(share, held, g, both[start : start + half, :], both[start + half : start + height, :])
        outs[v][...] = held


def direct_kernel(share, count, *refs):
    uppers, green, kept, before = refs[:count], refs[count], refs[count + 1 : 2 * count + 1], refs[2 * count + 1 : -count]
    outs = refs[-count:]
    for v in range(count):
        outs[v][...] = report(share, before[v][...], 0, dot(uppers[v][...], green[...]), kept[v][...])


def contract(kernel, count, vectors, green, *more, kept_rows=0, scratch_rows=0):
    wide = green.shape[1]
    kept = [jax.ShapeDtypeStruct((kept_rows, wide), F32)] * count if kept_rows else []
    return pl.pallas_call(
        kernel,
        out_shape=[jax.ShapeDtypeStruct((8, 128), F32)] * count + kept,
        in_specs=[whole()] * (len(vectors) + 1 + len(more)),
        out_specs=[whole()] * (count + len(kept)),
        scratch_shapes=[pltpu.VMEM((scratch_rows, wide), F32)] if scratch_rows else [],
        compiler_params=pltpu.CompilerParams(vmem_limit_bytes=VMEM_LIMIT),
        cost_estimate=pl.CostEstimate(
            flops=sum(2 * v.size * wide for v in vectors),
            bytes_accessed=sum(2 * v.size for v in vectors) + 2 * green.size,
            transcendentals=0,
        ),
        name="contract",
    )(*vectors, green, *more)


def unpack_kernel(n, share, masks, *refs):
    arrived, outs = refs[:n], refs[n:]
    vectors, per = outs[0].shape
    for which, out in enumerate(outs):
        for g in range(vectors):
            line = jnp.zeros((1, 128), F32)
            for k in range(n):
                for r in range(share):
                    at = which * (arrived[k].shape[0] // 2) + g * share + r
                    line = jnp.where(masks[k * share + r : k * share + r + 1, :] > 0.0, arrived[k][at : at + 1, :], line)
            out[g : g + 1, :] = line[:, :per]


def unpack(n, per, share, vectors, masks, arrived):
    return pl.pallas_call(
        functools.partial(unpack_kernel, n, share),
        out_shape=[jax.ShapeDtypeStruct((vectors, per), F32)] * 2,
        in_specs=[whole()] * (1 + n),
        out_specs=[whole()] * 2,
        compiler_params=pltpu.CompilerParams(vmem_limit_bytes=SMALL_LIMIT),
        name="unpack",
    )(masks, *arrived)


def at_the_source(walkers, trial_orbitals, cholesky, branches, counts, field):
    n = lax.axis_size("walk")
    per = walkers.shape[0]
    share = per // n
    row_size = lax.axis_size("row")
    vectors = cholesky.shape[0]
    pairs = [(w, q) for w in range(n) for q in range(n)]
    move = lambda x, k: lax.ppermute(x, SR, [(i, i ^ k) for i in range(n)])
    swap = lambda x: lax.ppermute(x, "walk", [(w, w ^ 1) for w in range(n)])
    ask = lambda x: lax.ppermute(x, ALL, [(w * n + q, (w ^ q) * n + q) for w, q in pairs])
    answer = lambda x, k: lax.ppermute(x, ALL, [(w * n + q, (w ^ q) * n + (q ^ k)) for w, q in pairs])
    near = [k for k in range(n) if k < row_size]
    far = [k for k in range(n) if k >= row_size]

    def spread(x):
        held = {}
        for k in far:
            low = k & (row_size - 1)
            held[k] = move(held[k ^ low], low) if low else move(x, k)
        return held

    def along(held):
        return {k: move(held[k & ~(row_size - 1)], k & (row_size - 1)) if k & (row_size - 1) else held[k] for k in far}

    ordered = lambda x, *first: lax.optimization_barrier((x,) + first)[0]
    heads = [k for k in far if not k & (row_size - 1)]
    height = cholesky.shape[1]
    rows = cholesky.reshape(vectors * height, cholesky.shape[2])
    direct_rows = height // 2
    shared_rows = (rows.shape[0] - direct_rows) // 2
    at = direct_rows + (lax.axis_index("walk") & 1) * shared_rows
    shared = lax.dynamic_slice_in_dim(rows, at, shared_rows, 0)
    sends = select(n, per, share, branches, walkers)
    own = message(ordered(trial_orbitals, sends[0]), field)
    messages = {0: own, **spread(own)}
    messages.update({k: move(own, k) for k in near[1:]})
    messages = [messages[k] for k in range(n)]
    crossed = {k: move(shared, k) for k in heads}
    close = [rows] + [move(rows, k) for k in near[1:]]
    early = [messages[far[0]], *close[1:]]
    blocks = [sends[0]] + [
        move(ordered(sends[k], *(crossed.values() if k == n - 1 else early)), k) for k in range(1, n)
    ]
    asked = ask(pick_fields(n, per, share, branches, messages))
    turned, masks = turn(n, per, share, branches, counts, messages)
    direct = {k: move(ordered(rows[:direct_rows], asked, turned), k) for k in heads}
    other = {k: swap(x) for k, x in crossed.items()}
    green = make_green(n, share, blocks, turned, asked)
    crossed, other, direct = (along({k: ordered(x, green) for k, x in held.items()}) for held in (crossed, other, direct))
    results = contract(functools.partial(near_kernel, share, len(near), height), len(near), close, green)
    late = contract(
        functools.partial(shared_kernel, share, len(far), height),
        len(far),
        [crossed[k] for k in far] + [other[k] for k in far],
        ordered(green, results[0]),
        kept_rows=direct_rows,
        scratch_rows=2 * shared_rows,
    )
    late = contract(
        functools.partial(direct_kernel, share, len(far)), len(far), [direct[k] for k in far], green,
        *late[len(far) :], *late[: len(far)],
    )
    arrived = [answer(x if k in far else ordered(x, late[0]), k) for k, x in enumerate(list(results) + list(late))]
    return tuple(x.T for x in unpack(n, per, share, vectors, masks, arrived))


def newton_schulz(intersection):
    column_max = jnp.max(jnp.sum(jnp.abs(intersection), axis=0))
    row_max = jnp.max(jnp.sum(jnp.abs(intersection), axis=1))
    inverse = intersection.T / (column_max * row_max)
    twice_identity = 2.0 * jnp.eye(intersection.shape[0], dtype=intersection.dtype)
    for iteration in range(ITERS):
        inverse = jnp.dot(
            inverse,
            twice_identity - jnp.dot(intersection, inverse, precision=HIGHEST),
            precision=HIGHEST,
        )
    return inverse


def pick(array, indices):
    return jnp.concatenate(
        [lax.dynamic_slice_in_dim(array, indices[i], 1, 0) for i in range(indices.shape[0])], axis=0
    )


def at_the_target(walkers, trial_orbitals, cholesky, branches, counts, field):
    walk_size = lax.axis_size("walk")
    position = lax.axis_index("walk")
    per_device, row_count, electrons = walkers.shape
    capacity = (per_device + walk_size - 1) // walk_size
    sender = branches.reshape(walk_size, per_device) // per_device
    local_index = branches.reshape(walk_size, per_device) % per_device
    same_sender = sender[:, :, None] == sender[:, None, :]
    earlier = jnp.arange(per_device)[None, :] < jnp.arange(per_device)[:, None]
    arrival_rank = jnp.sum(same_sender & earlier[None], axis=2)
    wanted = (sender[:, None, :] == position) & (
        arrival_rank[:, None, :] == jnp.arange(capacity, dtype=jnp.int32)[None, :, None]
    )
    chosen = jnp.sum(jnp.where(wanted, local_index[:, None, :], 0), axis=2).reshape(-1)
    outgoing = pick(walkers, chosen).reshape(walk_size, capacity, row_count, electrons)
    arrived = lax.all_to_all(outgoing, "walk", split_axis=0, concat_axis=0, tiled=True)
    my_sender = lax.dynamic_index_in_dim(sender, position, 0, keepdims=False)
    my_rank = lax.dynamic_index_in_dim(arrival_rank, position, 0, keepdims=False)
    arrived_flat = arrived.reshape(walk_size * capacity, row_count, electrons)
    migrated = pick(arrived_flat, my_sender * capacity + my_rank)
    propagated = (migrated.astype(F32) * field[:, :, None]).astype(BF16)
    everything = lax.all_gather(propagated, SR, axis=1, tiled=True)
    shard_count = lax.axis_size(SR)
    share = per_device // shard_count
    trial_whole = lax.all_gather(trial_orbitals, SR, axis=0, tiled=True)
    own_walkers = lax.dynamic_slice_in_dim(everything, lax.axis_index(SR) * share, share, 0)
    intersection = jnp.einsum("mn,wmk->wnk", trial_whole, own_walkers, preferred_element_type=F32)
    inverse = jax.vmap(newton_schulz)(intersection).astype(BF16)
    inverses = lax.all_gather(inverse, SR, axis=0, tiled=True)
    green = jnp.einsum("wmn,wnk->wmk", everything, inverses, preferred_element_type=F32).astype(BF16)
    contracted = jnp.einsum("gnm,wmk->wgnk", cholesky, green, preferred_element_type=F32)
    living = (jnp.arange(per_device, dtype=jnp.int32) < counts[0]).astype(F32)[:, None]
    force_bias = jnp.trace(contracted, axis1=2, axis2=3) * living
    exchange_energy = -0.5 * jnp.einsum("wgnk,wgkn->wg", contracted, contracted) * living
    return (force_bias, exchange_energy)


def on_device(walkers, trial_orbitals, cholesky, branches, counts, field):
    walk_size, shard_count = lax.axis_size("walk"), lax.axis_size(SR)
    per = walkers.shape[0]
    if walk_size == shard_count and per % walk_size == 0 and not walk_size & (walk_size - 1):
        if cholesky.shape[0] * (per // walk_size) <= 4 and cholesky.shape[1] % 64 == 0 and per <= 128:
            return at_the_source(walkers, trial_orbitals, cholesky, branches, counts, field)
    return at_the_target(walkers, trial_orbitals, cholesky, branches, counts, field)


def solution(mesh):
    return jax.shard_map(
        on_device,
        mesh=mesh,
        in_specs=(
            P(("parts", "walk"), SR, None),
            P(("parts",) + SR, None),
            P(("parts",) + SR, None, None),
            P("parts"),
            P(("parts", "walk")),
            P(("parts", "walk"), SR),
        ),
        out_specs=(P(("parts", "walk"), SR), P(("parts", "walk"), SR)),
        check_vma=False,
    )
```

```python
import functools

import jax
import jax.numpy as jnp
from jax import lax
from jax.experimental import pallas as pl
from jax.experimental.pallas import tpu as pltpu
from jax.sharding import PartitionSpec as P

ITERS = 10
EARLY = 3
SR = ("slab", "row")
ALL = ("walk", "slab", "row")
F32 = jnp.float32
BF16 = jnp.bfloat16
VMEM_LIMIT = 24 * 2**20
SMALL_LIMIT = 2**20
HIGHEST = lax.Precision.HIGHEST


def dot(a, b, dims=((1,), (0,))):
    return lax.dot_general(a, b, (dims, ((), ())), preferred_element_type=F32)


def split(x):
    high = x.astype(BF16)
    return high, (x - high.astype(F32)).astype(BF16)


def place():
    return lax.axis_index("walk"), lax.axis_index("slab") * lax.axis_size("row") + lax.axis_index("row")


def whole(memory=pltpu.VMEM):
    return pl.BlockSpec(memory_space=memory)


def picks(branches, start, per, sender, share):
    places, olds = [jnp.int32(0)] * share, [jnp.int32(0)] * share
    rank = jnp.int32(0)
    for i in range(per):
        branch = branches[start + i]
        hit = lax.div(branch, per) == sender
        old = lax.rem(branch, per)
        for r in range(share):
            here = hit & (rank == r)
            places[r] = jnp.where(here, i, places[r])
            olds[r] = jnp.where(here, old, olds[r])
        rank = rank + hit.astype(jnp.int32)
    return places, olds


def select_kernel(n, per, share, branches, walkers, *refs):
    sends, sems = refs[:n], refs[n]
    walk, q = place()
    copies = []
    for k in list(range(1, n)) + [0]:
        olds = picks(branches, (q ^ k ^ walk) * per, per, walk, share)[1]
        for r in range(share):
            copies.append(pltpu.make_async_copy(walkers.at[olds[r]], sends[k].at[r], sems.at[k, r]))
            copies[-1].start()
    for copy in copies:
        copy.wait()


def select(n, per, share, branches, walkers):
    rows, electrons = walkers.shape[1:]
    return pl.pallas_call(
        functools.partial(select_kernel, n, per, share),
        out_shape=[jax.ShapeDtypeStruct((share, rows, electrons), walkers.dtype)] * n,
        in_specs=[whole(pltpu.SMEM), whole(pl.ANY)],
        out_specs=[whole(pl.ANY)] * n,
        scratch_shapes=[pltpu.SemaphoreType.DMA((n, share))],
        compiler_params=pltpu.CompilerParams(vmem_limit_bytes=SMALL_LIMIT),
        name="select",
    )(branches, walkers)


def message_kernel(trial, field, out):
    rows = trial.shape[0]
    out[:rows, :] = trial[...]
    rest, parts = field[...], []
    for _ in range(3):
        parts.append(rest.astype(BF16).astype(F32))
        rest = rest - parts[-1]
    spare = out.shape[0] - rows - 3 * field.shape[0]
    if spare:
        parts.append(jnp.zeros((spare, field.shape[1]), F32))
    out[rows:, :] = jnp.concatenate(parts, axis=0).astype(BF16)


def message(trial, field):
    height = trial.shape[0] + -(-3 * field.shape[0] // 16) * 16
    return pl.pallas_call(
        message_kernel,
        out_shape=jax.ShapeDtypeStruct((height, trial.shape[1]), trial.dtype),
        in_specs=[whole()] * 2,
        out_specs=whole(),
        compiler_params=pltpu.CompilerParams(vmem_limit_bytes=SMALL_LIMIT),
        name="message",
    )(trial, field)


def fields_kernel(n, per, share, branches, *refs):
    messages, fields = refs[:n], refs[n]
    walk, q = place()
    rows = fields.shape[2]
    places = picks(branches, walk * per, per, walk ^ q, share)[0]
    walker = lax.broadcasted_iota(jnp.int32, (per, rows), 0)
    for k in range(n):
        terms = messages[k][rows:, :].astype(F32)
        value = terms[:per] + terms[per : 2 * per] + terms[2 * per : 3 * per]
        chosen = [jnp.sum(jnp.where(walker == p, value, 0.0), axis=0, keepdims=True) for p in places]
        fields[pl.ds(q ^ k, 1), :, :] = jnp.concatenate(chosen, axis=0)[None]


def pick_fields(n, per, share, branches, messages):
    return pl.pallas_call(
        functools.partial(fields_kernel, n, per, share),
        out_shape=jax.ShapeDtypeStruct((n, share, messages[0].shape[1]), F32),
        in_specs=[whole(pltpu.SMEM)] + [whole()] * n,
        out_specs=whole(),
        compiler_params=pltpu.CompilerParams(vmem_limit_bytes=SMALL_LIMIT),
        name="fields",
    )(branches, *messages)


def turn_kernel(n, per, share, branches, counts, *refs):
    messages, turned, masks = refs[:n], refs[n], refs[n + 1]
    walk, q = place()
    rows = turned.shape[1] // n
    for k in range(n):
        turned[:, k * rows : (k + 1) * rows] = messages[k][:rows, :].T
    lane = lax.broadcasted_iota(jnp.int32, (1, 128), 1)
    for k in range(n):
        places = picks(branches, walk * per, per, walk ^ q ^ k, share)[0]
        for r in range(share):
            here = (lane == places[r]) & (places[r] < counts[0])
            masks[k * share + r : k * share + r + 1, :] = here.astype(F32)


def turn(n, per, share, branches, counts, messages):
    electrons = messages[0].shape[1]
    rows = n * (messages[0].shape[0] - -(-3 * per // 16) * 16)
    return pl.pallas_call(
        functools.partial(turn_kernel, n, per, share),
        out_shape=[
            jax.ShapeDtypeStruct((electrons, rows), messages[0].dtype),
            jax.ShapeDtypeStruct((n * share, 128), F32),
        ],
        in_specs=[whole(pltpu.SMEM)] * 2 + [whole()] * n,
        out_specs=[whole()] * 2,
        compiler_params=pltpu.CompilerParams(vmem_limit_bytes=SMALL_LIMIT),
        name="turn",
    )(branches, counts, *messages)


def squared(high, low):
    mixed = dot(high, low)
    return dot(high, high) + (mixed + mixed.T)


def green_kernel(n, share, *refs):
    blocks, turned, fields = refs[:n], refs[n], refs[n + 1]
    green, moved, left, right = refs[n + 2 :]
    q = place()[1]
    rows, electrons = blocks[0].shape[1:]
    spare = jnp.zeros((-share % 8, rows), F32)
    for k in range(n):
        lines = fields[pl.ds(q ^ k, 1), :, :].reshape(share, rows)
        columns = (jnp.concatenate([lines, spare], axis=0) if share % 8 else lines).T
        for i in range(share):
            moved[k * rows : (k + 1) * rows, i * electrons : (i + 1) * electrons] = (
                blocks[k][i].astype(F32) * columns[:, i : i + 1]
            ).astype(BF16)
    overlaps = dot(turned[...], moved[...])
    for i in range(share):
        overlap = overlaps[:, i * electrons : (i + 1) * electrons]
        size = jnp.abs(overlap)
        scale = jnp.max(jnp.sum(size, axis=0)) * jnp.max(jnp.sum(size, axis=1))
        left[i] = overlap.T / scale
        high, low = split(overlap)
        mixed = dot(high, low, ((1,), (1,)))
        right[i] = (dot(high, high, ((1,), (1,))) + (mixed + mixed.T)) / scale

    def advance(exact, step, carry):
        for i in range(share):
            now, matrix = left[i], right[i]
            high, low = split(matrix)
            left_high, left_low = split(now)
            product = dot(left_high, high)
            if exact:
                product = product + (dot(left_high, low) + dot(left_low, high))
            left[i] = 2.0 * now - product
            right[i] = 2.0 * matrix - squared(high, low)
        return carry

    lax.fori_loop(0, EARLY, functools.partial(advance, False), 0)
    lax.fori_loop(EARLY, ITERS - 1, functools.partial(advance, True), 0)
    for i in range(share):
        high, low = split(right[i])
        left_high, left_low = split(left[i])
        product = dot(left_high, high) + (dot(left_high, low) + dot(left_low, high))
        inverse = (2.0 * left[i] - product).astype(BF16)
        for k in range(n):
            at = pl.multiple_of((q ^ k) * rows, rows)
            green[pl.ds(at, rows), i * electrons : (i + 1) * electrons] = dot(
                moved[k * rows : (k + 1) * rows, i * electrons : (i + 1) * electrons], inverse
            ).astype(BF16)


def make_green(n, share, blocks, turned, fields):
    rows, electrons = blocks[0].shape[1:]
    return pl.pallas_call(
        functools.partial(green_kernel, n, share),
        out_shape=jax.ShapeDtypeStruct((n * rows, share * electrons), BF16),
        in_specs=[whole()] * (n + 2),
        out_specs=whole(),
        scratch_shapes=[
            pltpu.VMEM((n * rows, share * electrons), BF16),
            pltpu.VMEM((share, electrons, electrons), F32),
            pltpu.VMEM((share, electrons, electrons), F32),
        ],
        compiler_params=pltpu.CompilerParams(vmem_limit_bytes=VMEM_LIMIT),
        name="green",
    )(*blocks, turned, fields)


def report(share, held, index, upper, lower):
    half = upper.shape[0]
    row = lax.broadcasted_iota(jnp.int32, (half, half), 0)
    column = lax.broadcasted_iota(jnp.int32, (half, half), 1)
    out_row = lax.broadcasted_iota(jnp.int32, held.shape, 0)
    for i in range(share):
        left, middle, right = 2 * i * half, (2 * i + 1) * half, 2 * (i + 1) * half
        a, b = upper[:, left:middle], upper[:, middle:right]
        c, d = lower[:, left:middle], lower[:, middle:right]
        trace = jnp.sum(jnp.where(row == column, a + d, 0.0))
        exchange = -0.5 * jnp.sum(a * a.T + d * d.T + 2.0 * (b * c.T))
        held = jnp.where(out_row == index * share + i, trace, held)
        held = jnp.where(out_row == held.shape[0] // 2 + index * share + i, exchange, held)
    return held


def near_kernel(share, count, height, *refs):
    vectors, green, outs = refs[:count], refs[count], refs[-1]
    for v in range(count):
        held = jnp.zeros(outs.shape[1:], F32)
        for g in range(vectors[v].shape[0] // height):
            full = dot(vectors[v][g * height : (g + 1) * height, :], green[...])
            held = report(share, held, g, full[: height // 2], full[height // 2 :])
        outs[v] = held


def shared_kernel(share, count, height, *refs):
    firsts, seconds, green = refs[:count], refs[count : 2 * count], refs[2 * count]
    outs, kept, both = refs[-count - 2], refs[-count - 1 : -1], refs[-1]
    parity = lax.axis_index("walk") & 1
    half = height // 2
    for v in range(count):
        rows = firsts[v].shape[0]
        for at, piece in ((parity, firsts[v]), (1 - parity, seconds[v])):
            both[pl.ds(pl.multiple_of(at * rows, 16), rows), :] = dot(piece[...], green[...])
        kept[v][...] = both[:half, :]
        held = jnp.zeros(outs.shape[1:], F32)
        for g in range(1, (2 * rows + half) // height):
            start = g * height - half
            held = report(share, held, g, both[start : start + half, :], both[start + half : start + height, :])
        outs[v] = held


def direct_kernel(share, count, *refs):
    uppers, green, kept = refs[:count], refs[count], refs[count + 1 : 2 * count + 1]
    before, outs = refs[-2:]
    for v in range(count):
        outs[v] = report(share, before[v], 0, dot(uppers[v][...], green[...]), kept[v][...])


def contract(kernel, count, vectors, green, *more, kept_rows=0, scratch_rows=0):
    wide = green.shape[1]
    kept = [jax.ShapeDtypeStruct((kept_rows, wide), F32)] * count if kept_rows else []
    return pl.pallas_call(
        kernel,
        out_shape=[jax.ShapeDtypeStruct((count, 8, 128), F32)] + kept,
        in_specs=[whole()] * (len(vectors) + 1 + len(more)),
        out_specs=[whole()] * (1 + len(kept)),
        scratch_shapes=[pltpu.VMEM((scratch_rows, wide), F32)] if scratch_rows else [],
        compiler_params=pltpu.CompilerParams(vmem_limit_bytes=VMEM_LIMIT),
        cost_estimate=pl.CostEstimate(
            flops=sum(2 * v.size * wide for v in vectors),
            bytes_accessed=sum(2 * v.size for v in vectors) + 2 * green.size,
            transcendentals=0,
        ),
        name="contract",
    )(*vectors, green, *more)


def unpack_kernel(n, share, masks, *refs):
    arrived, outs = refs[:n], refs[n:]
    vectors, per = outs[0].shape
    for which, out in enumerate(outs):
        for g in range(vectors):
            line = jnp.zeros((1, 128), F32)
            for k in range(n):
                for r in range(share):
                    cores, height = arrived[k].shape[:2]
                    at = which * (height // 2) + g * share + r
                    value = arrived[k][k % cores, at : at + 1, :]
                    line = jnp.where(masks[k * share + r : k * share + r + 1, :] > 0.0, value, line)
            out[g : g + 1, :] = line[:, :per]


def unpack(n, per, share, vectors, masks, arrived):
    return pl.pallas_call(
        functools.partial(unpack_kernel, n, share),
        out_shape=[jax.ShapeDtypeStruct((vectors, per), F32)] * 2,
        in_specs=[whole()] * (1 + n),
        out_specs=[whole()] * 2,
        compiler_params=pltpu.CompilerParams(vmem_limit_bytes=SMALL_LIMIT),
        name="unpack",
    )(masks, *arrived)


def at_the_source(walkers, trial_orbitals, cholesky, branches, counts, field):
    n = lax.axis_size("walk")
    per = walkers.shape[0]
    share = per // n
    row_size = lax.axis_size("row")
    vectors = cholesky.shape[0]
    pairs = [(w, q) for w in range(n) for q in range(n)]
    move = lambda x, k: lax.ppermute(x, SR, [(i, i ^ k) for i in range(n)])
    swap = lambda x: lax.ppermute(x, "walk", [(w, w ^ 1) for w in range(n)])
    ask = lambda x: lax.ppermute(x, ALL, [(w * n + q, (w ^ q) * n + q) for w, q in pairs])
    answer = lambda x, k: lax.ppermute(x, ALL, [(w * n + q, (w ^ q) * n + (q ^ k)) for w, q in pairs])
    near = [k for k in range(n) if k < row_size]
    far = [k for k in range(n) if k >= row_size]

    def spread(x):
        held = {}
        for k in far:
            low = k & (row_size - 1)
            held[k] = move(held[k ^ low], low) if low else move(x, k)
        return held

    def along(held):
        return {k: move(held[k & ~(row_size - 1)], k & (row_size - 1)) if k & (row_size - 1) else held[k] for k in far}

    ordered = lambda x, *first: lax.optimization_barrier((x,) + first)[0]
    heads = [k for k in far if not k & (row_size - 1)]
    height = cholesky.shape[1]
    rows = cholesky.reshape(vectors * height, cholesky.shape[2])
    direct_rows = height // 2
    shared_rows = (rows.shape[0] - direct_rows) // 2
    at = direct_rows + (lax.axis_index("walk") & 1) * shared_rows
    shared = lax.dynamic_slice_in_dim(rows, at, shared_rows, 0)
    sends = select(n, per, share, branches, walkers)
    own = message(ordered(trial_orbitals, sends[0]), field)
    messages = {0: own, **spread(own)}
    messages.update({k: move(own, k) for k in near[1:]})
    messages = [messages[k] for k in range(n)]
    crossed = {k: move(shared, k) for k in heads}
    close = [rows] + [move(rows, k) for k in near[1:]]
    early = [messages[far[0]], *close[1:]]
    blocks = [sends[0]] + [
        move(ordered(sends[k], *(crossed.values() if k == n - 1 else early)), k) for k in range(1, n)
    ]
    asked = ask(pick_fields(n, per, share, branches, messages))
    turned, masks = turn(n, per, share, branches, counts, messages)
    direct = {k: move(ordered(rows[:direct_rows], asked, turned), k) for k in heads}
    other = {k: swap(x) for k, x in crossed.items()}
    green = make_green(n, share, blocks, turned, asked)
    crossed, other, direct = (along({k: ordered(x, green) for k, x in held.items()}) for held in (crossed, other, direct))
    [results] = contract(functools.partial(near_kernel, share, len(near), height), len(near), close, green)
    late, *kept = contract(
        functools.partial(shared_kernel, share, len(far), height),
        len(far),
        [crossed[k] for k in far] + [other[k] for k in far],
        ordered(green, results),
        kept_rows=direct_rows,
        scratch_rows=2 * shared_rows,
    )
    [late] = contract(
        functools.partial(direct_kernel, share, len(far)), len(far), [direct[k] for k in far], green, *kept, late
    )
    answers = [answer(late, far[0]), answer(ordered(results, late), 0)]
    arrived = [[x] + [move(x, k) for k in near[1:]] for x in reversed(answers)]
    return tuple(x.T for x in unpack(n, per, share, vectors, masks, [x for held in arrived for x in held]))


def newton_schulz(intersection):
    column_max = jnp.max(jnp.sum(jnp.abs(intersection), axis=0))
    row_max = jnp.max(jnp.sum(jnp.abs(intersection), axis=1))
    inverse = intersection.T / (column_max * row_max)
    twice_identity = 2.0 * jnp.eye(intersection.shape[0], dtype=intersection.dtype)
    for iteration in range(ITERS):
        inverse = jnp.dot(
            inverse,
            twice_identity - jnp.dot(intersection, inverse, precision=HIGHEST),
            precision=HIGHEST,
        )
    return inverse


def pick(array, indices):
    return jnp.concatenate(
        [lax.dynamic_slice_in_dim(array, indices[i], 1, 0) for i in range(indices.shape[0])], axis=0
    )


def at_the_target(walkers, trial_orbitals, cholesky, branches, counts, field):
    walk_size = lax.axis_size("walk")
    position = lax.axis_index("walk")
    per_device, row_count, electrons = walkers.shape
    capacity = (per_device + walk_size - 1) // walk_size
    sender = branches.reshape(walk_size, per_device) // per_device
    local_index = branches.reshape(walk_size, per_device) % per_device
    same_sender = sender[:, :, None] == sender[:, None, :]
    earlier = jnp.arange(per_device)[None, :] < jnp.arange(per_device)[:, None]
    arrival_rank = jnp.sum(same_sender & earlier[None], axis=2)
    wanted = (sender[:, None, :] == position) & (
        arrival_rank[:, None, :] == jnp.arange(capacity, dtype=jnp.int32)[None, :, None]
    )
    chosen = jnp.sum(jnp.where(wanted, local_index[:, None, :], 0), axis=2).reshape(-1)
    outgoing = pick(walkers, chosen).reshape(walk_size, capacity, row_count, electrons)
    arrived = lax.all_to_all(outgoing, "walk", split_axis=0, concat_axis=0, tiled=True)
    my_sender = lax.dynamic_index_in_dim(sender, position, 0, keepdims=False)
    my_rank = lax.dynamic_index_in_dim(arrival_rank, position, 0, keepdims=False)
    arrived_flat = arrived.reshape(walk_size * capacity, row_count, electrons)
    migrated = pick(arrived_flat, my_sender * capacity + my_rank)
    propagated = (migrated.astype(F32) * field[:, :, None]).astype(BF16)
    everything = lax.all_gather(propagated, SR, axis=1, tiled=True)
    shard_count = lax.axis_size(SR)
    share = per_device // shard_count
    trial_whole = lax.all_gather(trial_orbitals, SR, axis=0, tiled=True)
    own_walkers = lax.dynamic_slice_in_dim(everything, lax.axis_index(SR) * share, share, 0)
    intersection = jnp.einsum("mn,wmk->wnk", trial_whole, own_walkers, preferred_element_type=F32)
    inverse = jax.vmap(newton_schulz)(intersection).astype(BF16)
    inverses = lax.all_gather(inverse, SR, axis=0, tiled=True)
    green = jnp.einsum("wmn,wnk->wmk", everything, inverses, preferred_element_type=F32).astype(BF16)
    contracted = jnp.einsum("gnm,wmk->wgnk", cholesky, green, preferred_element_type=F32)
    living = (jnp.arange(per_device, dtype=jnp.int32) < counts[0]).astype(F32)[:, None]
    force_bias = jnp.trace(contracted, axis1=2, axis2=3) * living
    exchange_energy = -0.5 * jnp.einsum("wgnk,wgkn->wg", contracted, contracted) * living
    return (force_bias, exchange_energy)


def on_device(walkers, trial_orbitals, cholesky, branches, counts, field):
    walk_size, shard_count = lax.axis_size("walk"), lax.axis_size(SR)
    per = walkers.shape[0]
    if walk_size == shard_count and lax.axis_size("slab") == 2 and per % walk_size == 0 and not walk_size & (walk_size - 1):
        if cholesky.shape[0] * (per // walk_size) <= 4 and cholesky.shape[1] % 64 == 0 and per <= 128:
            return at_the_source(walkers, trial_orbitals, cholesky, branches, counts, field)
    return at_the_target(walkers, trial_orbitals, cholesky, branches, counts, field)


def solution(mesh):
    return jax.shard_map(
        on_device,
        mesh=mesh,
        in_specs=(
            P(("parts", "walk"), SR, None),
            P(("parts",) + SR, None),
            P(("parts",) + SR, None, None),
            P("parts"),
            P(("parts", "walk")),
            P(("parts", "walk"), SR),
        ),
        out_specs=(P(("parts", "walk"), SR), P(("parts", "walk"), SR)),
        check_vma=False,
    )
```

```python
import functools

import jax
import jax.numpy as jnp
from jax import lax
from jax.experimental import pallas as pl
from jax.experimental.pallas import tpu as pltpu
from jax.sharding import PartitionSpec as P

ITERS = 10
EARLY = 3
SR = ("slab", "row")
ALL = ("walk", "slab", "row")
F32 = jnp.float32
BF16 = jnp.bfloat16
VMEM_LIMIT = 24 * 2**20
SMALL_LIMIT = 2**20
AHEAD = pl.CostEstimate(flops=2**36, bytes_accessed=2**22, transcendentals=0)
HIGHEST = lax.Precision.HIGHEST


def dot(a, b, dims=((1,), (0,))):
    return lax.dot_general(a, b, (dims, ((), ())), preferred_element_type=F32)


def split(x):
    high = x.astype(BF16)
    return high, (x - high.astype(F32)).astype(BF16)


def place():
    return lax.axis_index("walk"), lax.axis_index("slab") * lax.axis_size("row") + lax.axis_index("row")


def whole(memory=pltpu.VMEM):
    return pl.BlockSpec(memory_space=memory)


def picks(branches, start, per, sender, share):
    places, olds = [jnp.int32(0)] * share, [jnp.int32(0)] * share
    rank = jnp.int32(0)
    for i in range(per):
        branch = branches[start + i]
        hit = lax.div(branch, per) == sender
        old = lax.rem(branch, per)
        for r in range(share):
            here = hit & (rank == r)
            places[r] = jnp.where(here, i, places[r])
            olds[r] = jnp.where(here, old, olds[r])
        rank = rank + hit.astype(jnp.int32)
    return places, olds


def select_kernel(n, per, share, branches, walkers, *refs):
    sends, sems = refs[:n], refs[n]
    walk, q = place()
    copies = []
    for k in list(range(1, n)) + [0]:
        olds = picks(branches, (q ^ k ^ walk) * per, per, walk, share)[1]
        for r in range(share):
            copies.append(pltpu.make_async_copy(walkers.at[olds[r]], sends[k].at[r], sems.at[k, r]))
            copies[-1].start()
    for copy in copies:
        copy.wait()


def select(n, per, share, branches, walkers):
    rows, electrons = walkers.shape[1:]
    return pl.pallas_call(
        functools.partial(select_kernel, n, per, share),
        out_shape=[jax.ShapeDtypeStruct((share, rows, electrons), walkers.dtype)] * n,
        in_specs=[whole(pltpu.SMEM), whole(pl.ANY)],
        out_specs=[whole(pl.ANY)] * n,
        scratch_shapes=[pltpu.SemaphoreType.DMA((n, share))],
        compiler_params=pltpu.CompilerParams(vmem_limit_bytes=SMALL_LIMIT),
        name="select",
    )(branches, walkers)


def message_kernel(trial, field, out):
    rows = trial.shape[0]
    out[:rows, :] = trial[...]
    rest, parts = field[...], []
    for _ in range(3):
        parts.append(rest.astype(BF16).astype(F32))
        rest = rest - parts[-1]
    spare = out.shape[0] - rows - 3 * field.shape[0]
    if spare:
        parts.append(jnp.zeros((spare, field.shape[1]), F32))
    out[rows:, :] = jnp.concatenate(parts, axis=0).astype(BF16)


def message(trial, field):
    height = trial.shape[0] + -(-3 * field.shape[0] // 16) * 16
    return pl.pallas_call(
        message_kernel,
        out_shape=jax.ShapeDtypeStruct((height, trial.shape[1]), trial.dtype),
        in_specs=[whole()] * 2,
        out_specs=whole(),
        compiler_params=pltpu.CompilerParams(vmem_limit_bytes=SMALL_LIMIT),
        name="message",
    )(trial, field)


def fields_kernel(n, per, share, branches, *refs):
    messages, fields = refs[:n], refs[n]
    walk, q = place()
    rows = fields.shape[2]
    places = picks(branches, walk * per, per, walk ^ q, share)[0]
    walker = lax.broadcasted_iota(jnp.int32, (per, rows), 0)
    for k in range(n):
        terms = messages[k][rows:, :].astype(F32)
        value = terms[:per] + terms[per : 2 * per] + terms[2 * per : 3 * per]
        chosen = [jnp.sum(jnp.where(walker == p, value, 0.0), axis=0, keepdims=True) for p in places]
        fields[pl.ds(q ^ k, 1), :, :] = jnp.concatenate(chosen, axis=0)[None]


def pick_fields(n, per, share, branches, messages):
    return pl.pallas_call(
        functools.partial(fields_kernel, n, per, share),
        out_shape=jax.ShapeDtypeStruct((n, share, messages[0].shape[1]), F32),
        in_specs=[whole(pltpu.SMEM)] + [whole()] * n,
        out_specs=whole(),
        compiler_params=pltpu.CompilerParams(vmem_limit_bytes=SMALL_LIMIT),
        name="fields",
    )(branches, *messages)


def turn_kernel(n, per, share, branches, counts, *refs):
    messages, turned, masks = refs[:n], refs[n], refs[n + 1]
    walk, q = place()
    rows = turned.shape[1] // n
    for k in range(n):
        turned[:, k * rows : (k + 1) * rows] = messages[k][:rows, :].T
    lane = lax.broadcasted_iota(jnp.int32, (1, 128), 1)
    for k in range(n):
        places = picks(branches, walk * per, per, walk ^ q ^ k, share)[0]
        for r in range(share):
            here = (lane == places[r]) & (places[r] < counts[0])
            masks[k * share + r : k * share + r + 1, :] = here.astype(F32)


def turn(n, per, share, branches, counts, messages):
    electrons = messages[0].shape[1]
    rows = n * (messages[0].shape[0] - -(-3 * per // 16) * 16)
    return pl.pallas_call(
        functools.partial(turn_kernel, n, per, share),
        out_shape=[
            jax.ShapeDtypeStruct((electrons, rows), messages[0].dtype),
            jax.ShapeDtypeStruct((n * share, 128), F32),
        ],
        in_specs=[whole(pltpu.SMEM)] * 2 + [whole()] * n,
        out_specs=[whole()] * 2,
        compiler_params=pltpu.CompilerParams(vmem_limit_bytes=SMALL_LIMIT),
        name="turn",
    )(branches, counts, *messages)


def squared(high, low):
    mixed = dot(high, low)
    return dot(high, high) + (mixed + mixed.T)


def propagate(share, k, block, fields, moved, start):
    q = place()[1]
    rows, electrons = block.shape[1:]
    lines = fields[pl.ds(q ^ k, 1), :, :].reshape(share, rows)
    if share % 8:
        lines = jnp.concatenate([lines, jnp.zeros((-share % 8, rows), F32)], axis=0)
    columns = lines.T
    for i in range(share):
        moved[start : start + rows, i * electrons : (i + 1) * electrons] = (
            block[i].astype(F32) * columns[:, i : i + 1]
        ).astype(BF16)


def first_kernel(n, share, *refs):
    blocks, turned, fields, moved, overlaps = refs[: n - 1], *refs[n - 1 :]
    rows = blocks[0].shape[1]
    for k in range(n - 1):
        propagate(share, k, blocks[k], fields, moved, k * rows)
    overlaps[...] = dot(turned[:, : (n - 1) * rows], moved[...])


def first_blocks(n, share, blocks, turned, fields):
    rows, electrons = blocks[0].shape[1:]
    return pl.pallas_call(
        functools.partial(first_kernel, n, share),
        out_shape=[
            jax.ShapeDtypeStruct(((n - 1) * rows, share * electrons), BF16),
            jax.ShapeDtypeStruct((electrons, share * electrons), F32),
        ],
        in_specs=[whole()] * (n + 1),
        out_specs=[whole()] * 2,
        compiler_params=pltpu.CompilerParams(vmem_limit_bytes=VMEM_LIMIT),
        cost_estimate=AHEAD,
        name="first",
    )(*blocks, turned, fields)


def green_kernel(n, share, *refs):
    block, turned, fields, earlier, begun = refs[:5]
    green, moved, left, right = refs[5:]
    q = place()[1]
    rows, electrons = block.shape[1:]
    propagate(share, n - 1, block, fields, moved, 0)
    overlaps = begun[...] + dot(turned[:, (n - 1) * rows :], moved[...])
    for i in range(share):
        overlap = overlaps[:, i * electrons : (i + 1) * electrons]
        size = jnp.abs(overlap)
        scale = jnp.max(jnp.sum(size, axis=0)) * jnp.max(jnp.sum(size, axis=1))
        left[i] = overlap.T / scale
        high, low = split(overlap)
        mixed = dot(high, low, ((1,), (1,)))
        right[i] = (dot(high, high, ((1,), (1,))) + (mixed + mixed.T)) / scale

    def advance(exact, step, carry):
        for i in range(share):
            now, matrix = left[i], right[i]
            high, low = split(matrix)
            left_high, left_low = split(now)
            product = dot(left_high, high)
            if exact:
                product = product + (dot(left_high, low) + dot(left_low, high))
            left[i] = 2.0 * now - product
            right[i] = 2.0 * matrix - squared(high, low)
        return carry

    lax.fori_loop(0, EARLY, functools.partial(advance, False), 0)
    lax.fori_loop(EARLY, ITERS - 1, functools.partial(advance, True), 0)
    for i in range(share):
        high, low = split(right[i])
        left_high, left_low = split(left[i])
        product = dot(left_high, high) + (dot(left_high, low) + dot(left_low, high))
        inverse = (2.0 * left[i] - product).astype(BF16)
        for k in range(n):
            at = pl.multiple_of((q ^ k) * rows, rows)
            held, start = (moved, 0) if k == n - 1 else (earlier, k * rows)
            green[pl.ds(at, rows), i * electrons : (i + 1) * electrons] = dot(
                held[start : start + rows, i * electrons : (i + 1) * electrons], inverse
            ).astype(BF16)


def make_green(n, share, block, turned, fields, earlier, begun):
    rows, electrons = block.shape[1:]
    return pl.pallas_call(
        functools.partial(green_kernel, n, share),
        out_shape=jax.ShapeDtypeStruct((n * rows, share * electrons), BF16),
        in_specs=[whole()] * 5,
        out_specs=whole(),
        scratch_shapes=[
            pltpu.VMEM((rows, share * electrons), BF16),
            pltpu.VMEM((share, electrons, electrons), F32),
            pltpu.VMEM((share, electrons, electrons), F32),
        ],
        compiler_params=pltpu.CompilerParams(vmem_limit_bytes=VMEM_LIMIT),
        name="green",
    )(block, turned, fields, earlier, begun)


def report(share, held, index, upper, lower):
    half = upper.shape[0]
    row = lax.broadcasted_iota(jnp.int32, (half, half), 0)
    column = lax.broadcasted_iota(jnp.int32, (half, half), 1)
    out_row = lax.broadcasted_iota(jnp.int32, held.shape, 0)
    for i in range(share):
        left, middle, right = 2 * i * half, (2 * i + 1) * half, 2 * (i + 1) * half
        a, b = upper[:, left:middle], upper[:, middle:right]
        c, d = lower[:, left:middle], lower[:, middle:right]
        trace = jnp.sum(jnp.where(row == column, a + d, 0.0))
        exchange = -0.5 * jnp.sum(a * a.T + d * d.T + 2.0 * (b * c.T))
        held = jnp.where(out_row == index * share + i, trace, held)
        held = jnp.where(out_row == held.shape[0] // 2 + index * share + i, exchange, held)
    return held


def near_kernel(share, count, height, *refs):
    vectors, green, outs = refs[:count], refs[count], refs[-1]
    for v in range(count):
        held = jnp.zeros(outs.shape[1:], F32)
        for g in range(vectors[v].shape[0] // height):
            full = dot(vectors[v][g * height : (g + 1) * height, :], green[...])
            held = report(share, held, g, full[: height // 2], full[height // 2 :])
        outs[v] = held


def shared_kernel(share, count, height, *refs):
    firsts, seconds, green = refs[:count], refs[count : 2 * count], refs[2 * count]
    outs, kept, both = refs[-count - 2], refs[-count - 1 : -1], refs[-1]
    parity = lax.axis_index("walk") & 1
    half = height // 2
    for v in range(count):
        rows = firsts[v].shape[0]
        for at, piece in ((parity, firsts[v]), (1 - parity, seconds[v])):
            both[pl.ds(pl.multiple_of(at * rows, 16), rows), :] = dot(piece[...], green[...])
        kept[v][...] = both[:half, :]
        held = jnp.zeros(outs.shape[1:], F32)
        for g in range(1, (2 * rows + half) // height):
            start = g * height - half
            held = report(share, held, g, both[start : start + half, :], both[start + half : start + height, :])
        outs[v] = held


def direct_kernel(share, count, *refs):
    uppers, green, kept = refs[:count], refs[count], refs[count + 1 : 2 * count + 1]
    before, outs = refs[-2:]
    for v in range(count):
        outs[v] = report(share, before[v], 0, dot(uppers[v][...], green[...]), kept[v][...])


def contract(kernel, count, vectors, green, *more, kept_rows=0, scratch_rows=0):
    wide = green.shape[1]
    kept = [jax.ShapeDtypeStruct((kept_rows, wide), F32)] * count if kept_rows else []
    return pl.pallas_call(
        kernel,
        out_shape=[jax.ShapeDtypeStruct((count, 8, 128), F32)] + kept,
        in_specs=[whole()] * (len(vectors) + 1 + len(more)),
        out_specs=[whole()] * (1 + len(kept)),
        scratch_shapes=[pltpu.VMEM((scratch_rows, wide), F32)] if scratch_rows else [],
        compiler_params=pltpu.CompilerParams(vmem_limit_bytes=VMEM_LIMIT),
        cost_estimate=pl.CostEstimate(
            flops=sum(2 * v.size * wide for v in vectors),
            bytes_accessed=sum(2 * v.size for v in vectors) + 2 * green.size,
            transcendentals=0,
        ),
        name="contract",
    )(*vectors, green, *more)


def unpack_kernel(n, share, masks, *refs):
    arrived, outs = refs[:n], refs[n:]
    vectors, per = outs[0].shape
    for which, out in enumerate(outs):
        for g in range(vectors):
            line = jnp.zeros((1, 128), F32)
            for k in range(n):
                for r in range(share):
                    cores, height = arrived[k].shape[:2]
                    at = which * (height // 2) + g * share + r
                    value = arrived[k][k % cores, at : at + 1, :]
                    line = jnp.where(masks[k * share + r : k * share + r + 1, :] > 0.0, value, line)
            out[g : g + 1, :] = line[:, :per]


def unpack(n, per, share, vectors, masks, arrived):
    return pl.pallas_call(
        functools.partial(unpack_kernel, n, share),
        out_shape=[jax.ShapeDtypeStruct((vectors, per), F32)] * 2,
        in_specs=[whole()] * (1 + n),
        out_specs=[whole()] * 2,
        compiler_params=pltpu.CompilerParams(vmem_limit_bytes=SMALL_LIMIT),
        name="unpack",
    )(masks, *arrived)


def at_the_source(walkers, trial_orbitals, cholesky, branches, counts, field):
    n = lax.axis_size("walk")
    per = walkers.shape[0]
    share = per // n
    row_size = lax.axis_size("row")
    vectors = cholesky.shape[0]
    pairs = [(w, q) for w in range(n) for q in range(n)]
    move = lambda x, k: lax.ppermute(x, SR, [(i, i ^ k) for i in range(n)])
    swap = lambda x: lax.ppermute(x, "walk", [(w, w ^ 1) for w in range(n)])
    ask = lambda x: lax.ppermute(x, ALL, [(w * n + q, (w ^ q) * n + q) for w, q in pairs])
    answer = lambda x, k: lax.ppermute(x, ALL, [(w * n + q, (w ^ q) * n + (q ^ k)) for w, q in pairs])
    near = [k for k in range(n) if k < row_size]
    far = [k for k in range(n) if k >= row_size]

    def spread(x):
        held = {}
        for k in far:
            low = k & (row_size - 1)
            held[k] = move(held[k ^ low], low) if low else move(x, k)
        return held

    def along(held):
        return {k: move(held[k & ~(row_size - 1)], k & (row_size - 1)) if k & (row_size - 1) else held[k] for k in far}

    ordered = lambda x, *first: lax.optimization_barrier((x,) + first)[0]
    heads = [k for k in far if not k & (row_size - 1)]
    height = cholesky.shape[1]
    rows = cholesky.reshape(vectors * height, cholesky.shape[2])
    direct_rows = height // 2
    shared_rows = (rows.shape[0] - direct_rows) // 2
    at = direct_rows + (lax.axis_index("walk") & 1) * shared_rows
    shared = lax.dynamic_slice_in_dim(rows, at, shared_rows, 0)
    sends = select(n, per, share, branches, walkers)
    own = message(ordered(trial_orbitals, sends[0]), field)
    messages = {0: own, **spread(own)}
    messages.update({k: move(own, k) for k in near[1:]})
    messages = [messages[k] for k in range(n)]
    crossed = {k: move(shared, k) for k in heads}
    close = [rows] + [move(rows, k) for k in near[1:]]
    early = close[1:]
    blocks = [sends[0]] + [
        move(ordered(sends[k], *(crossed.values() if k == n - 1 else early)), k) for k in range(1, n)
    ]
    asked = ask(pick_fields(n, per, share, branches, messages))
    turned, masks = turn(n, per, share, branches, counts, messages)
    other = {k: swap(x) for k, x in crossed.items()}
    earlier, begun = first_blocks(n, share, blocks[:-1], turned, asked)
    direct = {k: move(ordered(rows[:direct_rows], begun), k) for k in heads}
    green = make_green(n, share, blocks[n - 1], turned, asked, earlier, begun)
    crossed, other, direct = (along({k: ordered(x, green) for k, x in held.items()}) for held in (crossed, other, direct))
    [results] = contract(functools.partial(near_kernel, share, len(near), height), len(near), close, green)
    late, *kept = contract(
        functools.partial(shared_kernel, share, len(far), height),
        len(far),
        [crossed[k] for k in far] + [other[k] for k in far],
        ordered(green, results),
        kept_rows=direct_rows,
        scratch_rows=2 * shared_rows,
    )
    [late] = contract(
        functools.partial(direct_kernel, share, len(far)), len(far), [direct[k] for k in far], green, *kept, late
    )
    answers = [answer(late, far[0]), answer(ordered(results, late), 0)]
    arrived = [[x] + [move(x, k) for k in near[1:]] for x in reversed(answers)]
    return tuple(x.T for x in unpack(n, per, share, vectors, masks, [x for held in arrived for x in held]))


def newton_schulz(intersection):
    column_max = jnp.max(jnp.sum(jnp.abs(intersection), axis=0))
    row_max = jnp.max(jnp.sum(jnp.abs(intersection), axis=1))
    inverse = intersection.T / (column_max * row_max)
    twice_identity = 2.0 * jnp.eye(intersection.shape[0], dtype=intersection.dtype)
    for iteration in range(ITERS):
        inverse = jnp.dot(
            inverse,
            twice_identity - jnp.dot(intersection, inverse, precision=HIGHEST),
            precision=HIGHEST,
        )
    return inverse


def pick(array, indices):
    return jnp.concatenate(
        [lax.dynamic_slice_in_dim(array, indices[i], 1, 0) for i in range(indices.shape[0])], axis=0
    )


def at_the_target(walkers, trial_orbitals, cholesky, branches, counts, field):
    walk_size = lax.axis_size("walk")
    position = lax.axis_index("walk")
    per_device, row_count, electrons = walkers.shape
    capacity = (per_device + walk_size - 1) // walk_size
    sender = branches.reshape(walk_size, per_device) // per_device
    local_index = branches.reshape(walk_size, per_device) % per_device
    same_sender = sender[:, :, None] == sender[:, None, :]
    earlier = jnp.arange(per_device)[None, :] < jnp.arange(per_device)[:, None]
    arrival_rank = jnp.sum(same_sender & earlier[None], axis=2)
    wanted = (sender[:, None, :] == position) & (
        arrival_rank[:, None, :] == jnp.arange(capacity, dtype=jnp.int32)[None, :, None]
    )
    chosen = jnp.sum(jnp.where(wanted, local_index[:, None, :], 0), axis=2).reshape(-1)
    outgoing = pick(walkers, chosen).reshape(walk_size, capacity, row_count, electrons)
    arrived = lax.all_to_all(outgoing, "walk", split_axis=0, concat_axis=0, tiled=True)
    my_sender = lax.dynamic_index_in_dim(sender, position, 0, keepdims=False)
    my_rank = lax.dynamic_index_in_dim(arrival_rank, position, 0, keepdims=False)
    arrived_flat = arrived.reshape(walk_size * capacity, row_count, electrons)
    migrated = pick(arrived_flat, my_sender * capacity + my_rank)
    propagated = (migrated.astype(F32) * field[:, :, None]).astype(BF16)
    everything = lax.all_gather(propagated, SR, axis=1, tiled=True)
    shard_count = lax.axis_size(SR)
    share = per_device // shard_count
    trial_whole = lax.all_gather(trial_orbitals, SR, axis=0, tiled=True)
    own_walkers = lax.dynamic_slice_in_dim(everything, lax.axis_index(SR) * share, share, 0)
    intersection = jnp.einsum("mn,wmk->wnk", trial_whole, own_walkers, preferred_element_type=F32)
    inverse = jax.vmap(newton_schulz)(intersection).astype(BF16)
    inverses = lax.all_gather(inverse, SR, axis=0, tiled=True)
    green = jnp.einsum("wmn,wnk->wmk", everything, inverses, preferred_element_type=F32).astype(BF16)
    contracted = jnp.einsum("gnm,wmk->wgnk", cholesky, green, preferred_element_type=F32)
    living = (jnp.arange(per_device, dtype=jnp.int32) < counts[0]).astype(F32)[:, None]
    force_bias = jnp.trace(contracted, axis1=2, axis2=3) * living
    exchange_energy = -0.5 * jnp.einsum("wgnk,wgkn->wg", contracted, contracted) * living
    return (force_bias, exchange_energy)


def on_device(walkers, trial_orbitals, cholesky, branches, counts, field):
    walk_size, shard_count = lax.axis_size("walk"), lax.axis_size(SR)
    per = walkers.shape[0]
    if walk_size == shard_count and lax.axis_size("slab") == 2 and per % walk_size == 0 and not walk_size & (walk_size - 1):
        if cholesky.shape[0] * (per // walk_size) <= 4 and cholesky.shape[1] % 64 == 0 and per <= 128:
            return at_the_source(walkers, trial_orbitals, cholesky, branches, counts, field)
    return at_the_target(walkers, trial_orbitals, cholesky, branches, counts, field)


def solution(mesh):
    return jax.shard_map(
        on_device,
        mesh=mesh,
        in_specs=(
            P(("parts", "walk"), SR, None),
            P(("parts",) + SR, None),
            P(("parts",) + SR, None, None),
            P("parts"),
            P(("parts", "walk")),
            P(("parts", "walk"), SR),
        ),
        out_specs=(P(("parts", "walk"), SR), P(("parts", "walk"), SR)),
        check_vma=False,
    )
```

```python
import functools

import jax
import jax.numpy as jnp
from jax import lax
from jax.experimental import pallas as pl
from jax.experimental.pallas import tpu as pltpu
from jax.sharding import PartitionSpec as P

ITERS = 10
EARLY = 3
SR = ("slab", "row")
ALL = ("walk", "slab", "row")
F32 = jnp.float32
BF16 = jnp.bfloat16
VMEM_LIMIT = 24 * 2**20
SMALL_LIMIT = 2**20
AHEAD = pl.CostEstimate(flops=2**30, bytes_accessed=2**20, transcendentals=0)
HIGHEST = lax.Precision.HIGHEST


def dot(a, b, dims=((1,), (0,))):
    return lax.dot_general(a, b, (dims, ((), ())), preferred_element_type=F32)


def split(x):
    high = x.astype(BF16)
    return high, (x - high.astype(F32)).astype(BF16)


def place():
    return lax.axis_index("walk"), lax.axis_index("slab") * lax.axis_size("row") + lax.axis_index("row")


def whole(memory=pltpu.VMEM):
    return pl.BlockSpec(memory_space=memory)


def picks(branches, start, per, sender, share):
    places, olds = [jnp.int32(0)] * share, [jnp.int32(0)] * share
    rank = jnp.int32(0)
    for i in range(per):
        branch = branches[start + i]
        hit = lax.div(branch, per) == sender
        old = lax.rem(branch, per)
        for r in range(share):
            here = hit & (rank == r)
            places[r] = jnp.where(here, i, places[r])
            olds[r] = jnp.where(here, old, olds[r])
        rank = rank + hit.astype(jnp.int32)
    return places, olds


def select_kernel(n, per, share, branches, walkers, *refs):
    sends, sems = refs[:n], refs[n]
    walk, q = place()
    copies = []
    for k in list(range(1, n)) + [0]:
        olds = picks(branches, (q ^ k ^ walk) * per, per, walk, share)[1]
        for r in range(share):
            copies.append(pltpu.make_async_copy(walkers.at[olds[r]], sends[k].at[r], sems.at[k, r]))
            copies[-1].start()
    for copy in copies:
        copy.wait()


def select(n, per, share, branches, walkers):
    rows, electrons = walkers.shape[1:]
    return pl.pallas_call(
        functools.partial(select_kernel, n, per, share),
        out_shape=[jax.ShapeDtypeStruct((share, rows, electrons), walkers.dtype)] * n,
        in_specs=[whole(pltpu.SMEM), whole(pl.ANY)],
        out_specs=[whole(pl.ANY)] * n,
        scratch_shapes=[pltpu.SemaphoreType.DMA((n, share))],
        compiler_params=pltpu.CompilerParams(vmem_limit_bytes=SMALL_LIMIT),
        name="select",
    )(branches, walkers)


def message_kernel(trial, field, out):
    rows = trial.shape[0]
    out[:rows, :] = trial[...]
    rest, parts = field[...], []
    for _ in range(3):
        parts.append(rest.astype(BF16).astype(F32))
        rest = rest - parts[-1]
    spare = out.shape[0] - rows - 3 * field.shape[0]
    if spare:
        parts.append(jnp.zeros((spare, field.shape[1]), F32))
    out[rows:, :] = jnp.concatenate(parts, axis=0).astype(BF16)


def message(trial, field):
    height = trial.shape[0] + -(-3 * field.shape[0] // 16) * 16
    return pl.pallas_call(
        message_kernel,
        out_shape=jax.ShapeDtypeStruct((height, trial.shape[1]), trial.dtype),
        in_specs=[whole()] * 2,
        out_specs=whole(),
        compiler_params=pltpu.CompilerParams(vmem_limit_bytes=SMALL_LIMIT),
        name="message",
    )(trial, field)


def fields_kernel(n, per, share, branches, *refs):
    messages, fields = refs[:n], refs[n]
    walk, q = place()
    rows = fields.shape[2]
    places = picks(branches, walk * per, per, walk ^ q, share)[0]
    walker = lax.broadcasted_iota(jnp.int32, (per, rows), 0)
    for k in range(n):
        terms = messages[k][rows:, :].astype(F32)
        value = terms[:per] + terms[per : 2 * per] + terms[2 * per : 3 * per]
        chosen = [jnp.sum(jnp.where(walker == p, value, 0.0), axis=0, keepdims=True) for p in places]
        fields[pl.ds(q ^ k, 1), :, :] = jnp.concatenate(chosen, axis=0)[None]


def pick_fields(n, per, share, branches, messages):
    return pl.pallas_call(
        functools.partial(fields_kernel, n, per, share),
        out_shape=jax.ShapeDtypeStruct((n, share, messages[0].shape[1]), F32),
        in_specs=[whole(pltpu.SMEM)] + [whole()] * n,
        out_specs=whole(),
        compiler_params=pltpu.CompilerParams(vmem_limit_bytes=SMALL_LIMIT),
        name="fields",
    )(branches, *messages)


def turn_kernel(n, per, share, branches, counts, *refs):
    messages, turned, masks = refs[:n], refs[n], refs[n + 1]
    walk, q = place()
    rows = turned.shape[1] // n
    for k in range(n):
        turned[:, k * rows : (k + 1) * rows] = messages[k][:rows, :].T
    lane = lax.broadcasted_iota(jnp.int32, (1, 128), 1)
    for k in range(n):
        places = picks(branches, walk * per, per, walk ^ q ^ k, share)[0]
        for r in range(share):
            here = (lane == places[r]) & (places[r] < counts[0])
            masks[k * share + r : k * share + r + 1, :] = here.astype(F32)


def turn(n, per, share, branches, counts, messages):
    electrons = messages[0].shape[1]
    rows = n * (messages[0].shape[0] - -(-3 * per // 16) * 16)
    return pl.pallas_call(
        functools.partial(turn_kernel, n, per, share),
        out_shape=[
            jax.ShapeDtypeStruct((electrons, rows), messages[0].dtype),
            jax.ShapeDtypeStruct((n * share, 128), F32),
        ],
        in_specs=[whole(pltpu.SMEM)] * 2 + [whole()] * n,
        out_specs=[whole()] * 2,
        compiler_params=pltpu.CompilerParams(vmem_limit_bytes=SMALL_LIMIT),
        name="turn",
    )(branches, counts, *messages)


def squared(high, low):
    mixed = dot(high, low)
    return dot(high, high) + (mixed + mixed.T)


def propagate(share, k, block, fields, moved, start):
    q = place()[1]
    rows, electrons = block.shape[1:]
    lines = fields[pl.ds(q ^ k, 1), :, :].reshape(share, rows)
    if share % 8:
        lines = jnp.concatenate([lines, jnp.zeros((-share % 8, rows), F32)], axis=0)
    columns = lines.T
    for i in range(share):
        moved[start : start + rows, i * electrons : (i + 1) * electrons] = (
            block[i].astype(F32) * columns[:, i : i + 1]
        ).astype(BF16)


def first_kernel(n, share, *refs):
    blocks, turned, fields, moved, overlaps = refs[: n - 1], *refs[n - 1 :]
    rows = blocks[0].shape[1]
    for k in range(n - 1):
        propagate(share, k, blocks[k], fields, moved, k * rows)
    overlaps[...] = dot(turned[:, : (n - 1) * rows], moved[...])


def first_blocks(n, share, blocks, turned, fields):
    rows, electrons = blocks[0].shape[1:]
    return pl.pallas_call(
        functools.partial(first_kernel, n, share),
        out_shape=[
            jax.ShapeDtypeStruct(((n - 1) * rows, share * electrons), BF16),
            jax.ShapeDtypeStruct((electrons, share * electrons), F32),
        ],
        in_specs=[whole()] * (n + 1),
        out_specs=[whole()] * 2,
        compiler_params=pltpu.CompilerParams(vmem_limit_bytes=VMEM_LIMIT),
        cost_estimate=AHEAD,
        name="first",
    )(*blocks, turned, fields)


def green_kernel(n, share, *refs):
    block, turned, fields, earlier, begun = refs[:5]
    green, moved, left, right = refs[5:]
    q = place()[1]
    rows, electrons = block.shape[1:]
    propagate(share, n - 1, block, fields, moved, 0)
    overlaps = begun[...] + dot(turned[:, (n - 1) * rows :], moved[...])
    for i in range(share):
        overlap = overlaps[:, i * electrons : (i + 1) * electrons]
        size = jnp.abs(overlap)
        scale = jnp.max(jnp.sum(size, axis=0)) * jnp.max(jnp.sum(size, axis=1))
        left[i] = overlap.T / scale
        high, low = split(overlap)
        mixed = dot(high, low, ((1,), (1,)))
        right[i] = (dot(high, high, ((1,), (1,))) + (mixed + mixed.T)) / scale

    def advance(exact, step, carry):
        for i in range(share):
            now, matrix = left[i], right[i]
            high, low = split(matrix)
            left_high, left_low = split(now)
            product = dot(left_high, high)
            if exact:
                product = product + (dot(left_high, low) + dot(left_low, high))
            left[i] = 2.0 * now - product
            right[i] = 2.0 * matrix - squared(high, low)
        return carry

    lax.fori_loop(0, EARLY, functools.partial(advance, False), 0)
    lax.fori_loop(EARLY, ITERS - 1, functools.partial(advance, True), 0)
    for i in range(share):
        high, low = split(right[i])
        left_high, left_low = split(left[i])
        product = dot(left_high, high) + (dot(left_high, low) + dot(left_low, high))
        inverse = (2.0 * left[i] - product).astype(BF16)
        for k in range(n):
            at = pl.multiple_of((q ^ k) * rows, rows)
            held, start = (moved, 0) if k == n - 1 else (earlier, k * rows)
            green[pl.ds(at, rows), i * electrons : (i + 1) * electrons] = dot(
                held[start : start + rows, i * electrons : (i + 1) * electrons], inverse
            ).astype(BF16)


def make_green(n, share, block, turned, fields, earlier, begun):
    rows, electrons = block.shape[1:]
    return pl.pallas_call(
        functools.partial(green_kernel, n, share),
        out_shape=jax.ShapeDtypeStruct((n * rows, share * electrons), BF16),
        in_specs=[whole()] * 5,
        out_specs=whole(),
        scratch_shapes=[
            pltpu.VMEM((rows, share * electrons), BF16),
            pltpu.VMEM((share, electrons, electrons), F32),
            pltpu.VMEM((share, electrons, electrons), F32),
        ],
        compiler_params=pltpu.CompilerParams(vmem_limit_bytes=VMEM_LIMIT),
        name="green",
    )(block, turned, fields, earlier, begun)


def report(share, held, index, upper, lower):
    half = upper.shape[0]
    row = lax.broadcasted_iota(jnp.int32, (half, half), 0)
    column = lax.broadcasted_iota(jnp.int32, (half, half), 1)
    out_row = lax.broadcasted_iota(jnp.int32, held.shape, 0)
    for i in range(share):
        left, middle, right = 2 * i * half, (2 * i + 1) * half, 2 * (i + 1) * half
        a, b = upper[:, left:middle], upper[:, middle:right]
        c, d = lower[:, left:middle], lower[:, middle:right]
        trace = jnp.sum(jnp.where(row == column, a + d, 0.0))
        exchange = -0.5 * jnp.sum(a * a.T + d * d.T + 2.0 * (b * c.T))
        held = jnp.where(out_row == index * share + i, trace, held)
        held = jnp.where(out_row == held.shape[0] // 2 + index * share + i, exchange, held)
    return held


def near_kernel(share, count, height, *refs):
    vectors, green, outs = refs[:count], refs[count], refs[-1]
    for v in range(count):
        held = jnp.zeros(outs.shape[1:], F32)
        for g in range(vectors[v].shape[0] // height):
            full = dot(vectors[v][g * height : (g + 1) * height, :], green[...])
            held = report(share, held, g, full[: height // 2], full[height // 2 :])
        outs[v] = held


def shared_kernel(share, count, height, *refs):
    firsts, seconds, green = refs[:count], refs[count : 2 * count], refs[2 * count]
    outs, kept, both = refs[-count - 2], refs[-count - 1 : -1], refs[-1]
    parity = lax.axis_index("walk") & 1
    half = height // 2
    for v in range(count):
        rows = firsts[v].shape[0]
        for at, piece in ((parity, firsts[v]), (1 - parity, seconds[v])):
            both[pl.ds(pl.multiple_of(at * rows, 16), rows), :] = dot(piece[...], green[...])
        kept[v][...] = both[:half, :]
        held = jnp.zeros(outs.shape[1:], F32)
        for g in range(1, (2 * rows + half) // height):
            start = g * height - half
            held = report(share, held, g, both[start : start + half, :], both[start + half : start + height, :])
        outs[v] = held


def direct_kernel(share, count, *refs):
    uppers, green, kept = refs[:count], refs[count], refs[count + 1 : 2 * count + 1]
    before, outs = refs[-2:]
    for v in range(count):
        outs[v] = report(share, before[v], 0, dot(uppers[v][...], green[...]), kept[v][...])


def contract(kernel, count, vectors, green, *more, kept_rows=0, scratch_rows=0):
    wide = green.shape[1]
    kept = [jax.ShapeDtypeStruct((kept_rows, wide), F32)] * count if kept_rows else []
    return pl.pallas_call(
        kernel,
        out_shape=[jax.ShapeDtypeStruct((count, 8, 128), F32)] + kept,
        in_specs=[whole()] * (len(vectors) + 1 + len(more)),
        out_specs=[whole()] * (1 + len(kept)),
        scratch_shapes=[pltpu.VMEM((scratch_rows, wide), F32)] if scratch_rows else [],
        compiler_params=pltpu.CompilerParams(vmem_limit_bytes=VMEM_LIMIT),
        cost_estimate=pl.CostEstimate(
            flops=sum(2 * v.size * wide for v in vectors),
            bytes_accessed=sum(2 * v.size for v in vectors) + 2 * green.size,
            transcendentals=0,
        ),
        name="contract",
    )(*vectors, green, *more)


def unpack_kernel(n, share, masks, *refs):
    arrived, outs = refs[:n], refs[n:]
    vectors, per = outs[0].shape
    for which, out in enumerate(outs):
        for g in range(vectors):
            line = jnp.zeros((1, 128), F32)
            for k in range(n):
                for r in range(share):
                    cores, height = arrived[k].shape[:2]
                    at = which * (height // 2) + g * share + r
                    value = arrived[k][k % cores, at : at + 1, :]
                    line = jnp.where(masks[k * share + r : k * share + r + 1, :] > 0.0, value, line)
            out[g : g + 1, :] = line[:, :per]


def unpack(n, per, share, vectors, masks, arrived):
    return pl.pallas_call(
        functools.partial(unpack_kernel, n, share),
        out_shape=[jax.ShapeDtypeStruct((vectors, per), F32)] * 2,
        in_specs=[whole()] * (1 + n),
        out_specs=[whole()] * 2,
        compiler_params=pltpu.CompilerParams(vmem_limit_bytes=SMALL_LIMIT),
        name="unpack",
    )(masks, *arrived)


def at_the_source(walkers, trial_orbitals, cholesky, branches, counts, field):
    n = lax.axis_size("walk")
    per = walkers.shape[0]
    share = per // n
    row_size = lax.axis_size("row")
    vectors = cholesky.shape[0]
    pairs = [(w, q) for w in range(n) for q in range(n)]
    move = lambda x, k: lax.ppermute(x, SR, [(i, i ^ k) for i in range(n)])
    swap = lambda x: lax.ppermute(x, "walk", [(w, w ^ 1) for w in range(n)])
    ask = lambda x: lax.ppermute(x, ALL, [(w * n + q, (w ^ q) * n + q) for w, q in pairs])
    answer = lambda x, k: lax.ppermute(x, ALL, [(w * n + q, (w ^ q) * n + (q ^ k)) for w, q in pairs])
    near = [k for k in range(n) if k < row_size]
    far = [k for k in range(n) if k >= row_size]

    def spread(x):
        held = {}
        for k in far:
            low = k & (row_size - 1)
            held[k] = move(held[k ^ low], low) if low else move(x, k)
        return held

    def along(held):
        return {k: move(held[k & ~(row_size - 1)], k & (row_size - 1)) if k & (row_size - 1) else held[k] for k in far}

    ordered = lambda x, *first: lax.optimization_barrier((x,) + first)[0]
    heads = [k for k in far if not k & (row_size - 1)]
    height = cholesky.shape[1]
    rows = cholesky.reshape(vectors * height, cholesky.shape[2])
    direct_rows = height // 2
    shared_rows = (rows.shape[0] - direct_rows) // 2
    at = direct_rows + (lax.axis_index("walk") & 1) * shared_rows
    shared = lax.dynamic_slice_in_dim(rows, at, shared_rows, 0)
    sends = select(n, per, share, branches, walkers)
    own = message(ordered(trial_orbitals, sends[0]), field)
    messages = {0: own, **spread(own)}
    messages.update({k: move(own, k) for k in near[1:]})
    messages = [messages[k] for k in range(n)]
    crossed = {k: move(shared, k) for k in heads}
    close = [rows] + [move(rows, k) for k in near[1:]]
    early = close[1:]
    blocks = [sends[0]] + [
        move(ordered(sends[k], *(crossed.values() if k == n - 1 else early)), k) for k in range(1, n)
    ]
    asked = ask(pick_fields(n, per, share, branches, messages))
    turned, masks = turn(n, per, share, branches, counts, messages)
    other = {k: swap(x) for k, x in crossed.items()}
    earlier, begun = first_blocks(n, share, blocks[:-1], turned, asked)
    direct = {k: move(ordered(rows[:direct_rows], begun), k) for k in heads}
    green = make_green(n, share, blocks[n - 1], turned, asked, earlier, begun)
    crossed, other, direct = (along({k: ordered(x, green) for k, x in held.items()}) for held in (crossed, other, direct))
    [results] = contract(functools.partial(near_kernel, share, len(near), height), len(near), close, green)
    late, *kept = contract(
        functools.partial(shared_kernel, share, len(far), height),
        len(far),
        [crossed[k] for k in far] + [other[k] for k in far],
        ordered(green, results),
        kept_rows=direct_rows,
        scratch_rows=2 * shared_rows,
    )
    [late] = contract(
        functools.partial(direct_kernel, share, len(far)), len(far), [direct[k] for k in far], green, *kept, late
    )
    answers = [answer(late, far[0]), answer(ordered(results, late), 0)]
    arrived = [[x] + [move(x, k) for k in near[1:]] for x in reversed(answers)]
    return tuple(x.T for x in unpack(n, per, share, vectors, masks, [x for held in arrived for x in held]))


def newton_schulz(intersection):
    column_max = jnp.max(jnp.sum(jnp.abs(intersection), axis=0))
    row_max = jnp.max(jnp.sum(jnp.abs(intersection), axis=1))
    inverse = intersection.T / (column_max * row_max)
    twice_identity = 2.0 * jnp.eye(intersection.shape[0], dtype=intersection.dtype)
    for iteration in range(ITERS):
        inverse = jnp.dot(
            inverse,
            twice_identity - jnp.dot(intersection, inverse, precision=HIGHEST),
            precision=HIGHEST,
        )
    return inverse


def pick(array, indices):
    return jnp.concatenate(
        [lax.dynamic_slice_in_dim(array, indices[i], 1, 0) for i in range(indices.shape[0])], axis=0
    )


def at_the_target(walkers, trial_orbitals, cholesky, branches, counts, field):
    walk_size = lax.axis_size("walk")
    position = lax.axis_index("walk")
    per_device, row_count, electrons = walkers.shape
    capacity = (per_device + walk_size - 1) // walk_size
    sender = branches.reshape(walk_size, per_device) // per_device
    local_index = branches.reshape(walk_size, per_device) % per_device
    same_sender = sender[:, :, None] == sender[:, None, :]
    earlier = jnp.arange(per_device)[None, :] < jnp.arange(per_device)[:, None]
    arrival_rank = jnp.sum(same_sender & earlier[None], axis=2)
    wanted = (sender[:, None, :] == position) & (
        arrival_rank[:, None, :] == jnp.arange(capacity, dtype=jnp.int32)[None, :, None]
    )
    chosen = jnp.sum(jnp.where(wanted, local_index[:, None, :], 0), axis=2).reshape(-1)
    outgoing = pick(walkers, chosen).reshape(walk_size, capacity, row_count, electrons)
    arrived = lax.all_to_all(outgoing, "walk", split_axis=0, concat_axis=0, tiled=True)
    my_sender = lax.dynamic_index_in_dim(sender, position, 0, keepdims=False)
    my_rank = lax.dynamic_index_in_dim(arrival_rank, position, 0, keepdims=False)
    arrived_flat = arrived.reshape(walk_size * capacity, row_count, electrons)
    migrated = pick(arrived_flat, my_sender * capacity + my_rank)
    propagated = (migrated.astype(F32) * field[:, :, None]).astype(BF16)
    everything = lax.all_gather(propagated, SR, axis=1, tiled=True)
    shard_count = lax.axis_size(SR)
    share = per_device // shard_count
    trial_whole = lax.all_gather(trial_orbitals, SR, axis=0, tiled=True)
    own_walkers = lax.dynamic_slice_in_dim(everything, lax.axis_index(SR) * share, share, 0)
    intersection = jnp.einsum("mn,wmk->wnk", trial_whole, own_walkers, preferred_element_type=F32)
    inverse = jax.vmap(newton_schulz)(intersection).astype(BF16)
    inverses = lax.all_gather(inverse, SR, axis=0, tiled=True)
    green = jnp.einsum("wmn,wnk->wmk", everything, inverses, preferred_element_type=F32).astype(BF16)
    contracted = jnp.einsum("gnm,wmk->wgnk", cholesky, green, preferred_element_type=F32)
    living = (jnp.arange(per_device, dtype=jnp.int32) < counts[0]).astype(F32)[:, None]
    force_bias = jnp.trace(contracted, axis1=2, axis2=3) * living
    exchange_energy = -0.5 * jnp.einsum("wgnk,wgkn->wg", contracted, contracted) * living
    return (force_bias, exchange_energy)


def on_device(walkers, trial_orbitals, cholesky, branches, counts, field):
    walk_size, shard_count = lax.axis_size("walk"), lax.axis_size(SR)
    per = walkers.shape[0]
    if walk_size == shard_count and lax.axis_size("slab") == 2 and per % walk_size == 0 and not walk_size & (walk_size - 1):
        if cholesky.shape[0] * (per // walk_size) <= 4 and cholesky.shape[1] % 64 == 0 and per <= 128:
            return at_the_source(walkers, trial_orbitals, cholesky, branches, counts, field)
    return at_the_target(walkers, trial_orbitals, cholesky, branches, counts, field)


def solution(mesh):
    return jax.shard_map(
        on_device,
        mesh=mesh,
        in_specs=(
            P(("parts", "walk"), SR, None),
            P(("parts",) + SR, None),
            P(("parts",) + SR, None, None),
            P("parts"),
            P(("parts", "walk")),
            P(("parts", "walk"), SR),
        ),
        out_specs=(P(("parts", "walk"), SR), P(("parts", "walk"), SR)),
        check_vma=False,
    )
```

```python
import functools

import jax
import jax.numpy as jnp
from jax import lax
from jax.experimental import pallas as pl
from jax.experimental.pallas import tpu as pltpu
from jax.sharding import PartitionSpec as P

ITERS = 10
EARLY = 3
SR = ("slab", "row")
ALL = ("walk", "slab", "row")
F32 = jnp.float32
BF16 = jnp.bfloat16
VMEM_LIMIT = 24 * 2**20
SMALL_LIMIT = 2**20
AHEAD = pl.CostEstimate(flops=2**30, bytes_accessed=2**20, transcendentals=0)
HIGHEST = lax.Precision.HIGHEST


def dot(a, b, dims=((1,), (0,))):
    return lax.dot_general(a, b, (dims, ((), ())), preferred_element_type=F32)


def split(x):
    high = x.astype(BF16)
    return high, (x - high.astype(F32)).astype(BF16)


def place():
    return lax.axis_index("walk"), lax.axis_index("slab") * lax.axis_size("row") + lax.axis_index("row")


def whole(memory=pltpu.VMEM):
    return pl.BlockSpec(memory_space=memory)


def picks(branches, start, per, sender, share):
    places, olds = [jnp.int32(0)] * share, [jnp.int32(0)] * share
    rank = jnp.int32(0)
    for i in range(per):
        branch = branches[start + i]
        hit = lax.div(branch, per) == sender
        old = lax.rem(branch, per)
        for r in range(share):
            here = hit & (rank == r)
            places[r] = jnp.where(here, i, places[r])
            olds[r] = jnp.where(here, old, olds[r])
        rank = rank + hit.astype(jnp.int32)
    return places, olds


def select_kernel(n, per, share, branches, walkers, *refs):
    sends, sems = refs[:n], refs[n]
    walk, q = place()
    copies = []
    for k in list(range(1, n)) + [0]:
        olds = picks(branches, (q ^ k ^ walk) * per, per, walk, share)[1]
        for r in range(share):
            copies.append(pltpu.make_async_copy(walkers.at[olds[r]], sends[k].at[r], sems.at[k, r]))
            copies[-1].start()
    for copy in copies:
        copy.wait()


def select(n, per, share, branches, walkers):
    rows, electrons = walkers.shape[1:]
    return pl.pallas_call(
        functools.partial(select_kernel, n, per, share),
        out_shape=[jax.ShapeDtypeStruct((share, rows, electrons), walkers.dtype)] * n,
        in_specs=[whole(pltpu.SMEM), whole(pl.ANY)],
        out_specs=[whole(pl.ANY)] * n,
        scratch_shapes=[pltpu.SemaphoreType.DMA((n, share))],
        compiler_params=pltpu.CompilerParams(vmem_limit_bytes=SMALL_LIMIT),
        name="select",
    )(branches, walkers)


def message_kernel(trial, field, out):
    rows = trial.shape[0]
    out[:rows, :] = trial[...]
    rest, parts = field[...], []
    for _ in range(3):
        parts.append(rest.astype(BF16).astype(F32))
        rest = rest - parts[-1]
    spare = out.shape[0] - rows - 3 * field.shape[0]
    if spare:
        parts.append(jnp.zeros((spare, field.shape[1]), F32))
    out[rows:, :] = jnp.concatenate(parts, axis=0).astype(BF16)


def message(trial, field):
    height = trial.shape[0] + -(-3 * field.shape[0] // 16) * 16
    return pl.pallas_call(
        message_kernel,
        out_shape=jax.ShapeDtypeStruct((height, trial.shape[1]), trial.dtype),
        in_specs=[whole()] * 2,
        out_specs=whole(),
        compiler_params=pltpu.CompilerParams(vmem_limit_bytes=SMALL_LIMIT),
        name="message",
    )(trial, field)


def fields_kernel(n, per, share, branches, *refs):
    messages, fields = refs[:n], refs[n]
    walk, q = place()
    rows = fields.shape[2]
    places = picks(branches, walk * per, per, walk ^ q, share)[0]
    walker = lax.broadcasted_iota(jnp.int32, (per, rows), 0)
    for k in range(n):
        terms = messages[k][rows:, :].astype(F32)
        value = terms[:per] + terms[per : 2 * per] + terms[2 * per : 3 * per]
        chosen = [jnp.sum(jnp.where(walker == p, value, 0.0), axis=0, keepdims=True) for p in places]
        fields[pl.ds(q ^ k, 1), :, :] = jnp.concatenate(chosen, axis=0)[None]


def pick_fields(n, per, share, branches, messages):
    return pl.pallas_call(
        functools.partial(fields_kernel, n, per, share),
        out_shape=jax.ShapeDtypeStruct((n, share, messages[0].shape[1]), F32),
        in_specs=[whole(pltpu.SMEM)] + [whole()] * n,
        out_specs=whole(),
        compiler_params=pltpu.CompilerParams(vmem_limit_bytes=SMALL_LIMIT),
        name="fields",
    )(branches, *messages)


def turn_kernel(n, per, share, branches, counts, *refs):
    messages, turned, masks = refs[:n], refs[n], refs[n + 1]
    walk, q = place()
    rows = turned.shape[1] // n
    for k in range(n):
        turned[:, k * rows : (k + 1) * rows] = messages[k][:rows, :].T
    lane = lax.broadcasted_iota(jnp.int32, (1, 128), 1)
    for k in range(n):
        places = picks(branches, walk * per, per, walk ^ q ^ k, share)[0]
        for r in range(share):
            here = (lane == places[r]) & (places[r] < counts[0])
            masks[k * share + r : k * share + r + 1, :] = here.astype(F32)


def turn(n, per, share, branches, counts, messages):
    electrons = messages[0].shape[1]
    rows = n * (messages[0].shape[0] - -(-3 * per // 16) * 16)
    return pl.pallas_call(
        functools.partial(turn_kernel, n, per, share),
        out_shape=[
            jax.ShapeDtypeStruct((electrons, rows), messages[0].dtype),
            jax.ShapeDtypeStruct((n * share, 128), F32),
        ],
        in_specs=[whole(pltpu.SMEM)] * 2 + [whole()] * n,
        out_specs=[whole()] * 2,
        compiler_params=pltpu.CompilerParams(vmem_limit_bytes=SMALL_LIMIT),
        name="turn",
    )(branches, counts, *messages)


def squared(high, low):
    mixed = dot(high, low)
    return dot(high, high) + (mixed + mixed.T)


def propagate(share, k, block, fields, moved, start):
    q = place()[1]
    rows, electrons = block.shape[1:]
    lines = fields[pl.ds(q ^ k, 1), :, :].reshape(share, rows)
    if share % 8:
        lines = jnp.concatenate([lines, jnp.zeros((-share % 8, rows), F32)], axis=0)
    columns = lines.T
    for i in range(share):
        moved[start : start + rows, i * electrons : (i + 1) * electrons] = (
            block[i].astype(F32) * columns[:, i : i + 1]
        ).astype(BF16)


def first_kernel(n, share, *refs):
    blocks, turned, fields, moved, overlaps = refs[: n - 1], *refs[n - 1 :]
    rows = blocks[0].shape[1]
    for k in range(n - 1):
        propagate(share, k, blocks[k], fields, moved, k * rows)
    overlaps[...] = dot(turned[:, : (n - 1) * rows], moved[...])


def first_blocks(n, share, blocks, turned, fields):
    rows, electrons = blocks[0].shape[1:]
    return pl.pallas_call(
        functools.partial(first_kernel, n, share),
        out_shape=[
            jax.ShapeDtypeStruct(((n - 1) * rows, share * electrons), BF16),
            jax.ShapeDtypeStruct((electrons, share * electrons), F32),
        ],
        in_specs=[whole()] * (n + 1),
        out_specs=[whole()] * 2,
        compiler_params=pltpu.CompilerParams(vmem_limit_bytes=VMEM_LIMIT),
        cost_estimate=AHEAD,
        name="first",
    )(*blocks, turned, fields)


def green_kernel(n, share, *refs):
    block, turned, fields, earlier, begun = refs[:5]
    green, moved, left, right = refs[5:]
    q = place()[1]
    rows, electrons = block.shape[1:]
    propagate(share, n - 1, block, fields, moved, 0)
    overlaps = begun[...] + dot(turned[:, (n - 1) * rows :], moved[...])
    for i in range(share):
        overlap = overlaps[:, i * electrons : (i + 1) * electrons]
        size = jnp.abs(overlap)
        scale = jnp.max(jnp.sum(size, axis=0)) * jnp.max(jnp.sum(size, axis=1))
        left[i] = overlap.T / scale
        high, low = split(overlap)
        mixed = dot(high, low, ((1,), (1,)))
        right[i] = (dot(high, high, ((1,), (1,))) + (mixed + mixed.T)) / scale

    def advance(exact):
        for i in range(share):
            now, matrix = left[i], right[i]
            high, low = split(matrix)
            left_high, left_low = split(now)
            product = dot(left_high, high)
            if exact:
                product = product + (dot(left_high, low) + dot(left_low, high))
            left[i] = 2.0 * now - product
            right[i] = 2.0 * matrix - squared(high, low)

    for step in range(ITERS - 1):
        advance(step >= EARLY)
    for i in range(share):
        high, low = split(right[i])
        left_high, left_low = split(left[i])
        product = dot(left_high, high) + (dot(left_high, low) + dot(left_low, high))
        inverse = (2.0 * left[i] - product).astype(BF16)
        for k in range(n):
            at = pl.multiple_of((q ^ k) * rows, rows)
            held, start = (moved, 0) if k == n - 1 else (earlier, k * rows)
            green[pl.ds(at, rows), i * electrons : (i + 1) * electrons] = dot(
                held[start : start + rows, i * electrons : (i + 1) * electrons], inverse
            ).astype(BF16)


def make_green(n, share, block, turned, fields, earlier, begun):
    rows, electrons = block.shape[1:]
    return pl.pallas_call(
        functools.partial(green_kernel, n, share),
        out_shape=jax.ShapeDtypeStruct((n * rows, share * electrons), BF16),
        in_specs=[whole()] * 5,
        out_specs=whole(),
        scratch_shapes=[
            pltpu.VMEM((rows, share * electrons), BF16),
            pltpu.VMEM((share, electrons, electrons), F32),
            pltpu.VMEM((share, electrons, electrons), F32),
        ],
        compiler_params=pltpu.CompilerParams(vmem_limit_bytes=VMEM_LIMIT),
        name="green",
    )(block, turned, fields, earlier, begun)


def report(share, held, index, upper, lower):
    half = upper.shape[0]
    row = lax.broadcasted_iota(jnp.int32, (half, half), 0)
    column = lax.broadcasted_iota(jnp.int32, (half, half), 1)
    out_row = lax.broadcasted_iota(jnp.int32, held.shape, 0)
    for i in range(share):
        left, middle, right = 2 * i * half, (2 * i + 1) * half, 2 * (i + 1) * half
        a, b = upper[:, left:middle], upper[:, middle:right]
        c, d = lower[:, left:middle], lower[:, middle:right]
        trace = jnp.sum(jnp.where(row == column, a + d, 0.0))
        exchange = -0.5 * jnp.sum(a * a.T + d * d.T + 2.0 * (b * c.T))
        held = jnp.where(out_row == index * share + i, trace, held)
        held = jnp.where(out_row == held.shape[0] // 2 + index * share + i, exchange, held)
    return held


def near_kernel(share, count, height, *refs):
    vectors, green, outs = refs[:count], refs[count], refs[-1]
    for v in range(count):
        held = jnp.zeros(outs.shape[1:], F32)
        for g in range(vectors[v].shape[0] // height):
            full = dot(vectors[v][g * height : (g + 1) * height, :], green[...])
            held = report(share, held, g, full[: height // 2], full[height // 2 :])
        outs[v] = held


def shared_kernel(share, count, height, *refs):
    firsts, seconds, green = refs[:count], refs[count : 2 * count], refs[2 * count]
    outs, kept, both = refs[-count - 2], refs[-count - 1 : -1], refs[-1]
    parity = lax.axis_index("walk") & 1
    half = height // 2
    for v in range(count):
        rows = firsts[v].shape[0]
        for at, piece in ((parity, firsts[v]), (1 - parity, seconds[v])):
            both[pl.ds(pl.multiple_of(at * rows, 16), rows), :] = dot(piece[...], green[...])
        kept[v][...] = both[:half, :]
        held = jnp.zeros(outs.shape[1:], F32)
        for g in range(1, (2 * rows + half) // height):
            start = g * height - half
            held = report(share, held, g, both[start : start + half, :], both[start + half : start + height, :])
        outs[v] = held


def direct_kernel(share, count, *refs):
    uppers, green, kept = refs[:count], refs[count], refs[count + 1 : 2 * count + 1]
    before, outs = refs[-2:]
    for v in range(count):
        outs[v] = report(share, before[v], 0, dot(uppers[v][...], green[...]), kept[v][...])


def contract(kernel, count, vectors, green, *more, kept_rows=0, scratch_rows=0):
    wide = green.shape[1]
    kept = [jax.ShapeDtypeStruct((kept_rows, wide), F32)] * count if kept_rows else []
    return pl.pallas_call(
        kernel,
        out_shape=[jax.ShapeDtypeStruct((count, 8, 128), F32)] + kept,
        in_specs=[whole()] * (len(vectors) + 1 + len(more)),
        out_specs=[whole()] * (1 + len(kept)),
        scratch_shapes=[pltpu.VMEM((scratch_rows, wide), F32)] if scratch_rows else [],
        compiler_params=pltpu.CompilerParams(vmem_limit_bytes=VMEM_LIMIT),
        cost_estimate=pl.CostEstimate(
            flops=sum(2 * v.size * wide for v in vectors),
            bytes_accessed=sum(2 * v.size for v in vectors) + 2 * green.size,
            transcendentals=0,
        ),
        name="contract",
    )(*vectors, green, *more)


def unpack_kernel(n, share, masks, *refs):
    arrived, outs = refs[:n], refs[n:]
    vectors, per = outs[0].shape
    for which, out in enumerate(outs):
        for g in range(vectors):
            line = jnp.zeros((1, 128), F32)
            for k in range(n):
                for r in range(share):
                    cores, height = arrived[k].shape[:2]
                    at = which * (height // 2) + g * share + r
                    value = arrived[k][k % cores, at : at + 1, :]
                    line = jnp.where(masks[k * share + r : k * share + r + 1, :] > 0.0, value, line)
            out[g : g + 1, :] = line[:, :per]


def unpack(n, per, share, vectors, masks, arrived):
    return pl.pallas_call(
        functools.partial(unpack_kernel, n, share),
        out_shape=[jax.ShapeDtypeStruct((vectors, per), F32)] * 2,
        in_specs=[whole()] * (1 + n),
        out_specs=[whole()] * 2,
        compiler_params=pltpu.CompilerParams(vmem_limit_bytes=SMALL_LIMIT),
        name="unpack",
    )(masks, *arrived)


def at_the_source(walkers, trial_orbitals, cholesky, branches, counts, field):
    n = lax.axis_size("walk")
    per = walkers.shape[0]
    share = per // n
    row_size = lax.axis_size("row")
    vectors = cholesky.shape[0]
    pairs = [(w, q) for w in range(n) for q in range(n)]
    move = lambda x, k: lax.ppermute(x, SR, [(i, i ^ k) for i in range(n)])
    swap = lambda x: lax.ppermute(x, "walk", [(w, w ^ 1) for w in range(n)])
    ask = lambda x: lax.ppermute(x, ALL, [(w * n + q, (w ^ q) * n + q) for w, q in pairs])
    answer = lambda x, k: lax.ppermute(x, ALL, [(w * n + q, (w ^ q) * n + (q ^ k)) for w, q in pairs])
    near = [k for k in range(n) if k < row_size]
    far = [k for k in range(n) if k >= row_size]

    def spread(x):
        held = {}
        for k in far:
            low = k & (row_size - 1)
            held[k] = move(held[k ^ low], low) if low else move(x, k)
        return held

    def along(held):
        return {k: move(held[k & ~(row_size - 1)], k & (row_size - 1)) if k & (row_size - 1) else held[k] for k in far}

    ordered = lambda x, *first: lax.optimization_barrier((x,) + first)[0]
    heads = [k for k in far if not k & (row_size - 1)]
    height = cholesky.shape[1]
    rows = cholesky.reshape(vectors * height, cholesky.shape[2])
    direct_rows = height // 2
    shared_rows = (rows.shape[0] - direct_rows) // 2
    at = direct_rows + (lax.axis_index("walk") & 1) * shared_rows
    shared = lax.dynamic_slice_in_dim(rows, at, shared_rows, 0)
    sends = select(n, per, share, branches, walkers)
    own = message(ordered(trial_orbitals, sends[0]), field)
    messages = {0: own, **spread(own)}
    messages.update({k: move(own, k) for k in near[1:]})
    messages = [messages[k] for k in range(n)]
    crossed = {k: move(shared, k) for k in heads}
    close = [rows] + [move(rows, k) for k in near[1:]]
    early = close[1:]
    blocks = [sends[0]] + [
        move(ordered(sends[k], *(crossed.values() if k == n - 1 else early)), k) for k in range(1, n)
    ]
    asked = ask(pick_fields(n, per, share, branches, messages))
    turned, masks = turn(n, per, share, branches, counts, messages)
    other = {k: swap(x) for k, x in crossed.items()}
    earlier, begun = first_blocks(n, share, blocks[:-1], turned, asked)
    direct = {k: move(ordered(rows[:direct_rows], begun), k) for k in heads}
    green = make_green(n, share, blocks[n - 1], turned, asked, earlier, begun)
    crossed = along(crossed)
    other, direct = (along({k: ordered(x, green) for k, x in held.items()}) for held in (other, direct))
    [results] = contract(functools.partial(near_kernel, share, len(near), height), len(near), close, green)
    late, *kept = contract(
        functools.partial(shared_kernel, share, len(far), height),
        len(far),
        [crossed[k] for k in far] + [other[k] for k in far],
        ordered(green, results),
        kept_rows=direct_rows,
        scratch_rows=2 * shared_rows,
    )
    [late] = contract(
        functools.partial(direct_kernel, share, len(far)), len(far), [direct[k] for k in far], green, *kept, late
    )
    answers = [answer(late, far[0]), answer(ordered(results, late), 0)]
    arrived = [[x] + [move(x, k) for k in near[1:]] for x in reversed(answers)]
    return tuple(x.T for x in unpack(n, per, share, vectors, masks, [x for held in arrived for x in held]))


def newton_schulz(intersection):
    column_max = jnp.max(jnp.sum(jnp.abs(intersection), axis=0))
    row_max = jnp.max(jnp.sum(jnp.abs(intersection), axis=1))
    inverse = intersection.T / (column_max * row_max)
    twice_identity = 2.0 * jnp.eye(intersection.shape[0], dtype=intersection.dtype)
    for iteration in range(ITERS):
        inverse = jnp.dot(
            inverse,
            twice_identity - jnp.dot(intersection, inverse, precision=HIGHEST),
            precision=HIGHEST,
        )
    return inverse


def pick(array, indices):
    return jnp.concatenate(
        [lax.dynamic_slice_in_dim(array, indices[i], 1, 0) for i in range(indices.shape[0])], axis=0
    )


def at_the_target(walkers, trial_orbitals, cholesky, branches, counts, field):
    walk_size = lax.axis_size("walk")
    position = lax.axis_index("walk")
    per_device, row_count, electrons = walkers.shape
    capacity = (per_device + walk_size - 1) // walk_size
    sender = branches.reshape(walk_size, per_device) // per_device
    local_index = branches.reshape(walk_size, per_device) % per_device
    same_sender = sender[:, :, None] == sender[:, None, :]
    earlier = jnp.arange(per_device)[None, :] < jnp.arange(per_device)[:, None]
    arrival_rank = jnp.sum(same_sender & earlier[None], axis=2)
    wanted = (sender[:, None, :] == position) & (
        arrival_rank[:, None, :] == jnp.arange(capacity, dtype=jnp.int32)[None, :, None]
    )
    chosen = jnp.sum(jnp.where(wanted, local_index[:, None, :], 0), axis=2).reshape(-1)
    outgoing = pick(walkers, chosen).reshape(walk_size, capacity, row_count, electrons)
    arrived = lax.all_to_all(outgoing, "walk", split_axis=0, concat_axis=0, tiled=True)
    my_sender = lax.dynamic_index_in_dim(sender, position, 0, keepdims=False)
    my_rank = lax.dynamic_index_in_dim(arrival_rank, position, 0, keepdims=False)
    arrived_flat = arrived.reshape(walk_size * capacity, row_count, electrons)
    migrated = pick(arrived_flat, my_sender * capacity + my_rank)
    propagated = (migrated.astype(F32) * field[:, :, None]).astype(BF16)
    everything = lax.all_gather(propagated, SR, axis=1, tiled=True)
    shard_count = lax.axis_size(SR)
    share = per_device // shard_count
    trial_whole = lax.all_gather(trial_orbitals, SR, axis=0, tiled=True)
    own_walkers = lax.dynamic_slice_in_dim(everything, lax.axis_index(SR) * share, share, 0)
    intersection = jnp.einsum("mn,wmk->wnk", trial_whole, own_walkers, preferred_element_type=F32)
    inverse = jax.vmap(newton_schulz)(intersection).astype(BF16)
    inverses = lax.all_gather(inverse, SR, axis=0, tiled=True)
    green = jnp.einsum("wmn,wnk->wmk", everything, inverses, preferred_element_type=F32).astype(BF16)
    contracted = jnp.einsum("gnm,wmk->wgnk", cholesky, green, preferred_element_type=F32)
    living = (jnp.arange(per_device, dtype=jnp.int32) < counts[0]).astype(F32)[:, None]
    force_bias = jnp.trace(contracted, axis1=2, axis2=3) * living
    exchange_energy = -0.5 * jnp.einsum("wgnk,wgkn->wg", contracted, contracted) * living
    return (force_bias, exchange_energy)


def on_device(walkers, trial_orbitals, cholesky, branches, counts, field):
    walk_size, shard_count = lax.axis_size("walk"), lax.axis_size(SR)
    per = walkers.shape[0]
    if walk_size == shard_count and lax.axis_size("slab") == 2 and per % walk_size == 0 and not walk_size & (walk_size - 1):
        if cholesky.shape[0] * (per // walk_size) <= 4 and cholesky.shape[1] % 64 == 0 and per <= 128:
            return at_the_source(walkers, trial_orbitals, cholesky, branches, counts, field)
    return at_the_target(walkers, trial_orbitals, cholesky, branches, counts, field)


def solution(mesh):
    return jax.shard_map(
        on_device,
        mesh=mesh,
        in_specs=(
            P(("parts", "walk"), SR, None),
            P(("parts",) + SR, None),
            P(("parts",) + SR, None, None),
            P("parts"),
            P(("parts", "walk")),
            P(("parts", "walk"), SR),
        ),
        out_specs=(P(("parts", "walk"), SR), P(("parts", "walk"), SR)),
        check_vma=False,
    )
```

```python
import functools

import jax
import jax.numpy as jnp
from jax import lax
from jax.experimental import pallas as pl
from jax.experimental.pallas import tpu as pltpu
from jax.sharding import PartitionSpec as P

ITERS = 10
EARLY = 3
SR = ("slab", "row")
ALL = ("walk", "slab", "row")
F32 = jnp.float32
BF16 = jnp.bfloat16
VMEM_LIMIT = 24 * 2**20
SMALL_LIMIT = 2**20
AHEAD = pl.CostEstimate(flops=2**30, bytes_accessed=2**20, transcendentals=0)
HIGHEST = lax.Precision.HIGHEST


def dot(a, b, dims=((1,), (0,))):
    return lax.dot_general(a, b, (dims, ((), ())), preferred_element_type=F32)


def split(x):
    high = x.astype(BF16)
    return high, (x - high.astype(F32)).astype(BF16)


def place():
    return lax.axis_index("walk"), lax.axis_index("slab") * lax.axis_size("row") + lax.axis_index("row")


def whole(memory=pltpu.VMEM):
    return pl.BlockSpec(memory_space=memory)


def picks(branches, start, per, sender, share):
    places, olds = [jnp.int32(0)] * share, [jnp.int32(0)] * share
    rank = jnp.int32(0)
    for i in range(per):
        branch = branches[start + i]
        hit = lax.div(branch, per) == sender
        old = lax.rem(branch, per)
        for r in range(share):
            here = hit & (rank == r)
            places[r] = jnp.where(here, i, places[r])
            olds[r] = jnp.where(here, old, olds[r])
        rank = rank + hit.astype(jnp.int32)
    return places, olds


def select_kernel(n, per, share, branches, walkers, *refs):
    sends, sems = refs[:n], refs[n]
    walk, q = place()
    copies = []
    for k in list(range(1, n)) + [0]:
        olds = picks(branches, (q ^ k ^ walk) * per, per, walk, share)[1]
        for r in range(share):
            copies.append(pltpu.make_async_copy(walkers.at[olds[r]], sends[k].at[r], sems.at[k, r]))
            copies[-1].start()
    for copy in copies:
        copy.wait()


def select(n, per, share, branches, walkers):
    rows, electrons = walkers.shape[1:]
    return pl.pallas_call(
        functools.partial(select_kernel, n, per, share),
        out_shape=[jax.ShapeDtypeStruct((share, rows, electrons), walkers.dtype)] * n,
        in_specs=[whole(pltpu.SMEM), whole(pl.ANY)],
        out_specs=[whole(pl.ANY)] * n,
        scratch_shapes=[pltpu.SemaphoreType.DMA((n, share))],
        compiler_params=pltpu.CompilerParams(vmem_limit_bytes=SMALL_LIMIT),
        name="select",
    )(branches, walkers)


def message_kernel(trial, field, out):
    rows = trial.shape[0]
    out[:rows, :] = trial[...]
    rest, parts = field[...], []
    for _ in range(3):
        parts.append(rest.astype(BF16).astype(F32))
        rest = rest - parts[-1]
    spare = out.shape[0] - rows - 3 * field.shape[0]
    if spare:
        parts.append(jnp.zeros((spare, field.shape[1]), F32))
    out[rows:, :] = jnp.concatenate(parts, axis=0).astype(BF16)


def message(trial, field):
    height = trial.shape[0] + -(-3 * field.shape[0] // 16) * 16
    return pl.pallas_call(
        message_kernel,
        out_shape=jax.ShapeDtypeStruct((height, trial.shape[1]), trial.dtype),
        in_specs=[whole()] * 2,
        out_specs=whole(),
        compiler_params=pltpu.CompilerParams(vmem_limit_bytes=SMALL_LIMIT),
        name="message",
    )(trial, field)


def fields_kernel(n, per, share, branches, *refs):
    messages, fields = refs[:n], refs[n]
    walk, q = place()
    rows = fields.shape[2]
    places = picks(branches, walk * per, per, walk ^ q, share)[0]
    walker = lax.broadcasted_iota(jnp.int32, (per, rows), 0)
    for k in range(n):
        terms = messages[k][rows:, :].astype(F32)
        value = terms[:per] + terms[per : 2 * per] + terms[2 * per : 3 * per]
        chosen = [jnp.sum(jnp.where(walker == p, value, 0.0), axis=0, keepdims=True) for p in places]
        fields[pl.ds(q ^ k, 1), :, :] = jnp.concatenate(chosen, axis=0)[None]


def pick_fields(n, per, share, branches, messages):
    return pl.pallas_call(
        functools.partial(fields_kernel, n, per, share),
        out_shape=jax.ShapeDtypeStruct((n, share, messages[0].shape[1]), F32),
        in_specs=[whole(pltpu.SMEM)] + [whole()] * n,
        out_specs=whole(),
        compiler_params=pltpu.CompilerParams(vmem_limit_bytes=SMALL_LIMIT),
        name="fields",
    )(branches, *messages)


def turn_kernel(n, per, share, branches, counts, *refs):
    messages, turned, masks = refs[:n], refs[n], refs[n + 1]
    walk, q = place()
    rows = turned.shape[1] // n
    for k in range(n):
        turned[:, k * rows : (k + 1) * rows] = messages[k][:rows, :].T
    lane = lax.broadcasted_iota(jnp.int32, (1, 128), 1)
    for k in range(n):
        places = picks(branches, walk * per, per, walk ^ q ^ k, share)[0]
        for r in range(share):
            here = (lane == places[r]) & (places[r] < counts[0])
            masks[k * share + r : k * share + r + 1, :] = here.astype(F32)


def turn(n, per, share, branches, counts, messages):
    electrons = messages[0].shape[1]
    rows = n * (messages[0].shape[0] - -(-3 * per // 16) * 16)
    return pl.pallas_call(
        functools.partial(turn_kernel, n, per, share),
        out_shape=[
            jax.ShapeDtypeStruct((electrons, rows), messages[0].dtype),
            jax.ShapeDtypeStruct((n * share, 128), F32),
        ],
        in_specs=[whole(pltpu.SMEM)] * 2 + [whole()] * n,
        out_specs=[whole()] * 2,
        compiler_params=pltpu.CompilerParams(vmem_limit_bytes=SMALL_LIMIT),
        name="turn",
    )(branches, counts, *messages)


def squared(high, low):
    mixed = dot(high, low)
    return dot(high, high) + (mixed + mixed.T)


def propagate(share, k, block, fields, moved, start):
    q = place()[1]
    rows, electrons = block.shape[1:]
    lines = fields[pl.ds(q ^ k, 1), :, :].reshape(share, rows)
    if share % 8:
        lines = jnp.concatenate([lines, jnp.zeros((-share % 8, rows), F32)], axis=0)
    columns = lines.T
    for i in range(share):
        moved[start : start + rows, i * electrons : (i + 1) * electrons] = (
            block[i].astype(F32) * columns[:, i : i + 1]
        ).astype(BF16)


def first_kernel(n, share, *refs):
    blocks, turned, fields, moved, overlaps = refs[: n - 1], *refs[n - 1 :]
    rows = blocks[0].shape[1]
    for k in range(n - 1):
        propagate(share, k, blocks[k], fields, moved, k * rows)
    overlaps[...] = dot(turned[:, : (n - 1) * rows], moved[...])


def first_blocks(n, share, blocks, turned, fields):
    rows, electrons = blocks[0].shape[1:]
    return pl.pallas_call(
        functools.partial(first_kernel, n, share),
        out_shape=[
            jax.ShapeDtypeStruct(((n - 1) * rows, share * electrons), BF16),
            jax.ShapeDtypeStruct((electrons, share * electrons), F32),
        ],
        in_specs=[whole()] * (n + 1),
        out_specs=[whole()] * 2,
        compiler_params=pltpu.CompilerParams(vmem_limit_bytes=VMEM_LIMIT),
        cost_estimate=AHEAD,
        name="first",
    )(*blocks, turned, fields)


def green_kernel(n, share, *refs):
    block, turned, fields, earlier, begun = refs[:5]
    green, moved, left, right = refs[5:]
    q = place()[1]
    rows, electrons = block.shape[1:]
    propagate(share, n - 1, block, fields, moved, 0)
    overlaps = begun[...] + dot(turned[:, (n - 1) * rows :], moved[...])
    for i in range(share):
        overlap = overlaps[:, i * electrons : (i + 1) * electrons]
        size = jnp.abs(overlap)
        scale = jnp.max(jnp.sum(size, axis=0)) * jnp.max(jnp.sum(size, axis=1))
        left[i] = overlap.T / scale
        high, low = split(overlap)
        mixed = dot(high, low, ((1,), (1,)))
        right[i] = (dot(high, high, ((1,), (1,))) + (mixed + mixed.T)) / scale

    def advance(exact):
        for i in range(share):
            now, matrix = left[i], right[i]
            high, low = split(matrix)
            left_high, left_low = split(now)
            product = dot(left_high, high)
            if exact:
                product = product + (dot(left_high, low) + dot(left_low, high))
            left[i] = 2.0 * now - product
            right[i] = 2.0 * matrix - squared(high, low)

    for step in range(ITERS - 1):
        advance(step >= EARLY)
    for i in range(share):
        high, low = split(right[i])
        left_high, left_low = split(left[i])
        product = dot(left_high, high) + (dot(left_high, low) + dot(left_low, high))
        inverse = (2.0 * left[i] - product).astype(BF16)
        for k in range(n):
            at = pl.multiple_of((q ^ k) * rows, rows)
            held, start = (moved, 0) if k == n - 1 else (earlier, k * rows)
            green[pl.ds(at, rows), i * electrons : (i + 1) * electrons] = dot(
                held[start : start + rows, i * electrons : (i + 1) * electrons], inverse
            ).astype(BF16)


def make_green(n, share, block, turned, fields, earlier, begun):
    rows, electrons = block.shape[1:]
    return pl.pallas_call(
        functools.partial(green_kernel, n, share),
        out_shape=jax.ShapeDtypeStruct((n * rows, share * electrons), BF16),
        in_specs=[whole()] * 5,
        out_specs=whole(),
        scratch_shapes=[
            pltpu.VMEM((rows, share * electrons), BF16),
            pltpu.VMEM((share, electrons, electrons), F32),
            pltpu.VMEM((share, electrons, electrons), F32),
        ],
        compiler_params=pltpu.CompilerParams(vmem_limit_bytes=VMEM_LIMIT),
        name="green",
    )(block, turned, fields, earlier, begun)


def report(share, held, index, upper, lower):
    half = upper.shape[0]
    row = lax.broadcasted_iota(jnp.int32, (half, half), 0)
    column = lax.broadcasted_iota(jnp.int32, (half, half), 1)
    out_row = lax.broadcasted_iota(jnp.int32, held.shape, 0)
    for i in range(share):
        left, middle, right = 2 * i * half, (2 * i + 1) * half, 2 * (i + 1) * half
        a, b = upper[:, left:middle], upper[:, middle:right]
        c, d = lower[:, left:middle], lower[:, middle:right]
        trace = jnp.sum(jnp.where(row == column, a + d, 0.0))
        exchange = -0.5 * jnp.sum(a * a.T + d * d.T + 2.0 * (b * c.T))
        held = jnp.where(out_row == index * share + i, trace, held)
        held = jnp.where(out_row == held.shape[0] // 2 + index * share + i, exchange, held)
    return held


def near_kernel(share, count, height, *refs):
    vectors, green, outs = refs[:count], refs[count], refs[-1]
    for v in range(count):
        held = jnp.zeros(outs.shape[1:], F32)
        for g in range(vectors[v].shape[0] // height):
            full = dot(vectors[v][g * height : (g + 1) * height, :], green[...])
            held = report(share, held, g, full[: height // 2], full[height // 2 :])
        outs[v] = held


def shared_kernel(share, count, height, *refs):
    firsts, seconds, green = refs[:count], refs[count : 2 * count], refs[2 * count]
    outs, kept, both = refs[-count - 2], refs[-count - 1 : -1], refs[-1]
    parity = lax.axis_index("walk") & 1
    half = height // 2
    for v in range(count):
        rows = firsts[v].shape[0]
        for at, piece in ((parity, firsts[v]), (1 - parity, seconds[v])):
            both[pl.ds(pl.multiple_of(at * rows, 16), rows), :] = dot(piece[...], green[...])
        kept[v][...] = both[:half, :]
        held = jnp.zeros(outs.shape[1:], F32)
        for g in range(1, (2 * rows + half) // height):
            start = g * height - half
            held = report(share, held, g, both[start : start + half, :], both[start + half : start + height, :])
        outs[v] = held


def direct_kernel(share, count, *refs):
    uppers, green, kept = refs[:count], refs[count], refs[count + 1 : 2 * count + 1]
    before, outs = refs[-2:]
    for v in range(count):
        outs[v] = report(share, before[v], 0, dot(uppers[v][...], green[...]), kept[v][...])


def contract(kernel, count, vectors, green, *more, kept_rows=0, scratch_rows=0):
    wide = green.shape[1]
    kept = [jax.ShapeDtypeStruct((kept_rows, wide), F32)] * count if kept_rows else []
    return pl.pallas_call(
        kernel,
        out_shape=[jax.ShapeDtypeStruct((count, 8, 128), F32)] + kept,
        in_specs=[whole()] * (len(vectors) + 1 + len(more)),
        out_specs=[whole()] * (1 + len(kept)),
        scratch_shapes=[pltpu.VMEM((scratch_rows, wide), F32)] if scratch_rows else [],
        compiler_params=pltpu.CompilerParams(vmem_limit_bytes=VMEM_LIMIT),
        cost_estimate=pl.CostEstimate(
            flops=sum(2 * v.size * wide for v in vectors),
            bytes_accessed=sum(2 * v.size for v in vectors) + 2 * green.size,
            transcendentals=0,
        ),
        name="contract",
    )(*vectors, green, *more)


def unpack_kernel(n, share, masks, *refs):
    arrived, outs = refs[:n], refs[n:]
    vectors, per = outs[0].shape
    for which, out in enumerate(outs):
        for g in range(vectors):
            line = jnp.zeros((1, 128), F32)
            for k in range(n):
                for r in range(share):
                    cores, height = arrived[k].shape[:2]
                    at = which * (height // 2) + g * share + r
                    value = arrived[k][k % cores, at : at + 1, :]
                    line = jnp.where(masks[k * share + r : k * share + r + 1, :] > 0.0, value, line)
            out[g : g + 1, :] = line[:, :per]


def unpack(n, per, share, vectors, masks, arrived):
    return pl.pallas_call(
        functools.partial(unpack_kernel, n, share),
        out_shape=[jax.ShapeDtypeStruct((vectors, per), F32)] * 2,
        in_specs=[whole()] * (1 + n),
        out_specs=[whole()] * 2,
        compiler_params=pltpu.CompilerParams(vmem_limit_bytes=SMALL_LIMIT),
        name="unpack",
    )(masks, *arrived)


def at_the_source(walkers, trial_orbitals, cholesky, branches, counts, field):
    n = lax.axis_size("walk")
    per = walkers.shape[0]
    share = per // n
    row_size = lax.axis_size("row")
    vectors = cholesky.shape[0]
    pairs = [(w, q) for w in range(n) for q in range(n)]
    move = lambda x, k: lax.ppermute(x, SR, [(i, i ^ k) for i in range(n)])
    swap = lambda x: lax.ppermute(x, "walk", [(w, w ^ 1) for w in range(n)])
    ask = lambda x: lax.ppermute(x, ALL, [(w * n + q, (w ^ q) * n + q) for w, q in pairs])
    answer = lambda x, k: lax.ppermute(x, ALL, [(w * n + q, (w ^ q) * n + (q ^ k)) for w, q in pairs])
    near = [k for k in range(n) if k < row_size]
    far = [k for k in range(n) if k >= row_size]

    def spread(x):
        held = {}
        for k in far:
            low = k & (row_size - 1)
            held[k] = move(held[k ^ low], low) if low else move(x, k)
        return held

    def along(held):
        return {k: move(held[k & ~(row_size - 1)], k & (row_size - 1)) if k & (row_size - 1) else held[k] for k in far}

    ordered = lambda x, *first: lax.optimization_barrier((x,) + first)[0]
    heads = [k for k in far if not k & (row_size - 1)]
    height = cholesky.shape[1]
    rows = cholesky.reshape(vectors * height, cholesky.shape[2])
    direct_rows = height // 2
    shared_rows = (rows.shape[0] - direct_rows) // 2
    at = direct_rows + (lax.axis_index("walk") & 1) * shared_rows
    shared = lax.dynamic_slice_in_dim(rows, at, shared_rows, 0)
    sends = select(n, per, share, branches, walkers)
    own = message(ordered(trial_orbitals, sends[0]), field)
    messages = {0: own, **spread(own)}
    messages.update({k: move(own, k) for k in near[1:]})
    messages = [messages[k] for k in range(n)]
    crossed = {k: move(shared, k) for k in heads}
    close = [rows] + [move(rows, k) for k in near[1:]]
    early = close[1:]
    blocks = [sends[0]] + [
        move(ordered(sends[k], *(crossed.values() if k == n - 1 else early)), k) for k in range(1, n)
    ]
    asked = ask(pick_fields(n, per, share, branches, messages))
    turned, masks = turn(n, per, share, branches, counts, messages)
    other = {k: swap(x) for k, x in crossed.items()}
    earlier, begun = first_blocks(n, share, blocks[:-1], turned, asked)
    direct = {k: move(ordered(rows[:direct_rows], begun), k) for k in heads}
    green = make_green(n, share, blocks[n - 1], turned, asked, earlier, begun)
    crossed = along(crossed)
    other = along({k: ordered(x, green) for k, x in other.items()})
    [results] = contract(functools.partial(near_kernel, share, len(near), height), len(near), close, green)
    direct = along({k: ordered(x, results) for k, x in direct.items()})
    late, *kept = contract(
        functools.partial(shared_kernel, share, len(far), height),
        len(far),
        [crossed[k] for k in far] + [other[k] for k in far],
        ordered(green, results),
        kept_rows=direct_rows,
        scratch_rows=2 * shared_rows,
    )
    [late] = contract(
        functools.partial(direct_kernel, share, len(far)), len(far), [direct[k] for k in far], green, *kept, late
    )
    answers = [answer(late, far[0]), answer(ordered(results, late), 0)]
    arrived = [[x] + [move(x, k) for k in near[1:]] for x in reversed(answers)]
    return tuple(x.T for x in unpack(n, per, share, vectors, masks, [x for held in arrived for x in held]))


def newton_schulz(intersection):
    column_max = jnp.max(jnp.sum(jnp.abs(intersection), axis=0))
    row_max = jnp.max(jnp.sum(jnp.abs(intersection), axis=1))
    inverse = intersection.T / (column_max * row_max)
    twice_identity = 2.0 * jnp.eye(intersection.shape[0], dtype=intersection.dtype)
    for iteration in range(ITERS):
        inverse = jnp.dot(
            inverse,
            twice_identity - jnp.dot(intersection, inverse, precision=HIGHEST),
            precision=HIGHEST,
        )
    return inverse


def pick(array, indices):
    return jnp.concatenate(
        [lax.dynamic_slice_in_dim(array, indices[i], 1, 0) for i in range(indices.shape[0])], axis=0
    )


def at_the_target(walkers, trial_orbitals, cholesky, branches, counts, field):
    walk_size = lax.axis_size("walk")
    position = lax.axis_index("walk")
    per_device, row_count, electrons = walkers.shape
    capacity = (per_device + walk_size - 1) // walk_size
    sender = branches.reshape(walk_size, per_device) // per_device
    local_index = branches.reshape(walk_size, per_device) % per_device
    same_sender = sender[:, :, None] == sender[:, None, :]
    earlier = jnp.arange(per_device)[None, :] < jnp.arange(per_device)[:, None]
    arrival_rank = jnp.sum(same_sender & earlier[None], axis=2)
    wanted = (sender[:, None, :] == position) & (
        arrival_rank[:, None, :] == jnp.arange(capacity, dtype=jnp.int32)[None, :, None]
    )
    chosen = jnp.sum(jnp.where(wanted, local_index[:, None, :], 0), axis=2).reshape(-1)
    outgoing = pick(walkers, chosen).reshape(walk_size, capacity, row_count, electrons)
    arrived = lax.all_to_all(outgoing, "walk", split_axis=0, concat_axis=0, tiled=True)
    my_sender = lax.dynamic_index_in_dim(sender, position, 0, keepdims=False)
    my_rank = lax.dynamic_index_in_dim(arrival_rank, position, 0, keepdims=False)
    arrived_flat = arrived.reshape(walk_size * capacity, row_count, electrons)
    migrated = pick(arrived_flat, my_sender * capacity + my_rank)
    propagated = (migrated.astype(F32) * field[:, :, None]).astype(BF16)
    everything = lax.all_gather(propagated, SR, axis=1, tiled=True)
    shard_count = lax.axis_size(SR)
    share = per_device // shard_count
    trial_whole = lax.all_gather(trial_orbitals, SR, axis=0, tiled=True)
    own_walkers = lax.dynamic_slice_in_dim(everything, lax.axis_index(SR) * share, share, 0)
    intersection = jnp.einsum("mn,wmk->wnk", trial_whole, own_walkers, preferred_element_type=F32)
    inverse = jax.vmap(newton_schulz)(intersection).astype(BF16)
    inverses = lax.all_gather(inverse, SR, axis=0, tiled=True)
    green = jnp.einsum("wmn,wnk->wmk", everything, inverses, preferred_element_type=F32).astype(BF16)
    contracted = jnp.einsum("gnm,wmk->wgnk", cholesky, green, preferred_element_type=F32)
    living = (jnp.arange(per_device, dtype=jnp.int32) < counts[0]).astype(F32)[:, None]
    force_bias = jnp.trace(contracted, axis1=2, axis2=3) * living
    exchange_energy = -0.5 * jnp.einsum("wgnk,wgkn->wg", contracted, contracted) * living
    return (force_bias, exchange_energy)


def on_device(walkers, trial_orbitals, cholesky, branches, counts, field):
    walk_size, shard_count = lax.axis_size("walk"), lax.axis_size(SR)
    per = walkers.shape[0]
    if walk_size == shard_count and lax.axis_size("slab") == 2 and per % walk_size == 0 and not walk_size & (walk_size - 1):
        if cholesky.shape[0] * (per // walk_size) <= 4 and cholesky.shape[1] % 64 == 0 and per <= 128:
            return at_the_source(walkers, trial_orbitals, cholesky, branches, counts, field)
    return at_the_target(walkers, trial_orbitals, cholesky, branches, counts, field)


def solution(mesh):
    return jax.shard_map(
        on_device,
        mesh=mesh,
        in_specs=(
            P(("parts", "walk"), SR, None),
            P(("parts",) + SR, None),
            P(("parts",) + SR, None, None),
            P("parts"),
            P(("parts", "walk")),
            P(("parts", "walk"), SR),
        ),
        out_specs=(P(("parts", "walk"), SR), P(("parts", "walk"), SR)),
        check_vma=False,
    )
```

```python
import functools

import jax
import jax.numpy as jnp
from jax import lax
from jax.experimental import pallas as pl
from jax.experimental.pallas import tpu as pltpu
from jax.sharding import PartitionSpec as P

ITERS = 10
EARLY = 3
SR = ("slab", "row")
ALL = ("walk", "slab", "row")
F32 = jnp.float32
BF16 = jnp.bfloat16
VMEM_LIMIT = 24 * 2**20
SMALL_LIMIT = 2**20
AHEAD = pl.CostEstimate(flops=2**30, bytes_accessed=2**20, transcendentals=0)
HIGHEST = lax.Precision.HIGHEST


def dot(a, b, dims=((1,), (0,))):
    return lax.dot_general(a, b, (dims, ((), ())), preferred_element_type=F32)


def split(x):
    high = x.astype(BF16)
    return high, (x - high.astype(F32)).astype(BF16)


def place():
    return lax.axis_index("walk"), lax.axis_index("slab") * lax.axis_size("row") + lax.axis_index("row")


def whole(memory=pltpu.VMEM):
    return pl.BlockSpec(memory_space=memory)


def picks(branches, start, per, sender, share):
    places, olds = [jnp.int32(0)] * share, [jnp.int32(0)] * share
    rank = jnp.int32(0)
    for i in range(per):
        branch = branches[start + i]
        hit = lax.div(branch, per) == sender
        old = lax.rem(branch, per)
        for r in range(share):
            here = hit & (rank == r)
            places[r] = jnp.where(here, i, places[r])
            olds[r] = jnp.where(here, old, olds[r])
        rank = rank + hit.astype(jnp.int32)
    return places, olds


def select_kernel(n, per, share, branches, walkers, *refs):
    sends, sems = refs[:n], refs[n]
    walk, q = place()
    copies = []
    for k in list(range(1, n)) + [0]:
        olds = picks(branches, (q ^ k ^ walk) * per, per, walk, share)[1]
        for r in range(share):
            copies.append(pltpu.make_async_copy(walkers.at[olds[r]], sends[k].at[r], sems.at[k, r]))
            copies[-1].start()
    for copy in copies:
        copy.wait()


def select(n, per, share, branches, walkers):
    rows, electrons = walkers.shape[1:]
    return pl.pallas_call(
        functools.partial(select_kernel, n, per, share),
        out_shape=[jax.ShapeDtypeStruct((share, rows, electrons), walkers.dtype)] * n,
        in_specs=[whole(pltpu.SMEM), whole(pl.ANY)],
        out_specs=[whole(pl.ANY)] * n,
        scratch_shapes=[pltpu.SemaphoreType.DMA((n, share))],
        compiler_params=pltpu.CompilerParams(vmem_limit_bytes=SMALL_LIMIT),
        name="select",
    )(branches, walkers)


def message_kernel(trial, field, out):
    rows = trial.shape[0]
    out[:rows, :] = trial[...]
    rest, parts = field[...], []
    for _ in range(3):
        parts.append(rest.astype(BF16).astype(F32))
        rest = rest - parts[-1]
    spare = out.shape[0] - rows - 3 * field.shape[0]
    if spare:
        parts.append(jnp.zeros((spare, field.shape[1]), F32))
    out[rows:, :] = jnp.concatenate(parts, axis=0).astype(BF16)


def message(trial, field):
    height = trial.shape[0] + -(-3 * field.shape[0] // 16) * 16
    return pl.pallas_call(
        message_kernel,
        out_shape=jax.ShapeDtypeStruct((height, trial.shape[1]), trial.dtype),
        in_specs=[whole()] * 2,
        out_specs=whole(),
        compiler_params=pltpu.CompilerParams(vmem_limit_bytes=SMALL_LIMIT),
        name="message",
    )(trial, field)


def fields_kernel(n, per, share, branches, *refs):
    messages, fields = refs[:n], refs[n]
    walk, q = place()
    rows = fields.shape[2]
    places = picks(branches, walk * per, per, walk ^ q, share)[0]
    walker = lax.broadcasted_iota(jnp.int32, (per, rows), 0)
    for k in range(n):
        terms = messages[k][rows:, :].astype(F32)
        value = terms[:per] + terms[per : 2 * per] + terms[2 * per : 3 * per]
        chosen = [jnp.sum(jnp.where(walker == p, value, 0.0), axis=0, keepdims=True) for p in places]
        fields[pl.ds(q ^ k, 1), :, :] = jnp.concatenate(chosen, axis=0)[None]


def pick_fields(n, per, share, branches, messages):
    return pl.pallas_call(
        functools.partial(fields_kernel, n, per, share),
        out_shape=jax.ShapeDtypeStruct((n, share, messages[0].shape[1]), F32),
        in_specs=[whole(pltpu.SMEM)] + [whole()] * n,
        out_specs=whole(),
        compiler_params=pltpu.CompilerParams(vmem_limit_bytes=SMALL_LIMIT),
        name="fields",
    )(branches, *messages)


def turn_kernel(n, per, share, branches, counts, *refs):
    messages, turned, masks = refs[:n], refs[n], refs[n + 1]
    walk, q = place()
    rows = turned.shape[1] // n
    for k in range(n):
        turned[:, k * rows : (k + 1) * rows] = messages[k][:rows, :].T
    lane = lax.broadcasted_iota(jnp.int32, (1, 128), 1)
    for k in range(n):
        places = picks(branches, walk * per, per, walk ^ q ^ k, share)[0]
        for r in range(share):
            here = (lane == places[r]) & (places[r] < counts[0])
            masks[k * share + r : k * share + r + 1, :] = here.astype(F32)


def turn(n, per, share, branches, counts, messages):
    electrons = messages[0].shape[1]
    rows = n * (messages[0].shape[0] - -(-3 * per // 16) * 16)
    return pl.pallas_call(
        functools.partial(turn_kernel, n, per, share),
        out_shape=[
            jax.ShapeDtypeStruct((electrons, rows), messages[0].dtype),
            jax.ShapeDtypeStruct((n * share, 128), F32),
        ],
        in_specs=[whole(pltpu.SMEM)] * 2 + [whole()] * n,
        out_specs=[whole()] * 2,
        compiler_params=pltpu.CompilerParams(vmem_limit_bytes=SMALL_LIMIT),
        name="turn",
    )(branches, counts, *messages)


def squared(high, low):
    mixed = dot(high, low)
    return dot(high, high) + (mixed + mixed.T)


def propagate(share, k, block, fields, moved, start):
    q = place()[1]
    rows, electrons = block.shape[1:]
    lines = fields[pl.ds(q ^ k, 1), :, :].reshape(share, rows)
    if share % 8:
        lines = jnp.concatenate([lines, jnp.zeros((-share % 8, rows), F32)], axis=0)
    columns = lines.T
    for i in range(share):
        moved[start : start + rows, i * electrons : (i + 1) * electrons] = (
            block[i].astype(F32) * columns[:, i : i + 1]
        ).astype(BF16)


def first_kernel(n, share, *refs):
    blocks, turned, fields, moved, overlaps = refs[: n - 1], *refs[n - 1 :]
    rows = blocks[0].shape[1]
    for k in range(n - 1):
        propagate(share, k, blocks[k], fields, moved, k * rows)
    overlaps[...] = dot(turned[:, : (n - 1) * rows], moved[...])


def first_blocks(n, share, blocks, turned, fields):
    rows, electrons = blocks[0].shape[1:]
    return pl.pallas_call(
        functools.partial(first_kernel, n, share),
        out_shape=[
            jax.ShapeDtypeStruct(((n - 1) * rows, share * electrons), BF16),
            jax.ShapeDtypeStruct((electrons, share * electrons), F32),
        ],
        in_specs=[whole()] * (n + 1),
        out_specs=[whole()] * 2,
        compiler_params=pltpu.CompilerParams(vmem_limit_bytes=VMEM_LIMIT),
        cost_estimate=AHEAD,
        name="first",
    )(*blocks, turned, fields)


def green_kernel(n, share, *refs):
    block, turned, fields, earlier, begun = refs[:5]
    green, moved, left, right = refs[5:]
    q = place()[1]
    rows, electrons = block.shape[1:]
    propagate(share, n - 1, block, fields, moved, 0)
    overlaps = begun[...] + dot(turned[:, (n - 1) * rows :], moved[...])
    for i in range(share):
        overlap = overlaps[:, i * electrons : (i + 1) * electrons]
        size = jnp.abs(overlap)
        scale = jnp.max(jnp.sum(size, axis=0)) * jnp.max(jnp.sum(size, axis=1))
        left[i] = overlap.T / scale
        high, low = split(overlap)
        mixed = dot(high, low, ((1,), (1,)))
        right[i] = (dot(high, high, ((1,), (1,))) + (mixed + mixed.T)) / scale

    def advance(exact):
        for i in range(share):
            now, matrix = left[i], right[i]
            high, low = split(matrix)
            left_high, left_low = split(now)
            product = dot(left_high, high)
            if exact:
                product = product + (dot(left_high, low) + dot(left_low, high))
            left[i] = 2.0 * now - product
            right[i] = 2.0 * matrix - squared(high, low)

    for step in range(ITERS - 1):
        advance(step >= EARLY)
    for i in range(share):
        high, low = split(right[i])
        left_high, left_low = split(left[i])
        product = dot(left_high, high) + (dot(left_high, low) + dot(left_low, high))
        inverse = (2.0 * left[i] - product).astype(BF16)
        for k in range(n):
            at = pl.multiple_of((q ^ k) * rows, rows)
            held, start = (moved, 0) if k == n - 1 else (earlier, k * rows)
            green[pl.ds(at, rows), i * electrons : (i + 1) * electrons] = dot(
                held[start : start + rows, i * electrons : (i + 1) * electrons], inverse
            ).astype(BF16)


def make_green(n, share, block, turned, fields, earlier, begun):
    rows, electrons = block.shape[1:]
    return pl.pallas_call(
        functools.partial(green_kernel, n, share),
        out_shape=jax.ShapeDtypeStruct((n * rows, share * electrons), BF16),
        in_specs=[whole()] * 5,
        out_specs=whole(),
        scratch_shapes=[
            pltpu.VMEM((rows, share * electrons), BF16),
            pltpu.VMEM((share, electrons, electrons), F32),
            pltpu.VMEM((share, electrons, electrons), F32),
        ],
        compiler_params=pltpu.CompilerParams(vmem_limit_bytes=VMEM_LIMIT),
        name="green",
    )(block, turned, fields, earlier, begun)


def report(share, held, index, upper, lower):
    half = upper.shape[0]
    row = lax.broadcasted_iota(jnp.int32, (half, half), 0)
    column = lax.broadcasted_iota(jnp.int32, (half, half), 1)
    out_row = lax.broadcasted_iota(jnp.int32, held.shape, 0)
    for i in range(share):
        left, middle, right = 2 * i * half, (2 * i + 1) * half, 2 * (i + 1) * half
        a, b = upper[:, left:middle], upper[:, middle:right]
        c, d = lower[:, left:middle], lower[:, middle:right]
        trace = jnp.sum(jnp.where(row == column, a + d, 0.0))
        exchange = -0.5 * jnp.sum(a * a.T + d * d.T + 2.0 * (b * c.T))
        held = jnp.where(out_row == index * share + i, trace, held)
        held = jnp.where(out_row == held.shape[0] // 2 + index * share + i, exchange, held)
    return held


def near_kernel(share, count, height, *refs):
    vectors, green, outs = refs[:count], refs[count], refs[-1]
    for v in range(count):
        held = jnp.zeros(outs.shape[1:], F32)
        for g in range(vectors[v].shape[0] // height):
            full = dot(vectors[v][g * height : (g + 1) * height, :], green[...])
            held = report(share, held, g, full[: height // 2], full[height // 2 :])
        outs[v] = held


def shared_kernel(share, count, height, *refs):
    firsts, seconds, green = refs[:count], refs[count : 2 * count], refs[2 * count]
    outs, kept, both = refs[-count - 2], refs[-count - 1 : -1], refs[-1]
    parity = lax.axis_index("walk") & 1
    half = height // 2
    for v in range(count):
        rows = firsts[v].shape[0]
        for at, piece in ((parity, firsts[v]), (1 - parity, seconds[v])):
            both[pl.ds(pl.multiple_of(at * rows, 16), rows), :] = dot(piece[...], green[...])
        kept[v][...] = both[:half, :]
        held = jnp.zeros(outs.shape[1:], F32)
        for g in range(1, (2 * rows + half) // height):
            start = g * height - half
            held = report(share, held, g, both[start : start + half, :], both[start + half : start + height, :])
        outs[v] = held


def direct_kernel(share, count, *refs):
    uppers, green, kept = refs[:count], refs[count], refs[count + 1 : 2 * count + 1]
    before, near, outs, near_out = refs[-4:]
    near_out[...] = near[...]
    for v in range(count):
        outs[v] = report(share, before[v], 0, dot(uppers[v][...], green[...]), kept[v][...])


def contract(kernel, count, vectors, green, *more, kept_rows=0, scratch_rows=0, outs=1):
    wide = green.shape[1]
    kept = [jax.ShapeDtypeStruct((kept_rows, wide), F32)] * count if kept_rows else []
    return pl.pallas_call(
        kernel,
        out_shape=[jax.ShapeDtypeStruct((count, 8, 128), F32)] * outs + kept,
        in_specs=[whole()] * (len(vectors) + 1 + len(more)),
        out_specs=[whole()] * (outs + len(kept)),
        scratch_shapes=[pltpu.VMEM((scratch_rows, wide), F32)] if scratch_rows else [],
        compiler_params=pltpu.CompilerParams(vmem_limit_bytes=VMEM_LIMIT),
        cost_estimate=pl.CostEstimate(
            flops=sum(2 * v.size * wide for v in vectors),
            bytes_accessed=sum(2 * v.size for v in vectors) + 2 * green.size,
            transcendentals=0,
        ),
        name="contract",
    )(*vectors, green, *more)


def unpack_kernel(n, share, order, masks, *refs):
    arrived, outs = dict(zip(order, refs)), refs[n:]
    vectors, per = outs[0].shape
    for which, out in enumerate(outs):
        for g in range(vectors):
            line = jnp.zeros((1, 128), F32)
            for k in range(n):
                for r in range(share):
                    cores, height = arrived[k].shape[:2]
                    at = which * (height // 2) + g * share + r
                    value = arrived[k][k % cores, at : at + 1, :]
                    line = jnp.where(masks[k * share + r : k * share + r + 1, :] > 0.0, value, line)
            out[g : g + 1, :] = line[:, :per]


def unpack(n, per, share, vectors, order, masks, arrived):
    return pl.pallas_call(
        functools.partial(unpack_kernel, n, share, order),
        out_shape=[jax.ShapeDtypeStruct((vectors, per), F32)] * 2,
        in_specs=[whole()] * (1 + n),
        out_specs=[whole()] * 2,
        compiler_params=pltpu.CompilerParams(vmem_limit_bytes=SMALL_LIMIT),
        name="unpack",
    )(masks, *arrived)


def at_the_source(walkers, trial_orbitals, cholesky, branches, counts, field):
    n = lax.axis_size("walk")
    per = walkers.shape[0]
    share = per // n
    row_size = lax.axis_size("row")
    vectors = cholesky.shape[0]
    pairs = [(w, q) for w in range(n) for q in range(n)]
    move = lambda x, k: lax.ppermute(x, SR, [(i, i ^ k) for i in range(n)])
    swap = lambda x: lax.ppermute(x, "walk", [(w, w ^ 1) for w in range(n)])
    ask = lambda x: lax.ppermute(x, ALL, [(w * n + q, (w ^ q) * n + q) for w, q in pairs])
    answer = lambda x, k: lax.ppermute(x, ALL, [(w * n + q, (w ^ q) * n + (q ^ k)) for w, q in pairs])
    near = [k for k in range(n) if k < row_size]
    far = [k for k in range(n) if k >= row_size]

    def spread(x):
        held = {}
        for k in far:
            low = k & (row_size - 1)
            held[k] = move(held[k ^ low], low) if low else move(x, k)
        return held

    def along(held):
        return {k: move(held[k & ~(row_size - 1)], k & (row_size - 1)) if k & (row_size - 1) else held[k] for k in far}

    ordered = lambda x, *first: lax.optimization_barrier((x,) + first)[0]
    heads = [k for k in far if not k & (row_size - 1)]
    height = cholesky.shape[1]
    rows = cholesky.reshape(vectors * height, cholesky.shape[2])
    direct_rows = height // 2
    shared_rows = (rows.shape[0] - direct_rows) // 2
    at = direct_rows + (lax.axis_index("walk") & 1) * shared_rows
    shared = lax.dynamic_slice_in_dim(rows, at, shared_rows, 0)
    sends = select(n, per, share, branches, walkers)
    own = message(ordered(trial_orbitals, sends[0]), field)
    messages = {0: own, **spread(own)}
    messages.update({k: move(own, k) for k in near[1:]})
    messages = [messages[k] for k in range(n)]
    crossed = {k: move(shared, k) for k in heads}
    close = [rows] + [move(rows, k) for k in near[1:]]
    early = close[1:]
    blocks = [sends[0]] + [
        move(ordered(sends[k], *(crossed.values() if k == n - 1 else early)), k) for k in range(1, n)
    ]
    asked = ask(pick_fields(n, per, share, branches, messages))
    turned, masks = turn(n, per, share, branches, counts, messages)
    other = {k: swap(x) for k, x in crossed.items()}
    earlier, begun = first_blocks(n, share, blocks[:-1], turned, asked)
    direct = {k: move(ordered(rows[:direct_rows], begun), k) for k in heads}
    green = make_green(n, share, blocks[n - 1], turned, asked, earlier, begun)
    crossed = along(crossed)
    other = along({k: ordered(x, green) for k, x in other.items()})
    [results] = contract(functools.partial(near_kernel, share, len(near), height), len(near), close, green)
    direct = along({k: ordered(x, results) for k, x in direct.items()})
    late, *kept = contract(
        functools.partial(shared_kernel, share, len(far), height),
        len(far),
        [crossed[k] for k in far] + [other[k] for k in far],
        ordered(green, results),
        kept_rows=direct_rows,
        scratch_rows=2 * shared_rows,
    )
    late, results = contract(
        functools.partial(direct_kernel, share, len(far)), len(far), [direct[k] for k in far], green, *kept, late,
        results, outs=2,
    )
    answers = [answer(late, far[0]), answer(results, 0)]
    arrived = [[x] + [move(x, k) for k in near[1:]] for x in answers]
    return tuple(x.T for x in unpack(n, per, share, vectors, far + near, masks, [x for held in arrived for x in held]))


def newton_schulz(intersection):
    column_max = jnp.max(jnp.sum(jnp.abs(intersection), axis=0))
    row_max = jnp.max(jnp.sum(jnp.abs(intersection), axis=1))
    inverse = intersection.T / (column_max * row_max)
    twice_identity = 2.0 * jnp.eye(intersection.shape[0], dtype=intersection.dtype)
    for iteration in range(ITERS):
        inverse = jnp.dot(
            inverse,
            twice_identity - jnp.dot(intersection, inverse, precision=HIGHEST),
            precision=HIGHEST,
        )
    return inverse


def pick(array, indices):
    return jnp.concatenate(
        [lax.dynamic_slice_in_dim(array, indices[i], 1, 0) for i in range(indices.shape[0])], axis=0
    )


def at_the_target(walkers, trial_orbitals, cholesky, branches, counts, field):
    walk_size = lax.axis_size("walk")
    position = lax.axis_index("walk")
    per_device, row_count, electrons = walkers.shape
    capacity = (per_device + walk_size - 1) // walk_size
    sender = branches.reshape(walk_size, per_device) // per_device
    local_index = branches.reshape(walk_size, per_device) % per_device
    same_sender = sender[:, :, None] == sender[:, None, :]
    earlier = jnp.arange(per_device)[None, :] < jnp.arange(per_device)[:, None]
    arrival_rank = jnp.sum(same_sender & earlier[None], axis=2)
    wanted = (sender[:, None, :] == position) & (
        arrival_rank[:, None, :] == jnp.arange(capacity, dtype=jnp.int32)[None, :, None]
    )
    chosen = jnp.sum(jnp.where(wanted, local_index[:, None, :], 0), axis=2).reshape(-1)
    outgoing = pick(walkers, chosen).reshape(walk_size, capacity, row_count, electrons)
    arrived = lax.all_to_all(outgoing, "walk", split_axis=0, concat_axis=0, tiled=True)
    my_sender = lax.dynamic_index_in_dim(sender, position, 0, keepdims=False)
    my_rank = lax.dynamic_index_in_dim(arrival_rank, position, 0, keepdims=False)
    arrived_flat = arrived.reshape(walk_size * capacity, row_count, electrons)
    migrated = pick(arrived_flat, my_sender * capacity + my_rank)
    propagated = (migrated.astype(F32) * field[:, :, None]).astype(BF16)
    everything = lax.all_gather(propagated, SR, axis=1, tiled=True)
    shard_count = lax.axis_size(SR)
    share = per_device // shard_count
    trial_whole = lax.all_gather(trial_orbitals, SR, axis=0, tiled=True)
    own_walkers = lax.dynamic_slice_in_dim(everything, lax.axis_index(SR) * share, share, 0)
    intersection = jnp.einsum("mn,wmk->wnk", trial_whole, own_walkers, preferred_element_type=F32)
    inverse = jax.vmap(newton_schulz)(intersection).astype(BF16)
    inverses = lax.all_gather(inverse, SR, axis=0, tiled=True)
    green = jnp.einsum("wmn,wnk->wmk", everything, inverses, preferred_element_type=F32).astype(BF16)
    contracted = jnp.einsum("gnm,wmk->wgnk", cholesky, green, preferred_element_type=F32)
    living = (jnp.arange(per_device, dtype=jnp.int32) < counts[0]).astype(F32)[:, None]
    force_bias = jnp.trace(contracted, axis1=2, axis2=3) * living
    exchange_energy = -0.5 * jnp.einsum("wgnk,wgkn->wg", contracted, contracted) * living
    return (force_bias, exchange_energy)


def on_device(walkers, trial_orbitals, cholesky, branches, counts, field):
    walk_size, shard_count = lax.axis_size("walk"), lax.axis_size(SR)
    per = walkers.shape[0]
    if walk_size == shard_count and lax.axis_size("slab") == lax.axis_size("row") == 2 and per % walk_size == 0 and not walk_size & (walk_size - 1):
        if cholesky.shape[0] * (per // walk_size) <= 4 and cholesky.shape[1] % 64 == 0 and per <= 128:
            return at_the_source(walkers, trial_orbitals, cholesky, branches, counts, field)
    return at_the_target(walkers, trial_orbitals, cholesky, branches, counts, field)


def solution(mesh):
    return jax.shard_map(
        on_device,
        mesh=mesh,
        in_specs=(
            P(("parts", "walk"), SR, None),
            P(("parts",) + SR, None),
            P(("parts",) + SR, None, None),
            P("parts"),
            P(("parts", "walk")),
            P(("parts", "walk"), SR),
        ),
        out_specs=(P(("parts", "walk"), SR), P(("parts", "walk"), SR)),
        check_vma=False,
    )
```

```python
import functools

import jax
import jax.numpy as jnp
from jax import lax
from jax.experimental import pallas as pl
from jax.experimental.pallas import tpu as pltpu
from jax.sharding import PartitionSpec as P

ITERS = 10
EARLY = 3
SR = ("slab", "row")
ALL = ("walk", "slab", "row")
F32 = jnp.float32
BF16 = jnp.bfloat16
VMEM_LIMIT = 24 * 2**20
SMALL_LIMIT = 2**20
AHEAD = pl.CostEstimate(flops=2**30, bytes_accessed=2**20, transcendentals=0)
HIGHEST = lax.Precision.HIGHEST


def dot(a, b, dims=((1,), (0,))):
    return lax.dot_general(a, b, (dims, ((), ())), preferred_element_type=F32)


def split(x):
    high = x.astype(BF16)
    return high, (x - high.astype(F32)).astype(BF16)


def place():
    return lax.axis_index("walk"), lax.axis_index("slab") * lax.axis_size("row") + lax.axis_index("row")


def whole(memory=pltpu.VMEM):
    return pl.BlockSpec(memory_space=memory)


def picks(branches, start, per, sender, share):
    places, olds = [jnp.int32(0)] * share, [jnp.int32(0)] * share
    rank = jnp.int32(0)
    for i in range(per):
        branch = branches[start + i]
        hit = lax.div(branch, per) == sender
        old = lax.rem(branch, per)
        for r in range(share):
            here = hit & (rank == r)
            places[r] = jnp.where(here, i, places[r])
            olds[r] = jnp.where(here, old, olds[r])
        rank = rank + hit.astype(jnp.int32)
    return places, olds


def select_kernel(n, per, share, branches, walkers, *refs):
    sends, sems = refs[:n], refs[n]
    walk, q = place()
    copies = []
    for k in list(range(1, n)) + [0]:
        olds = picks(branches, (q ^ k ^ walk) * per, per, walk, share)[1]
        for r in range(share):
            copies.append(pltpu.make_async_copy(walkers.at[olds[r]], sends[k].at[r], sems.at[k, r]))
            copies[-1].start()
    for copy in copies:
        copy.wait()


def select(n, per, share, branches, walkers):
    rows, electrons = walkers.shape[1:]
    return pl.pallas_call(
        functools.partial(select_kernel, n, per, share),
        out_shape=[jax.ShapeDtypeStruct((share, rows, electrons), walkers.dtype)] * n,
        in_specs=[whole(pltpu.SMEM), whole(pl.ANY)],
        out_specs=[whole(pl.ANY)] * n,
        scratch_shapes=[pltpu.SemaphoreType.DMA((n, share))],
        compiler_params=pltpu.CompilerParams(vmem_limit_bytes=SMALL_LIMIT),
        name="select",
    )(branches, walkers)


def message_kernel(trial, field, out):
    rows = trial.shape[0]
    out[:rows, :] = trial[...]
    rest, parts = field[...], []
    for _ in range(3):
        parts.append(rest.astype(BF16).astype(F32))
        rest = rest - parts[-1]
    spare = out.shape[0] - rows - 3 * field.shape[0]
    if spare:
        parts.append(jnp.zeros((spare, field.shape[1]), F32))
    out[rows:, :] = jnp.concatenate(parts, axis=0).astype(BF16)


def message(trial, field):
    height = trial.shape[0] + -(-3 * field.shape[0] // 16) * 16
    return pl.pallas_call(
        message_kernel,
        out_shape=jax.ShapeDtypeStruct((height, trial.shape[1]), trial.dtype),
        in_specs=[whole()] * 2,
        out_specs=whole(),
        compiler_params=pltpu.CompilerParams(vmem_limit_bytes=SMALL_LIMIT),
        name="message",
    )(trial, field)


def fields_kernel(n, per, share, branches, *refs):
    messages, fields = refs[:n], refs[n]
    walk, q = place()
    rows = fields.shape[2]
    places = picks(branches, walk * per, per, walk ^ q, share)[0]
    walker = lax.broadcasted_iota(jnp.int32, (per, rows), 0)
    for k in range(n):
        terms = messages[k][rows:, :].astype(F32)
        value = terms[:per] + terms[per : 2 * per] + terms[2 * per : 3 * per]
        chosen = [jnp.sum(jnp.where(walker == p, value, 0.0), axis=0, keepdims=True) for p in places]
        fields[pl.ds(q ^ k, 1), :, :] = jnp.concatenate(chosen, axis=0)[None]


def pick_fields(n, per, share, branches, messages):
    return pl.pallas_call(
        functools.partial(fields_kernel, n, per, share),
        out_shape=jax.ShapeDtypeStruct((n, share, messages[0].shape[1]), F32),
        in_specs=[whole(pltpu.SMEM)] + [whole()] * n,
        out_specs=whole(),
        compiler_params=pltpu.CompilerParams(vmem_limit_bytes=SMALL_LIMIT),
        name="fields",
    )(branches, *messages)


def turn_kernel(n, per, share, branches, counts, *refs):
    messages, turned, masks = refs[:n], refs[n], refs[n + 1]
    walk, q = place()
    rows = turned.shape[1] // n
    for k in range(n):
        turned[:, k * rows : (k + 1) * rows] = messages[k][:rows, :].T
    lane = lax.broadcasted_iota(jnp.int32, (1, 128), 1)
    for k in range(n):
        places = picks(branches, walk * per, per, walk ^ q ^ k, share)[0]
        for r in range(share):
            here = (lane == places[r]) & (places[r] < counts[0])
            masks[k * share + r : k * share + r + 1, :] = here.astype(F32)


def turn(n, per, share, branches, counts, messages):
    electrons = messages[0].shape[1]
    rows = n * (messages[0].shape[0] - -(-3 * per // 16) * 16)
    return pl.pallas_call(
        functools.partial(turn_kernel, n, per, share),
        out_shape=[
            jax.ShapeDtypeStruct((electrons, rows), messages[0].dtype),
            jax.ShapeDtypeStruct((n * share, 128), F32),
        ],
        in_specs=[whole(pltpu.SMEM)] * 2 + [whole()] * n,
        out_specs=[whole()] * 2,
        compiler_params=pltpu.CompilerParams(vmem_limit_bytes=SMALL_LIMIT),
        name="turn",
    )(branches, counts, *messages)


def squared(high, low):
    mixed = dot(high, low)
    return dot(high, high) + (mixed + mixed.T)


def propagate(share, k, block, fields, moved, start):
    q = place()[1]
    rows, electrons = block.shape[1:]
    lines = fields[pl.ds(q ^ k, 1), :, :].reshape(share, rows)
    if share % 8:
        lines = jnp.concatenate([lines, jnp.zeros((-share % 8, rows), F32)], axis=0)
    columns = lines.T
    for i in range(share):
        moved[start : start + rows, i * electrons : (i + 1) * electrons] = (
            block[i].astype(F32) * columns[:, i : i + 1]
        ).astype(BF16)


def first_kernel(n, share, *refs):
    blocks, turned, fields, moved, overlaps = refs[: n - 1], *refs[n - 1 :]
    rows = blocks[0].shape[1]
    for k in range(n - 1):
        propagate(share, k, blocks[k], fields, moved, k * rows)
    overlaps[...] = dot(turned[:, : (n - 1) * rows], moved[...])


def first_blocks(n, share, blocks, turned, fields):
    rows, electrons = blocks[0].shape[1:]
    return pl.pallas_call(
        functools.partial(first_kernel, n, share),
        out_shape=[
            jax.ShapeDtypeStruct(((n - 1) * rows, share * electrons), BF16),
            jax.ShapeDtypeStruct((electrons, share * electrons), F32),
        ],
        in_specs=[whole()] * (n + 1),
        out_specs=[whole()] * 2,
        compiler_params=pltpu.CompilerParams(vmem_limit_bytes=VMEM_LIMIT),
        cost_estimate=AHEAD,
        name="first",
    )(*blocks, turned, fields)


def green_kernel(n, share, *refs):
    block, turned, fields, earlier, begun = refs[:5]
    green, moved, left, right = refs[5:]
    q = place()[1]
    rows, electrons = block.shape[1:]
    propagate(share, n - 1, block, fields, moved, 0)
    overlaps = begun[...] + dot(turned[:, (n - 1) * rows :], moved[...])
    for i in range(share):
        overlap = overlaps[:, i * electrons : (i + 1) * electrons]
        size = jnp.abs(overlap)
        scale = jnp.max(jnp.sum(size, axis=0)) * jnp.max(jnp.sum(size, axis=1))
        left[i] = overlap.T / scale
        high, low = split(overlap)
        mixed = dot(high, low, ((1,), (1,)))
        right[i] = (dot(high, high, ((1,), (1,))) + (mixed + mixed.T)) / scale

    def advance(exact):
        for i in range(share):
            now, matrix = left[i], right[i]
            high, low = split(matrix)
            left_high, left_low = split(now)
            product = dot(left_high, high)
            if exact:
                product = product + (dot(left_high, low) + dot(left_low, high))
            left[i] = 2.0 * now - product
            right[i] = 2.0 * matrix - squared(high, low)

    for step in range(ITERS - 1):
        advance(step >= EARLY)
    for i in range(share):
        high, low = split(right[i])
        left_high, left_low = split(left[i])
        product = dot(left_high, high) + (dot(left_high, low) + dot(left_low, high))
        inverse = (2.0 * left[i] - product).astype(BF16)
        for k in range(n):
            at = pl.multiple_of((q ^ k) * rows, rows)
            held, start = (moved, 0) if k == n - 1 else (earlier, k * rows)
            green[pl.ds(at, rows), i * electrons : (i + 1) * electrons] = dot(
                held[start : start + rows, i * electrons : (i + 1) * electrons], inverse
            ).astype(BF16)


def make_green(n, share, block, turned, fields, earlier, begun):
    rows, electrons = block.shape[1:]
    return pl.pallas_call(
        functools.partial(green_kernel, n, share),
        out_shape=jax.ShapeDtypeStruct((n * rows, share * electrons), BF16),
        in_specs=[whole()] * 5,
        out_specs=whole(),
        scratch_shapes=[
            pltpu.VMEM((rows, share * electrons), BF16),
            pltpu.VMEM((share, electrons, electrons), F32),
            pltpu.VMEM((share, electrons, electrons), F32),
        ],
        compiler_params=pltpu.CompilerParams(vmem_limit_bytes=VMEM_LIMIT),
        name="green",
    )(block, turned, fields, earlier, begun)


def report(share, held, index, upper, lower):
    half = upper.shape[0]
    row = lax.broadcasted_iota(jnp.int32, (half, half), 0)
    column = lax.broadcasted_iota(jnp.int32, (half, half), 1)
    out_row = lax.broadcasted_iota(jnp.int32, held.shape, 0)
    for i in range(share):
        left, middle, right = 2 * i * half, (2 * i + 1) * half, 2 * (i + 1) * half
        a, b = upper[:, left:middle], upper[:, middle:right]
        c, d = lower[:, left:middle], lower[:, middle:right]
        trace = jnp.sum(jnp.where(row == column, a + d, 0.0))
        exchange = -0.5 * jnp.sum(a * a.T + d * d.T + 2.0 * (b * c.T))
        held = jnp.where(out_row == index * share + i, trace, held)
        held = jnp.where(out_row == held.shape[0] // 2 + index * share + i, exchange, held)
    return held


def near_kernel(share, count, height, *refs):
    vectors, green, outs = refs[:count], refs[count], refs[-1]
    for v in range(count):
        held = jnp.zeros(outs.shape[1:], F32)
        for g in range(vectors[v].shape[0] // height):
            full = dot(vectors[v][g * height : (g + 1) * height, :], green[...])
            held = report(share, held, g, full[: height // 2], full[height // 2 :])
        outs[v] = held


def shared_kernel(share, count, height, *refs):
    firsts, seconds, green = refs[:count], refs[count : 2 * count], refs[2 * count]
    outs, kept, both = refs[-count - 2], refs[-count - 1 : -1], refs[-1]
    parity = lax.axis_index("walk") & 1
    half = height // 2
    for v in range(count):
        rows = firsts[v].shape[0]
        for at, piece in ((parity, firsts[v]), (1 - parity, seconds[v])):
            both[pl.ds(pl.multiple_of(at * rows, 16), rows), :] = dot(piece[...], green[...])
        kept[v][...] = both[:half, :]
        held = jnp.zeros(outs.shape[1:], F32)
        for g in range(1, (2 * rows + half) // height):
            start = g * height - half
            held = report(share, held, g, both[start : start + half, :], both[start + half : start + height, :])
        outs[v] = held


def direct_kernel(share, count, *refs):
    uppers, green, kept = refs[:count], refs[count], refs[count + 1 : 2 * count + 1]
    before, near, outs, near_out = refs[-4:]
    near_out[...] = near[...]
    for v in range(count):
        outs[v] = report(share, before[v], 0, dot(uppers[v][...], green[...]), kept[v][...])


def contract(kernel, count, vectors, green, *more, kept_rows=0, scratch_rows=0, outs=1):
    wide = green.shape[1]
    kept = [jax.ShapeDtypeStruct((kept_rows, wide), F32)] * count if kept_rows else []
    return pl.pallas_call(
        kernel,
        out_shape=[jax.ShapeDtypeStruct((count, 8, 128), F32)] * outs + kept,
        in_specs=[whole()] * (len(vectors) + 1 + len(more)),
        out_specs=[whole()] * (outs + len(kept)),
        scratch_shapes=[pltpu.VMEM((scratch_rows, wide), F32)] if scratch_rows else [],
        compiler_params=pltpu.CompilerParams(vmem_limit_bytes=VMEM_LIMIT),
        cost_estimate=pl.CostEstimate(
            flops=sum(2 * v.size * wide for v in vectors),
            bytes_accessed=sum(2 * v.size for v in vectors) + 2 * green.size,
            transcendentals=0,
        ),
        name="contract",
    )(*vectors, green, *more)


def unpack_kernel(n, share, order, masks, *refs):
    arrived, outs = dict(zip(order, refs)), refs[n:]
    vectors, per = outs[0].shape
    for which, out in enumerate(outs):
        for g in range(vectors):
            line = jnp.zeros((1, 128), F32)
            for k in range(n):
                for r in range(share):
                    cores, height = arrived[k].shape[:2]
                    at = which * (height // 2) + g * share + r
                    value = arrived[k][k % cores, at : at + 1, :]
                    line = jnp.where(masks[k * share + r : k * share + r + 1, :] > 0.0, value, line)
            out[g : g + 1, :] = line[:, :per]


def unpack(n, per, share, vectors, order, masks, arrived):
    return pl.pallas_call(
        functools.partial(unpack_kernel, n, share, order),
        out_shape=[jax.ShapeDtypeStruct((vectors, per), F32)] * 2,
        in_specs=[whole()] * (1 + n),
        out_specs=[whole()] * 2,
        compiler_params=pltpu.CompilerParams(vmem_limit_bytes=SMALL_LIMIT),
        name="unpack",
    )(masks, *arrived)


def at_the_source(walkers, trial_orbitals, cholesky, branches, counts, field):
    n = lax.axis_size("walk")
    per = walkers.shape[0]
    share = per // n
    row_size = lax.axis_size("row")
    vectors = cholesky.shape[0]
    pairs = [(w, q) for w in range(n) for q in range(n)]
    move = lambda x, k: lax.ppermute(x, SR, [(i, i ^ k) for i in range(n)])
    swap = lambda x: lax.ppermute(x, "walk", [(w, w ^ 1) for w in range(n)])
    ask = lambda x: lax.ppermute(x, ALL, [(w * n + q, (w ^ q) * n + q) for w, q in pairs])
    answer = lambda x, k: lax.ppermute(x, ALL, [(w * n + q, (w ^ q) * n + (q ^ k)) for w, q in pairs])
    near = [k for k in range(n) if k < row_size]
    far = [k for k in range(n) if k >= row_size]

    def spread(x):
        held = {}
        for k in far:
            low = k & (row_size - 1)
            held[k] = move(held[k ^ low], low) if low else move(x, k)
        return held

    def along(held):
        return {k: move(held[k & ~(row_size - 1)], k & (row_size - 1)) if k & (row_size - 1) else held[k] for k in far}

    ordered = lambda x, *first: lax.optimization_barrier((x,) + first)[0]
    heads = [k for k in far if not k & (row_size - 1)]
    height = cholesky.shape[1]
    rows = cholesky.reshape(vectors * height, cholesky.shape[2])
    direct_rows = height // 2
    shared_rows = (rows.shape[0] - direct_rows) // 2
    at = direct_rows + (lax.axis_index("walk") & 1) * shared_rows
    shared = lax.dynamic_slice_in_dim(rows, at, shared_rows, 0)
    sends = select(n, per, share, branches, walkers)
    own = message(ordered(trial_orbitals, sends[0]), field)
    messages = {0: own, **spread(own)}
    messages.update({k: move(own, k) for k in near[1:]})
    messages = [messages[k] for k in range(n)]
    crossed = {k: move(shared, k) for k in heads}
    close = [rows] + [move(rows, k) for k in near[1:]]
    early = close[1:]
    blocks = [sends[0]] + [
        move(ordered(sends[k], *(crossed.values() if k == n - 1 else early)), k) for k in range(1, n)
    ]
    asked = ask(pick_fields(n, per, share, branches, messages))
    turned, masks = turn(n, per, share, branches, counts, messages)
    other = {k: swap(x) for k, x in crossed.items()}
    earlier, begun = first_blocks(n, share, blocks[:-1], turned, asked)
    direct = {k: move(ordered(rows[:direct_rows], turned), k) for k in heads}
    green = make_green(n, share, blocks[n - 1], turned, asked, earlier, begun)
    crossed = along(crossed)
    other = along({k: ordered(x, green) for k, x in other.items()})
    [results] = contract(functools.partial(near_kernel, share, len(near), height), len(near), close, green)
    direct = along({k: ordered(x, results) for k, x in direct.items()})
    late, *kept = contract(
        functools.partial(shared_kernel, share, len(far), height),
        len(far),
        [crossed[k] for k in far] + [other[k] for k in far],
        ordered(green, results),
        kept_rows=direct_rows,
        scratch_rows=2 * shared_rows,
    )
    late, results = contract(
        functools.partial(direct_kernel, share, len(far)), len(far), [direct[k] for k in far], green, *kept, late,
        results, outs=2,
    )
    answers = [answer(late, far[0]), answer(results, 0)]
    arrived = [[x] + [move(x, k) for k in near[1:]] for x in answers]
    return tuple(x.T for x in unpack(n, per, share, vectors, far + near, masks, [x for held in arrived for x in held]))


def newton_schulz(intersection):
    column_max = jnp.max(jnp.sum(jnp.abs(intersection), axis=0))
    row_max = jnp.max(jnp.sum(jnp.abs(intersection), axis=1))
    inverse = intersection.T / (column_max * row_max)
    twice_identity = 2.0 * jnp.eye(intersection.shape[0], dtype=intersection.dtype)
    for iteration in range(ITERS):
        inverse = jnp.dot(
            inverse,
            twice_identity - jnp.dot(intersection, inverse, precision=HIGHEST),
            precision=HIGHEST,
        )
    return inverse


def pick(array, indices):
    return jnp.concatenate(
        [lax.dynamic_slice_in_dim(array, indices[i], 1, 0) for i in range(indices.shape[0])], axis=0
    )


def at_the_target(walkers, trial_orbitals, cholesky, branches, counts, field):
    walk_size = lax.axis_size("walk")
    position = lax.axis_index("walk")
    per_device, row_count, electrons = walkers.shape
    capacity = (per_device + walk_size - 1) // walk_size
    sender = branches.reshape(walk_size, per_device) // per_device
    local_index = branches.reshape(walk_size, per_device) % per_device
    same_sender = sender[:, :, None] == sender[:, None, :]
    earlier = jnp.arange(per_device)[None, :] < jnp.arange(per_device)[:, None]
    arrival_rank = jnp.sum(same_sender & earlier[None], axis=2)
    wanted = (sender[:, None, :] == position) & (
        arrival_rank[:, None, :] == jnp.arange(capacity, dtype=jnp.int32)[None, :, None]
    )
    chosen = jnp.sum(jnp.where(wanted, local_index[:, None, :], 0), axis=2).reshape(-1)
    outgoing = pick(walkers, chosen).reshape(walk_size, capacity, row_count, electrons)
    arrived = lax.all_to_all(outgoing, "walk", split_axis=0, concat_axis=0, tiled=True)
    my_sender = lax.dynamic_index_in_dim(sender, position, 0, keepdims=False)
    my_rank = lax.dynamic_index_in_dim(arrival_rank, position, 0, keepdims=False)
    arrived_flat = arrived.reshape(walk_size * capacity, row_count, electrons)
    migrated = pick(arrived_flat, my_sender * capacity + my_rank)
    propagated = (migrated.astype(F32) * field[:, :, None]).astype(BF16)
    everything = lax.all_gather(propagated, SR, axis=1, tiled=True)
    shard_count = lax.axis_size(SR)
    share = per_device // shard_count
    trial_whole = lax.all_gather(trial_orbitals, SR, axis=0, tiled=True)
    own_walkers = lax.dynamic_slice_in_dim(everything, lax.axis_index(SR) * share, share, 0)
    intersection = jnp.einsum("mn,wmk->wnk", trial_whole, own_walkers, preferred_element_type=F32)
    inverse = jax.vmap(newton_schulz)(intersection).astype(BF16)
    inverses = lax.all_gather(inverse, SR, axis=0, tiled=True)
    green = jnp.einsum("wmn,wnk->wmk", everything, inverses, preferred_element_type=F32).astype(BF16)
    contracted = jnp.einsum("gnm,wmk->wgnk", cholesky, green, preferred_element_type=F32)
    living = (jnp.arange(per_device, dtype=jnp.int32) < counts[0]).astype(F32)[:, None]
    force_bias = jnp.trace(contracted, axis1=2, axis2=3) * living
    exchange_energy = -0.5 * jnp.einsum("wgnk,wgkn->wg", contracted, contracted) * living
    return (force_bias, exchange_energy)


def on_device(walkers, trial_orbitals, cholesky, branches, counts, field):
    walk_size, shard_count = lax.axis_size("walk"), lax.axis_size(SR)
    per = walkers.shape[0]
    if walk_size == shard_count and lax.axis_size("slab") == lax.axis_size("row") == 2 and per % walk_size == 0 and not walk_size & (walk_size - 1):
        if cholesky.shape[0] * (per // walk_size) <= 4 and cholesky.shape[1] % 64 == 0 and per <= 128:
            return at_the_source(walkers, trial_orbitals, cholesky, branches, counts, field)
    return at_the_target(walkers, trial_orbitals, cholesky, branches, counts, field)


def solution(mesh):
    return jax.shard_map(
        on_device,
        mesh=mesh,
        in_specs=(
            P(("parts", "walk"), SR, None),
            P(("parts",) + SR, None),
            P(("parts",) + SR, None, None),
            P("parts"),
            P(("parts", "walk")),
            P(("parts", "walk"), SR),
        ),
        out_specs=(P(("parts", "walk"), SR), P(("parts", "walk"), SR)),
        check_vma=False,
    )
```

```python
import functools

import jax
import jax.numpy as jnp
from jax import lax
from jax.experimental import pallas as pl
from jax.experimental.pallas import tpu as pltpu
from jax.sharding import PartitionSpec as P

ITERS = 10
EARLY = 3
SR = ("slab", "row")
ALL = ("walk", "slab", "row")
F32 = jnp.float32
BF16 = jnp.bfloat16
VMEM_LIMIT = 24 * 2**20
SMALL_LIMIT = 2**20
AHEAD = pl.CostEstimate(flops=2**30, bytes_accessed=2**20, transcendentals=0)
HIGHEST = lax.Precision.HIGHEST


def dot(a, b, dims=((1,), (0,))):
    return lax.dot_general(a, b, (dims, ((), ())), preferred_element_type=F32)


def split(x):
    high = x.astype(BF16)
    return high, (x - high.astype(F32)).astype(BF16)


def place():
    return lax.axis_index("walk"), lax.axis_index("slab") * lax.axis_size("row") + lax.axis_index("row")


def whole(memory=pltpu.VMEM):
    return pl.BlockSpec(memory_space=memory)


def picks(branches, start, per, sender, share):
    places, olds = [jnp.int32(0)] * share, [jnp.int32(0)] * share
    rank = jnp.int32(0)
    for i in range(per):
        branch = branches[start + i]
        hit = lax.div(branch, per) == sender
        old = lax.rem(branch, per)
        for r in range(share):
            here = hit & (rank == r)
            places[r] = jnp.where(here, i, places[r])
            olds[r] = jnp.where(here, old, olds[r])
        rank = rank + hit.astype(jnp.int32)
    return places, olds


def select_kernel(n, per, share, branches, walkers, *refs):
    sends, sems = refs[:n], refs[n]
    walk, q = place()
    copies = []
    for k in list(range(1, n)) + [0]:
        olds = picks(branches, (q ^ k ^ walk) * per, per, walk, share)[1]
        for r in range(share):
            copies.append(pltpu.make_async_copy(walkers.at[olds[r]], sends[k].at[r], sems.at[k, r]))
            copies[-1].start()
    for copy in copies:
        copy.wait()


def select(n, per, share, branches, walkers):
    rows, electrons = walkers.shape[1:]
    return pl.pallas_call(
        functools.partial(select_kernel, n, per, share),
        out_shape=[jax.ShapeDtypeStruct((share, rows, electrons), walkers.dtype)] * n,
        in_specs=[whole(pltpu.SMEM), whole(pl.ANY)],
        out_specs=[whole(pl.ANY)] * n,
        scratch_shapes=[pltpu.SemaphoreType.DMA((n, share))],
        compiler_params=pltpu.CompilerParams(vmem_limit_bytes=SMALL_LIMIT),
        name="select",
    )(branches, walkers)


def message_kernel(trial, field, out):
    rows = trial.shape[0]
    out[:rows, :] = trial[...]
    rest, parts = field[...], []
    for _ in range(3):
        parts.append(rest.astype(BF16).astype(F32))
        rest = rest - parts[-1]
    spare = out.shape[0] - rows - 3 * field.shape[0]
    if spare:
        parts.append(jnp.zeros((spare, field.shape[1]), F32))
    out[rows:, :] = jnp.concatenate(parts, axis=0).astype(BF16)


def message(trial, field):
    height = trial.shape[0] + -(-3 * field.shape[0] // 16) * 16
    return pl.pallas_call(
        message_kernel,
        out_shape=jax.ShapeDtypeStruct((height, trial.shape[1]), trial.dtype),
        in_specs=[whole()] * 2,
        out_specs=whole(),
        compiler_params=pltpu.CompilerParams(vmem_limit_bytes=SMALL_LIMIT),
        name="message",
    )(trial, field)


def fields_kernel(n, per, share, branches, *refs):
    messages, fields = refs[:n], refs[n]
    walk, q = place()
    rows = fields.shape[2]
    places = picks(branches, walk * per, per, walk ^ q, share)[0]
    walker = lax.broadcasted_iota(jnp.int32, (per, rows), 0)
    for k in range(n):
        terms = messages[k][rows:, :].astype(F32)
        value = terms[:per] + terms[per : 2 * per] + terms[2 * per : 3 * per]
        chosen = [jnp.sum(jnp.where(walker == p, value, 0.0), axis=0, keepdims=True) for p in places]
        fields[pl.ds(q ^ k, 1), :, :] = jnp.concatenate(chosen, axis=0)[None]


def pick_fields(n, per, share, branches, messages):
    return pl.pallas_call(
        functools.partial(fields_kernel, n, per, share),
        out_shape=jax.ShapeDtypeStruct((n, share, messages[0].shape[1]), F32),
        in_specs=[whole(pltpu.SMEM)] + [whole()] * n,
        out_specs=whole(),
        compiler_params=pltpu.CompilerParams(vmem_limit_bytes=SMALL_LIMIT),
        name="fields",
    )(branches, *messages)


def turn_kernel(n, per, share, branches, counts, *refs):
    messages, turned, masks = refs[:n], refs[n], refs[n + 1]
    walk, q = place()
    rows = turned.shape[1] // n
    for k in range(n):
        turned[:, k * rows : (k + 1) * rows] = messages[k][:rows, :].T
    lane = lax.broadcasted_iota(jnp.int32, (1, 128), 1)
    for k in range(n):
        places = picks(branches, walk * per, per, walk ^ q ^ k, share)[0]
        for r in range(share):
            here = (lane == places[r]) & (places[r] < counts[0])
            masks[k * share + r : k * share + r + 1, :] = here.astype(F32)


def turn(n, per, share, branches, counts, messages):
    electrons = messages[0].shape[1]
    rows = n * (messages[0].shape[0] - -(-3 * per // 16) * 16)
    return pl.pallas_call(
        functools.partial(turn_kernel, n, per, share),
        out_shape=[
            jax.ShapeDtypeStruct((electrons, rows), messages[0].dtype),
            jax.ShapeDtypeStruct((n * share, 128), F32),
        ],
        in_specs=[whole(pltpu.SMEM)] * 2 + [whole()] * n,
        out_specs=[whole()] * 2,
        compiler_params=pltpu.CompilerParams(vmem_limit_bytes=SMALL_LIMIT),
        name="turn",
    )(branches, counts, *messages)


def squared(high, low):
    mixed = dot(high, low)
    return dot(high, high) + (mixed + mixed.T)


def propagate(share, k, block, fields, moved, start):
    q = place()[1]
    rows, electrons = block.shape[1:]
    lines = fields[pl.ds(q ^ k, 1), :, :].reshape(share, rows)
    if share % 8:
        lines = jnp.concatenate([lines, jnp.zeros((-share % 8, rows), F32)], axis=0)
    columns = lines.T
    for i in range(share):
        moved[start : start + rows, i * electrons : (i + 1) * electrons] = (
            block[i].astype(F32) * columns[:, i : i + 1]
        ).astype(BF16)


def first_kernel(n, share, *refs):
    blocks, turned, fields, moved, overlaps = refs[: n - 1], *refs[n - 1 :]
    rows = blocks[0].shape[1]
    for k in range(n - 1):
        propagate(share, k, blocks[k], fields, moved, k * rows)
    overlaps[...] = dot(turned[:, : (n - 1) * rows], moved[...])


def first_blocks(n, share, blocks, turned, fields):
    rows, electrons = blocks[0].shape[1:]
    return pl.pallas_call(
        functools.partial(first_kernel, n, share),
        out_shape=[
            jax.ShapeDtypeStruct(((n - 1) * rows, share * electrons), BF16),
            jax.ShapeDtypeStruct((electrons, share * electrons), F32),
        ],
        in_specs=[whole()] * (n + 1),
        out_specs=[whole()] * 2,
        compiler_params=pltpu.CompilerParams(vmem_limit_bytes=VMEM_LIMIT),
        cost_estimate=AHEAD,
        name="first",
    )(*blocks, turned, fields)


def green_kernel(n, share, *refs):
    block, turned, fields, earlier, begun = refs[:5]
    green, moved, left, right = refs[5:]
    q = place()[1]
    rows, electrons = block.shape[1:]
    propagate(share, n - 1, block, fields, moved, 0)
    overlaps = begun[...] + dot(turned[:, (n - 1) * rows :], moved[...])
    for i in range(share):
        overlap = overlaps[:, i * electrons : (i + 1) * electrons]
        size = jnp.abs(overlap)
        scale = jnp.max(jnp.sum(size, axis=0)) * jnp.max(jnp.sum(size, axis=1))
        left[i] = overlap.T / scale
        high, low = split(overlap)
        mixed = dot(high, low, ((1,), (1,)))
        right[i] = (dot(high, high, ((1,), (1,))) + (mixed + mixed.T)) / scale

    def advance(exact):
        for i in range(share):
            now, matrix = left[i], right[i]
            high, low = split(matrix)
            left_high, left_low = split(now)
            product = dot(left_high, high)
            if exact:
                product = product + (dot(left_high, low) + dot(left_low, high))
            left[i] = 2.0 * now - product
            right[i] = 2.0 * matrix - squared(high, low)

    for step in range(ITERS - 1):
        advance(step >= EARLY)
    for i in range(share):
        high, low = split(right[i])
        left_high, left_low = split(left[i])
        product = dot(left_high, high) + (dot(left_high, low) + dot(left_low, high))
        inverse = (2.0 * left[i] - product).astype(BF16)
        for k in range(n):
            at = pl.multiple_of((q ^ k) * rows, rows)
            held, start = (moved, 0) if k == n - 1 else (earlier, k * rows)
            green[pl.ds(at, rows), i * electrons : (i + 1) * electrons] = dot(
                held[start : start + rows, i * electrons : (i + 1) * electrons], inverse
            ).astype(BF16)


def make_green(n, share, block, turned, fields, earlier, begun):
    rows, electrons = block.shape[1:]
    return pl.pallas_call(
        functools.partial(green_kernel, n, share),
        out_shape=jax.ShapeDtypeStruct((n * rows, share * electrons), BF16),
        in_specs=[whole()] * 5,
        out_specs=whole(),
        scratch_shapes=[
            pltpu.VMEM((rows, share * electrons), BF16),
            pltpu.VMEM((share, electrons, electrons), F32),
            pltpu.VMEM((share, electrons, electrons), F32),
        ],
        compiler_params=pltpu.CompilerParams(vmem_limit_bytes=VMEM_LIMIT),
        name="green",
    )(block, turned, fields, earlier, begun)


def report(share, held, index, upper, lower):
    half = upper.shape[0]
    row = lax.broadcasted_iota(jnp.int32, (half, half), 0)
    column = lax.broadcasted_iota(jnp.int32, (half, half), 1)
    out_row = lax.broadcasted_iota(jnp.int32, held.shape, 0)
    for i in range(share):
        left, middle, right = 2 * i * half, (2 * i + 1) * half, 2 * (i + 1) * half
        a, b = upper[:, left:middle], upper[:, middle:right]
        c, d = lower[:, left:middle], lower[:, middle:right]
        trace = jnp.sum(jnp.where(row == column, a + d, 0.0))
        exchange = -0.5 * jnp.sum(a * a.T + d * d.T + 2.0 * (b * c.T))
        held = jnp.where(out_row == index * share + i, trace, held)
        held = jnp.where(out_row == held.shape[0] // 2 + index * share + i, exchange, held)
    return held


def near_kernel(share, count, height, *refs):
    vectors, green, outs = refs[:count], refs[count], refs[-1]
    for v in range(count):
        held = jnp.zeros(outs.shape[1:], F32)
        for g in range(vectors[v].shape[0] // height):
            full = dot(vectors[v][g * height : (g + 1) * height, :], green[...])
            held = report(share, held, g, full[: height // 2], full[height // 2 :])
        outs[v] = held


def shared_kernel(share, count, height, *refs):
    firsts, seconds, green = refs[:count], refs[count : 2 * count], refs[2 * count]
    outs, kept, both = refs[-count - 2], refs[-count - 1 : -1], refs[-1]
    parity = lax.axis_index("walk") & 1
    half = height // 2
    for v in range(count):
        rows = firsts[v].shape[0]
        for at, piece in ((parity, firsts[v]), (1 - parity, seconds[v])):
            both[pl.ds(pl.multiple_of(at * rows, 16), rows), :] = dot(piece[...], green[...])
        kept[v][...] = both[:half, :]
        held = jnp.zeros(outs.shape[1:], F32)
        for g in range(1, (2 * rows + half) // height):
            start = g * height - half
            held = report(share, held, g, both[start : start + half, :], both[start + half : start + height, :])
        outs[v] = held


def direct_kernel(share, count, *refs):
    uppers, green, kept = refs[:count], refs[count], refs[count + 1 : 2 * count + 1]
    before, near, outs, near_out = refs[-4:]
    near_out[...] = near[...]
    for v in range(count):
        outs[v] = report(share, before[v], 0, dot(uppers[v][...], green[...]), kept[v][...])


def contract(kernel, count, vectors, green, *more, kept_rows=0, scratch_rows=0, outs=1):
    wide = green.shape[1]
    kept = [jax.ShapeDtypeStruct((kept_rows, wide), F32)] * count if kept_rows else []
    return pl.pallas_call(
        kernel,
        out_shape=[jax.ShapeDtypeStruct((count, 8, 128), F32)] * outs + kept,
        in_specs=[whole()] * (len(vectors) + 1 + len(more)),
        out_specs=[whole()] * (outs + len(kept)),
        scratch_shapes=[pltpu.VMEM((scratch_rows, wide), F32)] if scratch_rows else [],
        compiler_params=pltpu.CompilerParams(vmem_limit_bytes=VMEM_LIMIT),
        cost_estimate=pl.CostEstimate(
            flops=sum(2 * v.size * wide for v in vectors),
            bytes_accessed=sum(2 * v.size for v in vectors) + 2 * green.size,
            transcendentals=0,
        ),
        name="contract",
    )(*vectors, green, *more)


def unpack_kernel(n, share, order, masks, *refs):
    arrived, outs = dict(zip(order, refs)), refs[n:]
    vectors, per = outs[0].shape
    for which, out in enumerate(outs):
        for g in range(vectors):
            line = jnp.zeros((1, 128), F32)
            for k in range(n):
                for r in range(share):
                    cores, height = arrived[k].shape[:2]
                    at = which * (height // 2) + g * share + r
                    value = arrived[k][k % cores, at : at + 1, :]
                    line = jnp.where(masks[k * share + r : k * share + r + 1, :] > 0.0, value, line)
            out[g : g + 1, :] = line[:, :per]


def unpack(n, per, share, vectors, order, masks, arrived):
    return pl.pallas_call(
        functools.partial(unpack_kernel, n, share, order),
        out_shape=[jax.ShapeDtypeStruct((vectors, per), F32)] * 2,
        in_specs=[whole()] * (1 + n),
        out_specs=[whole()] * 2,
        compiler_params=pltpu.CompilerParams(vmem_limit_bytes=SMALL_LIMIT),
        name="unpack",
    )(masks, *arrived)


def at_the_source(walkers, trial_orbitals, cholesky, branches, counts, field):
    n = lax.axis_size("walk")
    per = walkers.shape[0]
    share = per // n
    row_size = lax.axis_size("row")
    vectors = cholesky.shape[0]
    pairs = [(w, q) for w in range(n) for q in range(n)]
    move = lambda x, k: lax.ppermute(x, SR, [(i, i ^ k) for i in range(n)])
    swap = lambda x: lax.ppermute(x, "walk", [(w, w ^ 1) for w in range(n)])
    ask = lambda x: lax.ppermute(x, ALL, [(w * n + q, (w ^ q) * n + q) for w, q in pairs])
    answer = lambda x, k: lax.ppermute(x, ALL, [(w * n + q, (w ^ q) * n + (q ^ k)) for w, q in pairs])
    near = [k for k in range(n) if k < row_size]
    far = [k for k in range(n) if k >= row_size]

    def spread(x):
        held = {}
        for k in far:
            low = k & (row_size - 1)
            held[k] = move(held[k ^ low], low) if low else move(x, k)
        return held

    def along(held):
        return {k: move(held[k & ~(row_size - 1)], k & (row_size - 1)) if k & (row_size - 1) else held[k] for k in far}

    ordered = lambda x, *first: lax.optimization_barrier((x,) + first)[0]
    heads = [k for k in far if not k & (row_size - 1)]
    height = cholesky.shape[1]
    rows = cholesky.reshape(vectors * height, cholesky.shape[2])
    direct_rows = height // 2
    shared_rows = (rows.shape[0] - direct_rows) // 2
    at = direct_rows + (lax.axis_index("walk") & 1) * shared_rows
    shared = lax.dynamic_slice_in_dim(rows, at, shared_rows, 0)
    sends = select(n, per, share, branches, walkers)
    own = message(ordered(trial_orbitals, sends[0]), field)
    messages = {0: own, **spread(own)}
    messages.update({k: move(own, k) for k in near[1:]})
    messages = [messages[k] for k in range(n)]
    crossed = {k: move(shared, k) for k in heads}
    close = [rows] + [move(rows, k) for k in near[1:]]
    early = close[1:]
    blocks = [sends[0]] + [
        move(ordered(sends[k], *(crossed.values() if k == n - 1 else early)), k) for k in range(1, n)
    ]
    asked = ask(pick_fields(n, per, share, branches, messages))
    turned, masks = turn(n, per, share, branches, counts, messages)
    other = {k: swap(x) for k, x in crossed.items()}
    earlier, begun = first_blocks(n, share, blocks[:-1], turned, asked)
    direct = {k: move(ordered(rows[:direct_rows], begun), k) for k in heads}
    green = make_green(n, share, blocks[n - 1], turned, asked, earlier, begun)
    crossed = along(crossed)
    other = along({k: ordered(x, green) for k, x in other.items()})
    [results] = contract(functools.partial(near_kernel, share, len(near), height), len(near), close, green)
    direct = along({k: ordered(x, results) for k, x in direct.items()})
    late, *kept = contract(
        functools.partial(shared_kernel, share, len(far), height),
        len(far),
        [crossed[k] for k in far] + [other[k] for k in far],
        ordered(green, results),
        kept_rows=direct_rows,
        scratch_rows=2 * shared_rows,
    )
    late, results = contract(
        functools.partial(direct_kernel, share, len(far)), len(far), [direct[k] for k in far], green, *kept, late,
        results, outs=2,
    )
    answers = [answer(late, far[0]), answer(results, 0)]
    arrived = [[answer(late, k) for k in far], [answers[1]] + [move(answers[1], k) for k in near[1:]]]
    return tuple(x.T for x in unpack(n, per, share, vectors, far + near, masks, [x for held in arrived for x in held]))


def newton_schulz(intersection):
    column_max = jnp.max(jnp.sum(jnp.abs(intersection), axis=0))
    row_max = jnp.max(jnp.sum(jnp.abs(intersection), axis=1))
    inverse = intersection.T / (column_max * row_max)
    twice_identity = 2.0 * jnp.eye(intersection.shape[0], dtype=intersection.dtype)
    for iteration in range(ITERS):
        inverse = jnp.dot(
            inverse,
            twice_identity - jnp.dot(intersection, inverse, precision=HIGHEST),
            precision=HIGHEST,
        )
    return inverse


def pick(array, indices):
    return jnp.concatenate(
        [lax.dynamic_slice_in_dim(array, indices[i], 1, 0) for i in range(indices.shape[0])], axis=0
    )


def at_the_target(walkers, trial_orbitals, cholesky, branches, counts, field):
    walk_size = lax.axis_size("walk")
    position = lax.axis_index("walk")
    per_device, row_count, electrons = walkers.shape
    capacity = (per_device + walk_size - 1) // walk_size
    sender = branches.reshape(walk_size, per_device) // per_device
    local_index = branches.reshape(walk_size, per_device) % per_device
    same_sender = sender[:, :, None] == sender[:, None, :]
    earlier = jnp.arange(per_device)[None, :] < jnp.arange(per_device)[:, None]
    arrival_rank = jnp.sum(same_sender & earlier[None], axis=2)
    wanted = (sender[:, None, :] == position) & (
        arrival_rank[:, None, :] == jnp.arange(capacity, dtype=jnp.int32)[None, :, None]
    )
    chosen = jnp.sum(jnp.where(wanted, local_index[:, None, :], 0), axis=2).reshape(-1)
    outgoing = pick(walkers, chosen).reshape(walk_size, capacity, row_count, electrons)
    arrived = lax.all_to_all(outgoing, "walk", split_axis=0, concat_axis=0, tiled=True)
    my_sender = lax.dynamic_index_in_dim(sender, position, 0, keepdims=False)
    my_rank = lax.dynamic_index_in_dim(arrival_rank, position, 0, keepdims=False)
    arrived_flat = arrived.reshape(walk_size * capacity, row_count, electrons)
    migrated = pick(arrived_flat, my_sender * capacity + my_rank)
    propagated = (migrated.astype(F32) * field[:, :, None]).astype(BF16)
    everything = lax.all_gather(propagated, SR, axis=1, tiled=True)
    shard_count = lax.axis_size(SR)
    share = per_device // shard_count
    trial_whole = lax.all_gather(trial_orbitals, SR, axis=0, tiled=True)
    own_walkers = lax.dynamic_slice_in_dim(everything, lax.axis_index(SR) * share, share, 0)
    intersection = jnp.einsum("mn,wmk->wnk", trial_whole, own_walkers, preferred_element_type=F32)
    inverse = jax.vmap(newton_schulz)(intersection).astype(BF16)
    inverses = lax.all_gather(inverse, SR, axis=0, tiled=True)
    green = jnp.einsum("wmn,wnk->wmk", everything, inverses, preferred_element_type=F32).astype(BF16)
    contracted = jnp.einsum("gnm,wmk->wgnk", cholesky, green, preferred_element_type=F32)
    living = (jnp.arange(per_device, dtype=jnp.int32) < counts[0]).astype(F32)[:, None]
    force_bias = jnp.trace(contracted, axis1=2, axis2=3) * living
    exchange_energy = -0.5 * jnp.einsum("wgnk,wgkn->wg", contracted, contracted) * living
    return (force_bias, exchange_energy)


def on_device(walkers, trial_orbitals, cholesky, branches, counts, field):
    walk_size, shard_count = lax.axis_size("walk"), lax.axis_size(SR)
    per = walkers.shape[0]
    if walk_size == shard_count and lax.axis_size("slab") == lax.axis_size("row") == 2 and per % walk_size == 0 and not walk_size & (walk_size - 1):
        if cholesky.shape[0] * (per // walk_size) <= 4 and cholesky.shape[1] % 64 == 0 and per <= 128:
            return at_the_source(walkers, trial_orbitals, cholesky, branches, counts, field)
    return at_the_target(walkers, trial_orbitals, cholesky, branches, counts, field)


def solution(mesh):
    return jax.shard_map(
        on_device,
        mesh=mesh,
        in_specs=(
            P(("parts", "walk"), SR, None),
            P(("parts",) + SR, None),
            P(("parts",) + SR, None, None),
            P("parts"),
            P(("parts", "walk")),
            P(("parts", "walk"), SR),
        ),
        out_specs=(P(("parts", "walk"), SR), P(("parts", "walk"), SR)),
        check_vma=False,
    )
```

```python
import functools

import jax
import jax.numpy as jnp
from jax import lax
from jax.experimental import pallas as pl
from jax.experimental.pallas import tpu as pltpu
from jax.sharding import PartitionSpec as P

ITERS = 10
EARLY = 4
SR = ("slab", "row")
ALL = ("walk", "slab", "row")
F32 = jnp.float32
BF16 = jnp.bfloat16
VMEM_LIMIT = 24 * 2**20
SMALL_LIMIT = 2**20
AHEAD = pl.CostEstimate(flops=2**30, bytes_accessed=2**20, transcendentals=0)
HIGHEST = lax.Precision.HIGHEST


def dot(a, b, dims=((1,), (0,))):
    return lax.dot_general(a, b, (dims, ((), ())), preferred_element_type=F32)


def split(x):
    high = x.astype(BF16)
    return high, (x - high.astype(F32)).astype(BF16)


def place():
    return lax.axis_index("walk"), lax.axis_index("slab") * lax.axis_size("row") + lax.axis_index("row")


def whole(memory=pltpu.VMEM):
    return pl.BlockSpec(memory_space=memory)


def picks(branches, start, per, sender, share):
    places, olds = [jnp.int32(0)] * share, [jnp.int32(0)] * share
    rank = jnp.int32(0)
    for i in range(per):
        branch = branches[start + i]
        hit = lax.div(branch, per) == sender
        old = lax.rem(branch, per)
        for r in range(share):
            here = hit & (rank == r)
            places[r] = jnp.where(here, i, places[r])
            olds[r] = jnp.where(here, old, olds[r])
        rank = rank + hit.astype(jnp.int32)
    return places, olds


def select_kernel(n, per, share, branches, walkers, *refs):
    sends, sems = refs[:n], refs[n]
    walk, q = place()
    copies = []
    for k in list(range(1, n)) + [0]:
        olds = picks(branches, (q ^ k ^ walk) * per, per, walk, share)[1]
        for r in range(share):
            copies.append(pltpu.make_async_copy(walkers.at[olds[r]], sends[k].at[r], sems.at[k, r]))
            copies[-1].start()
    for copy in copies:
        copy.wait()


def select(n, per, share, branches, walkers):
    rows, electrons = walkers.shape[1:]
    return pl.pallas_call(
        functools.partial(select_kernel, n, per, share),
        out_shape=[jax.ShapeDtypeStruct((share, rows, electrons), walkers.dtype)] * n,
        in_specs=[whole(pltpu.SMEM), whole(pl.ANY)],
        out_specs=[whole(pl.ANY)] * n,
        scratch_shapes=[pltpu.SemaphoreType.DMA((n, share))],
        compiler_params=pltpu.CompilerParams(vmem_limit_bytes=SMALL_LIMIT),
        name="select",
    )(branches, walkers)


def message_kernel(trial, field, out):
    rows = trial.shape[0]
    out[:rows, :] = trial[...]
    rest, parts = field[...], []
    for _ in range(3):
        parts.append(rest.astype(BF16).astype(F32))
        rest = rest - parts[-1]
    spare = out.shape[0] - rows - 3 * field.shape[0]
    if spare:
        parts.append(jnp.zeros((spare, field.shape[1]), F32))
    out[rows:, :] = jnp.concatenate(parts, axis=0).astype(BF16)


def message(trial, field):
    height = trial.shape[0] + -(-3 * field.shape[0] // 16) * 16
    return pl.pallas_call(
        message_kernel,
        out_shape=jax.ShapeDtypeStruct((height, trial.shape[1]), trial.dtype),
        in_specs=[whole()] * 2,
        out_specs=whole(),
        compiler_params=pltpu.CompilerParams(vmem_limit_bytes=SMALL_LIMIT),
        name="message",
    )(trial, field)


def fields_kernel(n, per, share, branches, *refs):
    messages, fields = refs[:n], refs[n]
    walk, q = place()
    rows = fields.shape[2]
    places = picks(branches, walk * per, per, walk ^ q, share)[0]
    walker = lax.broadcasted_iota(jnp.int32, (per, rows), 0)
    for k in range(n):
        terms = messages[k][rows:, :].astype(F32)
        value = terms[:per] + terms[per : 2 * per] + terms[2 * per : 3 * per]
        chosen = [jnp.sum(jnp.where(walker == p, value, 0.0), axis=0, keepdims=True) for p in places]
        fields[pl.ds(q ^ k, 1), :, :] = jnp.concatenate(chosen, axis=0)[None]


def pick_fields(n, per, share, branches, messages):
    return pl.pallas_call(
        functools.partial(fields_kernel, n, per, share),
        out_shape=jax.ShapeDtypeStruct((n, share, messages[0].shape[1]), F32),
        in_specs=[whole(pltpu.SMEM)] + [whole()] * n,
        out_specs=whole(),
        compiler_params=pltpu.CompilerParams(vmem_limit_bytes=SMALL_LIMIT),
        name="fields",
    )(branches, *messages)


def turn_kernel(n, per, share, branches, counts, *refs):
    messages, turned, masks = refs[:n], refs[n], refs[n + 1]
    walk, q = place()
    rows = turned.shape[1] // n
    for k in range(n):
        turned[:, k * rows : (k + 1) * rows] = messages[k][:rows, :].T
    lane = lax.broadcasted_iota(jnp.int32, (1, 128), 1)
    for k in range(n):
        places = picks(branches, walk * per, per, walk ^ q ^ k, share)[0]
        for r in range(share):
            here = (lane == places[r]) & (places[r] < counts[0])
            masks[k * share + r : k * share + r + 1, :] = here.astype(F32)


def turn(n, per, share, branches, counts, messages):
    electrons = messages[0].shape[1]
    rows = n * (messages[0].shape[0] - -(-3 * per // 16) * 16)
    return pl.pallas_call(
        functools.partial(turn_kernel, n, per, share),
        out_shape=[
            jax.ShapeDtypeStruct((electrons, rows), messages[0].dtype),
            jax.ShapeDtypeStruct((n * share, 128), F32),
        ],
        in_specs=[whole(pltpu.SMEM)] * 2 + [whole()] * n,
        out_specs=[whole()] * 2,
        compiler_params=pltpu.CompilerParams(vmem_limit_bytes=SMALL_LIMIT),
        name="turn",
    )(branches, counts, *messages)


def squared(high, low):
    mixed = dot(high, low)
    return dot(high, high) + (mixed + mixed.T)


def propagate(share, k, block, fields, moved, start):
    q = place()[1]
    rows, electrons = block.shape[1:]
    lines = fields[pl.ds(q ^ k, 1), :, :].reshape(share, rows)
    if share % 8:
        lines = jnp.concatenate([lines, jnp.zeros((-share % 8, rows), F32)], axis=0)
    columns = lines.T
    for i in range(share):
        moved[start : start + rows, i * electrons : (i + 1) * electrons] = (
            block[i].astype(F32) * columns[:, i : i + 1]
        ).astype(BF16)


def first_kernel(n, share, *refs):
    blocks, turned, fields, moved, overlaps = refs[: n - 1], *refs[n - 1 :]
    rows = blocks[0].shape[1]
    for k in range(n - 1):
        propagate(share, k, blocks[k], fields, moved, k * rows)
    overlaps[...] = dot(turned[:, : (n - 1) * rows], moved[...])


def first_blocks(n, share, blocks, turned, fields):
    rows, electrons = blocks[0].shape[1:]
    return pl.pallas_call(
        functools.partial(first_kernel, n, share),
        out_shape=[
            jax.ShapeDtypeStruct(((n - 1) * rows, share * electrons), BF16),
            jax.ShapeDtypeStruct((electrons, share * electrons), F32),
        ],
        in_specs=[whole()] * (n + 1),
        out_specs=[whole()] * 2,
        compiler_params=pltpu.CompilerParams(vmem_limit_bytes=VMEM_LIMIT),
        cost_estimate=AHEAD,
        name="first",
    )(*blocks, turned, fields)


def green_kernel(n, share, *refs):
    block, turned, fields, earlier, begun = refs[:5]
    green, moved, left, right = refs[5:]
    q = place()[1]
    rows, electrons = block.shape[1:]
    propagate(share, n - 1, block, fields, moved, 0)
    overlaps = begun[...] + dot(turned[:, (n - 1) * rows :], moved[...])
    for i in range(share):
        overlap = overlaps[:, i * electrons : (i + 1) * electrons]
        size = jnp.abs(overlap)
        scale = jnp.max(jnp.sum(size, axis=0)) * jnp.max(jnp.sum(size, axis=1))
        left[i] = overlap.T / scale
        high, low = split(overlap)
        mixed = dot(high, low, ((1,), (1,)))
        right[i] = (dot(high, high, ((1,), (1,))) + (mixed + mixed.T)) / scale

    def advance(exact):
        for i in range(share):
            now, matrix = left[i], right[i]
            high, low = split(matrix)
            left_high, left_low = split(now)
            product = dot(left_high, high)
            if exact:
                product = product + (dot(left_high, low) + dot(left_low, high))
            left[i] = 2.0 * now - product
            right[i] = 2.0 * matrix - squared(high, low)

    for step in range(ITERS - 1):
        advance(step >= EARLY)
    for i in range(share):
        high, low = split(right[i])
        left_high, left_low = split(left[i])
        product = dot(left_high, high) + (dot(left_high, low) + dot(left_low, high))
        inverse = (2.0 * left[i] - product).astype(BF16)
        for k in range(n):
            at = pl.multiple_of((q ^ k) * rows, rows)
            held, start = (moved, 0) if k == n - 1 else (earlier, k * rows)
            green[pl.ds(at, rows), i * electrons : (i + 1) * electrons] = dot(
                held[start : start + rows, i * electrons : (i + 1) * electrons], inverse
            ).astype(BF16)


def make_green(n, share, block, turned, fields, earlier, begun):
    rows, electrons = block.shape[1:]
    return pl.pallas_call(
        functools.partial(green_kernel, n, share),
        out_shape=jax.ShapeDtypeStruct((n * rows, share * electrons), BF16),
        in_specs=[whole()] * 5,
        out_specs=whole(),
        scratch_shapes=[
            pltpu.VMEM((rows, share * electrons), BF16),
            pltpu.VMEM((share, electrons, electrons), F32),
            pltpu.VMEM((share, electrons, electrons), F32),
        ],
        compiler_params=pltpu.CompilerParams(vmem_limit_bytes=VMEM_LIMIT),
        name="green",
    )(block, turned, fields, earlier, begun)


def report(share, held, index, upper, lower):
    half = upper.shape[0]
    row = lax.broadcasted_iota(jnp.int32, (half, half), 0)
    column = lax.broadcasted_iota(jnp.int32, (half, half), 1)
    out_row = lax.broadcasted_iota(jnp.int32, held.shape, 0)
    for i in range(share):
        left, middle, right = 2 * i * half, (2 * i + 1) * half, 2 * (i + 1) * half
        a, b = upper[:, left:middle], upper[:, middle:right]
        c, d = lower[:, left:middle], lower[:, middle:right]
        trace = jnp.sum(jnp.where(row == column, a + d, 0.0))
        exchange = -0.5 * jnp.sum(a * a.T + d * d.T + 2.0 * (b * c.T))
        held = jnp.where(out_row == index * share + i, trace, held)
        held = jnp.where(out_row == held.shape[0] // 2 + index * share + i, exchange, held)
    return held


def near_kernel(share, count, height, *refs):
    vectors, green, outs = refs[:count], refs[count], refs[-1]
    for v in range(count):
        held = jnp.zeros(outs.shape[1:], F32)
        for g in range(vectors[v].shape[0] // height):
            full = dot(vectors[v][g * height : (g + 1) * height, :], green[...])
            held = report(share, held, g, full[: height // 2], full[height // 2 :])
        outs[v] = held


def shared_kernel(share, count, height, *refs):
    firsts, seconds, green = refs[:count], refs[count : 2 * count], refs[2 * count]
    outs, kept, both = refs[-count - 2], refs[-count - 1 : -1], refs[-1]
    parity = lax.axis_index("walk") & 1
    half = height // 2
    for v in range(count):
        rows = firsts[v].shape[0]
        for at, piece in ((parity, firsts[v]), (1 - parity, seconds[v])):
            both[pl.ds(pl.multiple_of(at * rows, 16), rows), :] = dot(piece[...], green[...])
        kept[v][...] = both[:half, :]
        held = jnp.zeros(outs.shape[1:], F32)
        for g in range(1, (2 * rows + half) // height):
            start = g * height - half
            held = report(share, held, g, both[start : start + half, :], both[start + half : start + height, :])
        outs[v] = held


def direct_kernel(share, count, *refs):
    uppers, green, kept = refs[:count], refs[count], refs[count + 1 : 2 * count + 1]
    before, outs = refs[-2:]
    for v in range(count):
        outs[v] = report(share, before[v], 0, dot(uppers[v][...], green[...]), kept[v][...])


def contract(kernel, count, vectors, green, *more, kept_rows=0, scratch_rows=0):
    wide = green.shape[1]
    kept = [jax.ShapeDtypeStruct((kept_rows, wide), F32)] * count if kept_rows else []
    return pl.pallas_call(
        kernel,
        out_shape=[jax.ShapeDtypeStruct((count, 8, 128), F32)] + kept,
        in_specs=[whole()] * (len(vectors) + 1 + len(more)),
        out_specs=[whole()] * (1 + len(kept)),
        scratch_shapes=[pltpu.VMEM((scratch_rows, wide), F32)] if scratch_rows else [],
        compiler_params=pltpu.CompilerParams(vmem_limit_bytes=VMEM_LIMIT),
        cost_estimate=pl.CostEstimate(
            flops=sum(2 * v.size * wide for v in vectors),
            bytes_accessed=sum(2 * v.size for v in vectors) + 2 * green.size,
            transcendentals=0,
        ),
        name="contract",
    )(*vectors, green, *more)


def unpack_kernel(n, share, masks, *refs):
    arrived, outs = refs[:n], refs[n:]
    vectors, per = outs[0].shape
    for which, out in enumerate(outs):
        for g in range(vectors):
            line = jnp.zeros((1, 128), F32)
            for k in range(n):
                for r in range(share):
                    cores, height = arrived[k].shape[:2]
                    at = which * (height // 2) + g * share + r
                    value = arrived[k][k % cores, at : at + 1, :]
                    line = jnp.where(masks[k * share + r : k * share + r + 1, :] > 0.0, value, line)
            out[g : g + 1, :] = line[:, :per]


def unpack(n, per, share, vectors, masks, arrived):
    return pl.pallas_call(
        functools.partial(unpack_kernel, n, share),
        out_shape=[jax.ShapeDtypeStruct((vectors, per), F32)] * 2,
        in_specs=[whole()] * (1 + n),
        out_specs=[whole()] * 2,
        compiler_params=pltpu.CompilerParams(vmem_limit_bytes=SMALL_LIMIT),
        name="unpack",
    )(masks, *arrived)


def at_the_source(walkers, trial_orbitals, cholesky, branches, counts, field):
    n = lax.axis_size("walk")
    per = walkers.shape[0]
    share = per // n
    row_size = lax.axis_size("row")
    vectors = cholesky.shape[0]
    pairs = [(w, q) for w in range(n) for q in range(n)]
    move = lambda x, k: lax.ppermute(x, SR, [(i, i ^ k) for i in range(n)])
    swap = lambda x: lax.ppermute(x, "walk", [(w, w ^ 1) for w in range(n)])
    ask = lambda x: lax.ppermute(x, ALL, [(w * n + q, (w ^ q) * n + q) for w, q in pairs])
    answer = lambda x, k: lax.ppermute(x, ALL, [(w * n + q, (w ^ q) * n + (q ^ k)) for w, q in pairs])
    near = [k for k in range(n) if k < row_size]
    far = [k for k in range(n) if k >= row_size]

    def spread(x):
        held = {}
        for k in far:
            low = k & (row_size - 1)
            held[k] = move(held[k ^ low], low) if low else move(x, k)
        return held

    def along(held):
        return {k: move(held[k & ~(row_size - 1)], k & (row_size - 1)) if k & (row_size - 1) else held[k] for k in far}

    ordered = lambda x, *first: lax.optimization_barrier((x,) + first)[0]
    heads = [k for k in far if not k & (row_size - 1)]
    height = cholesky.shape[1]
    rows = cholesky.reshape(vectors * height, cholesky.shape[2])
    direct_rows = height // 2
    shared_rows = (rows.shape[0] - direct_rows) // 2
    at = direct_rows + (lax.axis_index("walk") & 1) * shared_rows
    shared = lax.dynamic_slice_in_dim(rows, at, shared_rows, 0)
    sends = select(n, per, share, branches, walkers)
    own = message(ordered(trial_orbitals, sends[0]), field)
    messages = {0: own, **spread(own)}
    messages.update({k: move(own, k) for k in near[1:]})
    messages = [messages[k] for k in range(n)]
    crossed = {k: move(shared, k) for k in heads}
    close = [rows] + [move(rows, k) for k in near[1:]]
    early = close[1:]
    blocks = [sends[0]] + [
        move(ordered(sends[k], *(crossed.values() if k == n - 1 else early)), k) for k in range(1, n)
    ]
    asked = ask(pick_fields(n, per, share, branches, messages))
    turned, masks = turn(n, per, share, branches, counts, messages)
    other = {k: swap(x) for k, x in crossed.items()}
    earlier, begun = first_blocks(n, share, blocks[:-1], turned, asked)
    direct = {k: move(ordered(rows[:direct_rows], begun), k) for k in heads}
    green = make_green(n, share, blocks[n - 1], turned, asked, earlier, begun)
    crossed = along(crossed)
    other = along({k: ordered(x, green) for k, x in other.items()})
    [results] = contract(functools.partial(near_kernel, share, len(near), height), len(near), close, green)
    direct = along({k: ordered(x, results) for k, x in direct.items()})
    late, *kept = contract(
        functools.partial(shared_kernel, share, len(far), height),
        len(far),
        [crossed[k] for k in far] + [other[k] for k in far],
        ordered(green, results),
        kept_rows=direct_rows,
        scratch_rows=2 * shared_rows,
    )
    [late] = contract(
        functools.partial(direct_kernel, share, len(far)), len(far), [direct[k] for k in far], green, *kept, late
    )
    answers = [answer(late, far[0]), answer(ordered(results, late), 0)]
    arrived = [[x] + [move(x, k) for k in near[1:]] for x in reversed(answers)]
    return tuple(x.T for x in unpack(n, per, share, vectors, masks, [x for held in arrived for x in held]))


def newton_schulz(intersection):
    column_max = jnp.max(jnp.sum(jnp.abs(intersection), axis=0))
    row_max = jnp.max(jnp.sum(jnp.abs(intersection), axis=1))
    inverse = intersection.T / (column_max * row_max)
    twice_identity = 2.0 * jnp.eye(intersection.shape[0], dtype=intersection.dtype)
    for iteration in range(ITERS):
        inverse = jnp.dot(
            inverse,
            twice_identity - jnp.dot(intersection, inverse, precision=HIGHEST),
            precision=HIGHEST,
        )
    return inverse


def pick(array, indices):
    return jnp.concatenate(
        [lax.dynamic_slice_in_dim(array, indices[i], 1, 0) for i in range(indices.shape[0])], axis=0
    )


def at_the_target(walkers, trial_orbitals, cholesky, branches, counts, field):
    walk_size = lax.axis_size("walk")
    position = lax.axis_index("walk")
    per_device, row_count, electrons = walkers.shape
    capacity = (per_device + walk_size - 1) // walk_size
    sender = branches.reshape(walk_size, per_device) // per_device
    local_index = branches.reshape(walk_size, per_device) % per_device
    same_sender = sender[:, :, None] == sender[:, None, :]
    earlier = jnp.arange(per_device)[None, :] < jnp.arange(per_device)[:, None]
    arrival_rank = jnp.sum(same_sender & earlier[None], axis=2)
    wanted = (sender[:, None, :] == position) & (
        arrival_rank[:, None, :] == jnp.arange(capacity, dtype=jnp.int32)[None, :, None]
    )
    chosen = jnp.sum(jnp.where(wanted, local_index[:, None, :], 0), axis=2).reshape(-1)
    outgoing = pick(walkers, chosen).reshape(walk_size, capacity, row_count, electrons)
    arrived = lax.all_to_all(outgoing, "walk", split_axis=0, concat_axis=0, tiled=True)
    my_sender = lax.dynamic_index_in_dim(sender, position, 0, keepdims=False)
    my_rank = lax.dynamic_index_in_dim(arrival_rank, position, 0, keepdims=False)
    arrived_flat = arrived.reshape(walk_size * capacity, row_count, electrons)
    migrated = pick(arrived_flat, my_sender * capacity + my_rank)
    propagated = (migrated.astype(F32) * field[:, :, None]).astype(BF16)
    everything = lax.all_gather(propagated, SR, axis=1, tiled=True)
    shard_count = lax.axis_size(SR)
    share = per_device // shard_count
    trial_whole = lax.all_gather(trial_orbitals, SR, axis=0, tiled=True)
    own_walkers = lax.dynamic_slice_in_dim(everything, lax.axis_index(SR) * share, share, 0)
    intersection = jnp.einsum("mn,wmk->wnk", trial_whole, own_walkers, preferred_element_type=F32)
    inverse = jax.vmap(newton_schulz)(intersection).astype(BF16)
    inverses = lax.all_gather(inverse, SR, axis=0, tiled=True)
    green = jnp.einsum("wmn,wnk->wmk", everything, inverses, preferred_element_type=F32).astype(BF16)
    contracted = jnp.einsum("gnm,wmk->wgnk", cholesky, green, preferred_element_type=F32)
    living = (jnp.arange(per_device, dtype=jnp.int32) < counts[0]).astype(F32)[:, None]
    force_bias = jnp.trace(contracted, axis1=2, axis2=3) * living
    exchange_energy = -0.5 * jnp.einsum("wgnk,wgkn->wg", contracted, contracted) * living
    return (force_bias, exchange_energy)


def on_device(walkers, trial_orbitals, cholesky, branches, counts, field):
    walk_size, shard_count = lax.axis_size("walk"), lax.axis_size(SR)
    per = walkers.shape[0]
    if walk_size == shard_count and lax.axis_size("slab") == 2 and per % walk_size == 0 and not walk_size & (walk_size - 1):
        if cholesky.shape[0] * (per // walk_size) <= 4 and cholesky.shape[1] % 64 == 0 and per <= 128:
            return at_the_source(walkers, trial_orbitals, cholesky, branches, counts, field)
    return at_the_target(walkers, trial_orbitals, cholesky, branches, counts, field)


def solution(mesh):
    return jax.shard_map(
        on_device,
        mesh=mesh,
        in_specs=(
            P(("parts", "walk"), SR, None),
            P(("parts",) + SR, None),
            P(("parts",) + SR, None, None),
            P("parts"),
            P(("parts", "walk")),
            P(("parts", "walk"), SR),
        ),
        out_specs=(P(("parts", "walk"), SR), P(("parts", "walk"), SR)),
        check_vma=False,
    )
```
